1024 devices in a mesh: gx: 16 (over y_lo, z), gy: 8 (over x), gz: 8 (over y_hi, core).
Axes of the slice: x: 8, y: 8 (y_hi: 4, y_lo: 2; y = y_hi * 2 + y_lo), z: 8, core: 2. Of those that a mesh axis runs over, the one named last changes fastest.
Arguments:
- positions: float32 [3, 524288], P(None, ('gx', 'gy', 'gz')), may hold values from 0 to 16, as said below
- velocities: float32 [3, 524288], P(None, ('gx', 'gy', 'gz')), may hold values from -6 to 6
- forces: float32 [3, 524288], P(None, ('gx', 'gy', 'gz')), may hold values from -24 to 24
- species: int32 [524288], P(('gx', 'gy', 'gz')), may hold values from 0 to 3
- cell_ids: int32 [48, 24, 24, 27], P('gx', 'gy', 'gz'), may hold values from 0 to 511, as said below
- centers: int32 [8192], P(('gx', 'gy', 'gz')), may hold values from 0 to 511, as said below
- neighbours: int32 [8192, 128], P(('gx', 'gy', 'gz')), may hold values from 0 to 3886, as said below
- w_embed: float32 [64, 16], replicated, may hold values from -1.5 to 1.5
- w_mix: float32 [64, 64], replicated, may hold values from -0.75 to 0.75
- w_value: float32 [1, 192, 64], replicated, may hold values from -0.75 to 0.75
- w_env: float32 [1, 192, 64], replicated, may hold values from -0.75 to 0.75
- w_latent: float32 [1, 64, 256], replicated, may hold values from -0.375 to 0.375
- w_head: float32 [64, 64], replicated, may hold values from -0.75 to 0.75
- w_energy: float32 [64], replicated, may hold values from -0.75 to 0.75
Outputs:
- new_positions: float32 [3, 524288], P(None, ('gx', 'gy', 'gz'))
- new_velocities: float32 [3, 524288], P(None, ('gx', 'gy', 'gz'))
- new_forces: float32 [3, 524288], P(None, ('gx', 'gy', 'gz'))
The draws below stay inside these ranges and needn't reach their ends.
Inputs may be any that keep to these rules, and one draw needn't show every extreme that they name: `positions`: each domain's 8**3 atoms fill the sites of a lattice of spacing 2 Angstrom, one each, within 0.6 Angstrom of the site centre. `cell_ids`: entry [3 X + a, 3 Y + b, 3 Z + c, :] lists the atoms of domain (X, Y, Z) lying in band a, b, c along the three dimensions (band 0: below 6, band 1: 6 to 10, band 2: above 10 Angstrom); each atom stands in exactly one cell, and a cell of fewer than 27 atoms repeats its first atom in the remaining slots. `centers`: A domain's live blocks come first, 1 to 8 of them; a dead block's entries all equal its centre. `neighbours`: A live block names up to 122 distinct table entries of real atoms (never a repeated slot) near its centre; its other entries equal the centre and are padding.
All inputs are finite; a program needn't handle non-finite values.
Results may differ from the reference program's by a relative error of at most 0.0003.
Values sent between devices are 32-bit elements; how exact they have to be, the bound alone decides.
No kernel may reach another device: no remote copies, remote signals or barrier semaphores. Data moves between devices by JAX's collectives and lax.ppermute only.
A program may use at most 32 MiB of HBM per device.

```python
import math
import jax
import jax.numpy as jnp
import numpy as np
from jax import lax

C = 64
NRAD = 8
NSPEC = 4
LAYERS = 1
ITERS = 2
SIDE = 8
BLK = 128
NB = 8
G = 27
ATOMS = 524288
N_GX = 16
N_GY = 8
N_GZ = 8
DEVICES = 1024


def sphere_offsets():
    rows = [(a, b, c) for a in range(-3, 4) for b in range(-3, 4) for c in range(-3, 4) if 0 < a * a + b * b + c * c <= 9]
    return np.array(rows, np.int32)


def cell_sites():
    starts = (0, 3, SIDE - 3)
    widths = (3, SIDE - 6, 3)
    table = np.zeros((3, 3, 3, G), np.int32)
    for first in range(3):
        for second in range(3):
            for third in range(3):
                sites = [((starts[first] + i) * SIDE + starts[second] + j) * SIDE + starts[third] + k for i in range(widths[first]) for j in range(widths[second]) for k in range(widths[third])]
                for slot in range(G):
                    table[first, second, third, slot] = sites[slot] if slot < len(sites) else sites[0]
    return table


def site_layout(key):
    count = SIDE ** 3
    keys = jax.random.split(jax.random.fold_in(key, 101), DEVICES)
    placed = jax.vmap(lambda item: jax.random.permutation(item, count))(keys).astype(jnp.int32)
    inverse = jax.vmap(lambda row: jnp.zeros((count,), jnp.int32).at[row].set(jnp.arange(count, dtype=jnp.int32)))(placed)
    return (placed, inverse)


def local_cell(coords):
    band = jnp.where(coords < 3, 0, jnp.where(coords < SIDE - 3, 1, 2))
    start = jnp.where(band == 0, 0, jnp.where(band == 1, 3, SIDE - 3))
    extent = jnp.where(band == 1, SIDE - 6, 3)
    offset = coords - start
    slot = (offset[..., 0] * extent[..., 1] + offset[..., 1]) * extent[..., 2] + offset[..., 2]
    return (band, slot)


def block_plan(key):
    count = SIDE ** 3
    placed, inverse = site_layout(key)
    pick_key, load_key, order_key = jax.random.split(jax.random.fold_in(key, 202), 3)
    picks = jax.vmap(lambda item: jax.random.permutation(item, count))(jax.random.split(pick_key, DEVICES))
    picks = picks[:, :NB].astype(jnp.int32)
    column = jnp.arange(DEVICES) // (N_GY * N_GZ)
    film = (column >= N_GX // 4) & (column < N_GX // 2)
    light = jax.random.randint(load_key, (DEVICES,), 1, max(NB // 4, 1) + 1)
    loads = jnp.where(film, NB, light)
    centre_site = jnp.take_along_axis(placed, picks, axis=1)
    coords = jnp.stack([centre_site // (SIDE * SIDE), centre_site // SIDE % SIDE, centre_site % SIDE], -1)
    offsets = jnp.asarray(sphere_offsets())
    reach = offsets.shape[0]
    orders = jax.vmap(lambda item: jax.random.permutation(item, reach))(jax.random.split(order_key, DEVICES * NB))
    orders = orders.reshape(DEVICES, NB, reach)
    target = coords[:, :, None, :] + offsets[orders]
    domain = jnp.floor_divide(target, SIDE)
    local = target - domain * SIDE
    local_site = (local[..., 0] * SIDE + local[..., 1]) * SIDE + local[..., 2]
    own_atom = jnp.take_along_axis(inverse, local_site.reshape(DEVICES, -1), axis=1).reshape(local_site.shape)
    band, slot = local_cell(local)
    cell = jnp.where(domain < 0, 0, jnp.where(domain > 0, 4, band + 1))
    ghost = count + ((cell[..., 0] * 5 + cell[..., 1]) * 5 + cell[..., 2]) * G + slot
    entry = jnp.where(jnp.all(domain == 0, axis=-1), own_atom, ghost)
    filler = jnp.broadcast_to(picks[:, :, None], (DEVICES, NB, BLK - reach))
    rows = jnp.concatenate([entry, filler], -1)
    alive = jnp.arange(NB)[None, :] < loads[:, None]
    rows = jnp.where(alive[:, :, None], rows, picks[:, :, None])
    return (picks.reshape(-1), rows.reshape(DEVICES * NB, BLK).astype(jnp.int32))


def draw_positions(key, part):
    placed, inverse = site_layout(key)
    key = jax.random.fold_in(key, 1)
    site = jnp.stack([placed // (SIDE * SIDE), placed // SIDE % SIDE, placed % SIDE], 0).astype(jnp.float32)
    jitter = 0.15 * jnp.clip(jax.random.normal(key, site.shape, jnp.float32), -2.0, 2.0)
    return (2.0 * (site + 0.5 + jitter)).reshape(3, DEVICES * SIDE ** 3)


def draw_cell_ids(key, part):
    placed, inverse = site_layout(key)
    table = jnp.asarray(cell_sites()).reshape(-1)
    ids = jnp.take(inverse, table, axis=1).reshape(N_GX, N_GY, N_GZ, 3, 3, 3, G)
    return ids.transpose(0, 3, 1, 4, 2, 5, 6).reshape(3 * N_GX, 3 * N_GY, 3 * N_GZ, G).astype(jnp.int32)


def draw_centers(key, part):
    centres, rows = block_plan(key)
    return centres


def draw_neighbours(key, part):
    centres, rows = block_plan(key)
    return rows


def with_ends(drawn, key, smallest, top_value):
    index_at = [jax.random.randint(jax.random.fold_in(key, axis), (), 0, length) for axis, length in enumerate(drawn.shape)]
    longest = drawn.shape.index(max(drawn.shape))
    next_to = index_at[:longest] + [(index_at[longest] + 1) % drawn.shape[longest]] + index_at[longest + 1:]
    return drawn.at[tuple(index_at)].set(smallest).at[tuple(next_to)].set(top_value)


def level_of(rng, shape, pieces, least, high):
    def one(axis_at, blocks):
        heights = jax.random.uniform(jax.random.fold_in(jax.random.fold_in(rng, 6), axis_at), (blocks,), jnp.float32, least / len(pieces), high / len(pieces))
        return jnp.repeat(jnp.exp(heights), shape[axis_at] // blocks).reshape((-1,) + (1,) * (len(shape) - axis_at - 1))

    gain = one(*pieces[0])
    for cut in pieces[1:]:
        gain = gain * one(*cut)
    return gain


def noise(own_key, shape, scale, most, cuts=(), kind=jnp.bfloat16):
    loudness = level_of(own_key, shape, cuts, -0.22, 0.18) if cuts else 1.0
    drawn = jax.random.normal(own_key, shape, jnp.float32) * scale * loudness
    return jnp.minimum(jnp.maximum(drawn, -most), most).astype(kind)


def setup_inputs(seed: int = 0) -> dict:
    arg_keys = jax.random.split(jax.random.key(seed), 15)
    positions = draw_positions(jax.random.fold_in(arg_keys[14], 71), 0)
    velocities = noise(arg_keys[1], (3, ATOMS), 1.0, 6.0, ((1, 1024),), jnp.float32)
    forces = noise(arg_keys[2], (3, ATOMS), 4.0, 24.0, ((1, 1024),), jnp.float32)
    species = with_ends(jax.random.randint(arg_keys[3], (ATOMS,), 0, NSPEC), jax.random.fold_in(arg_keys[3], 1), 0, NSPEC - 1).astype(jnp.int32)
    cell_ids = draw_cell_ids(jax.random.fold_in(arg_keys[14], 71), 0)
    centers = draw_centers(jax.random.fold_in(arg_keys[14], 71), 0)
    neighbours = draw_neighbours(jax.random.fold_in(arg_keys[14], 71), 0)
    w_embed = noise(arg_keys[7], (C, NRAD + 2 * NSPEC), (NRAD + 2 * NSPEC) ** -0.5, 1.5, (), jnp.float32)
    w_mix = noise(arg_keys[8], (C, C), C ** -0.5, 0.75, (), jnp.float32)
    w_value = noise(arg_keys[9], (LAYERS, 3 * C, C), C ** -0.5, 0.75, (), jnp.float32)
    w_env = noise(arg_keys[10], (LAYERS, 3 * C, C), C ** -0.5, 0.75, (), jnp.float32)
    w_latent = noise(arg_keys[11], (LAYERS, C, 4 * C), (4 * C) ** -0.5, 0.375, (), jnp.float32)
    w_head = noise(arg_keys[12], (C, C), C ** -0.5, 0.75, (), jnp.float32)
    w_energy = noise(arg_keys[13], (C,), C ** -0.5, 0.75, (), jnp.float32)
    return {"positions": positions, "velocities": velocities, "forces": forces, "species": species, "cell_ids": cell_ids, "centers": centers, "neighbours": neighbours, "w_embed": w_embed, "w_mix": w_mix, "w_value": w_value, "w_env": w_env, "w_latent": w_latent, "w_head": w_head, "w_energy": w_energy}


CUTOFF = 6.0
SOFTENING = 0.09
SPACING = 2.0
TIME_STEP = 0.1
ENV_SCALE = 0.1
ENERGY_SCALE = 50.0
MASSES = (1.008, 15.999, 22.99, 35.453)

def harmonics(direction):
    x_part, y_part, z_part = (direction[0], direction[1], direction[2])
    root_three = math.sqrt(3.0)
    root_fifteen = math.sqrt(15.0)
    root_five = math.sqrt(5.0)
    return jnp.stack([jnp.ones_like(x_part), root_three * x_part, root_three * y_part, root_three * z_part, root_fifteen * x_part * y_part, root_fifteen * y_part * z_part, 0.5 * root_five * (3.0 * z_part * z_part - 1.0), root_fifteen * x_part * z_part, 0.5 * root_fifteen * (x_part * x_part - y_part * y_part)], 0)

def block_energy(displacement, pair_kinds, w_embed, w_mix, w_value, w_env, w_latent, w_head, w_energy):
    highest = lax.Precision.HIGHEST
    channels = w_mix.shape[0]
    live_pair = (pair_kinds[1] >= 0).astype(jnp.float32)
    distance = jnp.sqrt(lax.optimization_barrier(jnp.sum(displacement * displacement, axis=0)) + SOFTENING)
    direction = displacement / distance[None, :]
    scaled = jnp.minimum(distance / CUTOFF, 1.0)
    envelope = (1.0 - 28.0 * scaled ** 6 + 48.0 * scaled ** 7 - 21.0 * scaled ** 8) * live_pair
    degrees = jnp.arange(1, NRAD + 1, dtype=jnp.float32)
    radial = math.sqrt(2.0 / CUTOFF) * jnp.sin(degrees[:, None] * (math.pi / CUTOFF) * distance[None, :]) / distance[None, :]
    labels = jnp.arange(NSPEC, dtype=jnp.int32)
    centre_hot = (pair_kinds[0][None, :] == labels[:, None]).astype(jnp.float32)
    other_hot = (pair_kinds[1][None, :] == labels[:, None]).astype(jnp.float32)
    features = jnp.concatenate([radial, centre_hot, other_hot], 0)
    hidden = jax.nn.silu(jnp.dot(w_embed, features, precision=highest))
    latent = jax.nn.silu(jnp.dot(w_mix, hidden, precision=highest)) * envelope[None, :]
    angular = harmonics(direction)
    bounds = ((0, 1), (1, 4), (4, 9))
    for layer_idx in range(w_value.shape[0]):
        values = jnp.dot(w_value[layer_idx], latent, precision=highest)
        weights = jnp.dot(w_env[layer_idx], latent, precision=highest)
        scalars = []
        for degree, (first_row, last_row) in enumerate(bounds):
            angular_part = angular[first_row:last_row]
            summed = ENV_SCALE * jnp.dot(weights[degree * channels:(degree + 1) * channels], angular_part.T, precision=highest)
            scalars.append(values[degree * channels:(degree + 1) * channels] * jnp.dot(summed, angular_part, precision=highest))
        combined = jnp.concatenate([latent] + scalars, 0)
        latent = latent + jax.nn.silu(jnp.dot(w_latent[layer_idx], combined, precision=highest)) * envelope[None, :]
    readout = jnp.dot(w_energy, jax.nn.silu(jnp.dot(w_head, latent, precision=highest)), precision=highest)
    return ENERGY_SCALE * jnp.sum(readout * envelope)

def block_force(displacement, pair_kinds, params):
    return jax.grad(block_energy)(displacement, pair_kinds, *params)

def ghost_ids(cell_ids):
    cells = cell_ids.reshape(N_GX, 3, N_GY, 3, N_GZ, 3, G).transpose(0, 2, 4, 1, 3, 5, 6)
    owners = jnp.arange(DEVICES, dtype=jnp.int32).reshape(N_GX, N_GY, N_GZ)
    table = cells + (owners * SIDE ** 3)[:, :, :, None, None, None, None]
    moves = (-1, 0, 0, 0, 1)
    bands = (2, 0, 1, 2, 0)
    for axis_dev in range(3):
        table = jnp.stack([jnp.take(jnp.roll(table, -moves[index], axis=axis_dev), bands[index], axis=3 + axis_dev) for index in range(5)], axis=3 + axis_dev)
    return table.reshape(DEVICES, 125 * G)

def ghost_offsets():
    edge = SPACING * SIDE
    shift_row = edge * jnp.array([-1.0, 0.0, 0.0, 0.0, 1.0], jnp.float32)
    shape = (5, 5, 5, G)
    along_x = jnp.broadcast_to(shift_row[:, None, None, None], shape)
    along_y = jnp.broadcast_to(shift_row[None, :, None, None], shape)
    along_z = jnp.broadcast_to(shift_row[None, None, :, None], shape)
    return jnp.stack([along_x, along_y, along_z], 0).reshape(3, -1)

def reference(positions, velocities, forces, species, cell_ids, centers, neighbours, w_embed, w_mix, w_value, w_env, w_latent, w_head, w_energy):
    params = (w_embed, w_mix, w_value, w_env, w_latent, w_head, w_energy)
    atoms = SIDE ** 3
    owners = jnp.arange(DEVICES, dtype=jnp.int32)
    table_ids = jnp.concatenate([owners[:, None] * atoms + jnp.arange(atoms, dtype=jnp.int32)[None, :], ghost_ids(cell_ids)], 1)
    table_shift = jnp.concatenate([jnp.zeros((3, atoms), jnp.float32), ghost_offsets()], 1)
    block_owner = jnp.repeat(owners, NB)
    centre_ids = (block_owner * atoms + centers).astype(jnp.int32)
    local_rows = neighbours.reshape(DEVICES, NB * BLK)
    target_ids = jnp.take_along_axis(table_ids, local_rows, axis=1).reshape(DEVICES * NB, BLK).astype(jnp.int32)
    target_shift = jnp.take(table_shift, neighbours, axis=1)
    live_pair = neighbours != centers[:, None]
    centre_kind = jnp.broadcast_to(jnp.take(species, centre_ids)[:, None], neighbours.shape)
    other_kind = jnp.where(live_pair, jnp.take(species, target_ids), -1)
    pair_kinds = jnp.stack([centre_kind, other_kind], 1)
    labels = jnp.arange(NSPEC, dtype=jnp.int32)
    inv_mass = lax.optimization_barrier(jnp.sum((species[None, :] == labels[:, None]).astype(jnp.float32) / jnp.array(MASSES, jnp.float32)[:, None], 0))

    def device_grads(item):
        return jax.vmap(lambda piece, kinds_piece: block_force(piece, kinds_piece, params))(item[0], item[1])
    for step_idx in range(ITERS):
        kick = velocities + 0.5 * TIME_STEP * forces * inv_mass[None, :]
        moved = positions + TIME_STEP * kick
        reached = jnp.take(moved, target_ids, axis=1) + target_shift
        anchor = jnp.take(moved, centre_ids, axis=1)
        displacement = jnp.moveaxis(reached - anchor[:, :, None], 0, 1)
        grads = lax.map(device_grads, (displacement.reshape(DEVICES, NB, 3, BLK), pair_kinds.reshape(DEVICES, NB, 2, BLK)))
        grads = grads.reshape(DEVICES * NB, 3, BLK)
        on_centre = lax.optimization_barrier(jnp.sum(grads, axis=2)).T
        spread = -jnp.moveaxis(grads, 1, 0).reshape(3, -1)
        forces = jnp.zeros((3, atoms * DEVICES), jnp.float32).at[:, centre_ids].add(on_centre)
        forces = forces.at[:, target_ids.reshape(-1)].add(spread)
        velocities = kick + 0.5 * TIME_STEP * forces * inv_mass[None, :]
        positions = moved
    return (positions, velocities, forces)
```

```python
import math
import jax, jax.numpy as jnp
from jax import lax
from jax.experimental import pallas as pl
from jax.experimental.pallas import tpu as pltpu

f32, bf16, i32 = jnp.float32, jnp.bfloat16, jnp.int32
NB, BLK, C = 8, 128, 64
PAIRS = NB * BLK
R3, R5, R15 = math.sqrt(3.0), math.sqrt(5.0), math.sqrt(15.0)

def nt(a, b):
    return lax.dot_general(a, b, (((1,), (1,)), ((), ())), preferred_element_type=f32)

def nn(a, b):
    return jnp.dot(a, b, preferred_element_type=f32)

def split(x):
    hi = x.astype(bf16)
    return hi, (x - hi.astype(f32)).astype(bf16)

def stack3(x):
    hi, lo = split(x)
    return jnp.concatenate([hi, lo, hi], 0)

def sigmoid(z):
    return 0.5 * jnp.tanh(0.5 * z) + 0.5

def harmonic_rows(ux, uy, uz):
    return [jnp.ones_like(ux), R3 * ux, R3 * uy, R3 * uz, R15 * ux * uy, R15 * uy * uz,
            0.5 * R5 * (3.0 * uz * uz - 1.0), R15 * ux * uz, 0.5 * R15 * (ux * ux - uy * uy)]

def wide(ref, rows):
    return jnp.concatenate([jnp.broadcast_to(ref[b:b + 1, :], (rows, BLK)) for b in range(NB)], 1)

def pair_grads(disp, kc, kn, live, w, s):
    dx, dy, dz = disp
    r = jnp.sqrt(dx * dx + dy * dy + dz * dz + 0.09)
    rinv = 1.0 / r
    ux, uy, uz = dx * rinv, dy * rinv, dz * rinv
    q = jnp.minimum(r * (1.0 / 6.0), 1.0)
    q2 = q * q
    q4 = q2 * q2
    q5 = q4 * q
    q6 = q4 * q2
    f = (1.0 - 28.0 * q6 + 48.0 * (q6 * q) - 21.0 * (q6 * q2)) * live
    fp = -28.0 * q5 * (1.0 - q) * (1.0 - q) * live
    theta = math.pi * q
    s1, c1 = jnp.sin(theta), jnp.cos(theta)
    sm, cm = s1, c1
    norm = math.sqrt(1.0 / 3.0)
    rn = norm * rinv
    slopes = []
    for m in range(8):
        basis = sm * rn
        s["feat"][m] = basis
        slopes.append((cm * (math.pi / 6.0 * (m + 1)) - sm * rinv) * rn)
        sm, cm = sm * c1 + cm * s1, cm * c1 - sm * s1
    ys = harmonic_rows(ux, uy, uz)
    for n in range(9):
        s["harm"][n] = ys[n]
    for n in range(9, 16):
        s["harm"][n] = jnp.zeros((8, 128), f32)
    s["sc"][0] = f
    s["sc"][1] = kc
    s["sc"][2] = kn
    fw = wide(s["sc"].at[0], 1)

    sub8 = lax.broadcasted_iota(i32, (8, BLK), 0).astype(f32)
    feats = []
    for b in range(NB):
        hot = jnp.where(sub8 < 4.0, jnp.broadcast_to(s["sc"][1, b:b + 1, :], (8, BLK)),
                        jnp.broadcast_to(s["sc"][2, b:b + 1, :], (8, BLK)) + 4.0) == sub8
        feats.append(jnp.concatenate([s["feat"][:, b, :], hot.astype(f32)], 0))
    feat = jnp.concatenate(feats, 1)

    z1 = nn(w["emb"][...], stack3(feat))
    g1 = sigmoid(z1)
    h = z1 * g1
    s["d1"][...] = g1 + h * (1.0 - g1)
    z2 = nn(w["mix"][...], stack3(h))
    g2 = sigmoid(z2)
    a = z2 * g2
    s["d2"][...] = g2 + a * (1.0 - g2)
    s["a"][...] = a
    x = a * fw
    vw = nn(w["ve"][...], stack3(x))
    s["vw"][...] = vw

    zero = jnp.zeros((16, BLK), f32)
    bd_h, bd_l, bd3, rep = [], [], [], []
    for j in range(NB // 2):
        y0, y1 = s["harm"][:, 2 * j, :], s["harm"][:, 2 * j + 1, :]
        bd = jnp.concatenate([jnp.concatenate([y0, zero], 1), jnp.concatenate([zero, y1], 1)], 0)
        hi, lo = split(bd)
        bd3.append(jnp.concatenate([hi, lo, hi], 0))
        rh, rl = jnp.concatenate([hi, hi, hi], 0), jnp.concatenate([lo, lo, lo], 0)
        rep.append(jnp.concatenate([rh, rl, rh], 1))

    row = lax.broadcasted_iota(i32, (192, 96), 0) // C
    col = lax.broadcasted_iota(i32, (192, 96), 1)
    part = col % 16
    order = jnp.where(part == 0, 0, jnp.where(part < 4, 1, jnp.where(part < 9, 2, 3)))
    mask = jnp.where(row == order, 0.1, 0.0).astype(f32)

    def moments(val, j):
        hi, lo = split(val)
        return nt(jnp.concatenate([hi, hi, lo], 1), rep[j]) * mask

    def sharp(m):
        hi, lo = split(m)
        return jnp.where(col < 64, hi.astype(f32), lo.astype(f32)).astype(bf16)

    sums, tees = [], []
    for j in range(NB // 2):
        lanes = slice(256 * j, 256 * j + 256)
        m = moments(s["vw"][192:384, lanes], j)
        s["sums"][j] = m
        t = nn(sharp(m), bd3[j])
        s["t"][:, lanes] = t
    sc = s["vw"][0:192, :] * s["t"][...]
    z3 = nn(w["lat"][...], stack3(jnp.concatenate([x, sc], 0)))
    g3 = sigmoid(z3)
    bb = z3 * g3
    s["d3"][...] = g3 + bb * (1.0 - g3)
    x2 = x + bb * fw
    z4 = nn(w["head"][...], stack3(x2))
    g4 = sigmoid(z4)
    hh = z4 * g4
    wen = w["energy"][...]
    e = jnp.sum(wen * hh, 0, keepdims=True)
    dz4 = wen * fw * (g4 + hh * (1.0 - g4))
    dx2 = nn(w["head_t"][...], stack3(dz4))
    df = e + jnp.sum(dx2 * bb, 0, keepdims=True)
    dz3 = dx2 * fw * s["d3"][...]
    dc = nn(w["lat_t"][...], stack3(dz3))
    dxa = dx2 + dc[0:64]
    ds = dc[64:256]
    s["dv"][...] = ds * s["t"][...]
    s["dt"][...] = ds * s["vw"][0:192, :]
    for j in range(NB // 2):
        lanes = slice(256 * j, 256 * j + 256)
        dt = s["dt"][:, lanes]
        m = moments(dt, j)
        s["dw"][:, lanes] = nn(sharp(m), bd3[j])
        acc = None
        for left, right in ((s["sums"][j], dt), (m, s["vw"][192:384, lanes])):
            lt = jnp.transpose(jnp.concatenate([left, jnp.zeros((192, 32), f32)], 1))[0:32]
            lh, ll = split(lt)
            rh, rl = split(right)
            both = nn(jnp.concatenate([lh, ll], 0), rh)
            one = both[0:32] + both[32:64] + nn(lh, rl)
            acc = one if acc is None else acc + one
        s["dy"][2 * j] = acc[0:16, 0:128]
        s["dy"][2 * j + 1] = acc[16:32, 128:256]
    dx = dxa + nn(w["ve_t"][...], stack3(jnp.concatenate([s["dv"][...], s["dw"][...]], 0)))
    df = df + jnp.sum(dx * s["a"][...], 0, keepdims=True)
    for b in range(NB):
        s["sc"][3, b:b + 1, :] = df[:, 128 * b:128 * b + 128]
    dz2 = dx * fw * s["d2"][...]
    dz1 = nn(w["mix_t"][...], stack3(dz2)) * s["d1"][...]
    dr8 = nn(w["emb_t"][...], stack3(dz1))
    for b in range(NB):
        s["dr"][b] = dr8[0:8, 128 * b:128 * b + 128]

    dr = s["sc"][3] * fp
    for m in range(8):
        dr = dr + s["dr"][:, m, :] * slopes[m]
    gy = [s["dy"][:, n, :] for n in range(9)]
    dux = R3 * gy[1] + R15 * (uy * gy[4] + uz * gy[7] + ux * gy[8])
    duy = R3 * gy[2] + R15 * (ux * gy[4] + uz * gy[5] - uy * gy[8])
    duz = R3 * gy[3] + R15 * (uy * gy[5] + ux * gy[7]) + (3.0 * R5) * uz * gy[6]
    dot = dux * ux + duy * uy + duz * uz
    along = dr - dot * rinv
    scale = 50.0
    return [scale * (du * rinv + along * u) for du, u in ((dux, ux), (duy, uy), (duz, uz))]

PAIR_SCRATCH = {
    "feat": (8, 8, 128), "harm": (16, 8, 128), "sc": (4, 8, 128), "d1": (C, PAIRS), "d2": (C, PAIRS), "a": (C, PAIRS),
    "vw": (384, PAIRS), "sums": (4, 192, 96), "t": (192, PAIRS), "d3": (C, PAIRS), "dv": (192, PAIRS), "dt": (192, PAIRS),
    "dw": (192, PAIRS), "dy": (8, 16, 128), "dr": (8, 8, 128),
}
WEIGHT_NAMES = ("emb", "mix", "ve", "lat", "head", "head_t", "lat_t", "ve_t", "mix_t", "emb_t", "energy")

def rounded(w):
    return lax.reduce_precision(w, 8, 7)

def stack_weights(w):
    hi = rounded(w)
    lo = rounded(w - hi)
    return jnp.concatenate([hi, hi, lo], 1).astype(bf16)

def prepare(w_embed, w_mix, w_value, w_env, w_latent, w_head, w_energy):
    ve = jnp.concatenate([w_value[0], w_env[0]], 0)
    emb_t = jnp.concatenate([w_embed[:, :8].T, jnp.zeros((8, C), f32)], 0)
    return (stack_weights(w_embed), stack_weights(w_mix), stack_weights(ve), stack_weights(w_latent[0]), stack_weights(w_head),
            stack_weights(w_head.T), stack_weights(w_latent[0].T), stack_weights(ve.T), stack_weights(w_mix.T), stack_weights(emb_t),
            w_energy[:, None])


SIDE = 8
ATOMS = SIDE ** 3
ROWS = 25
STEP = 0.1
MASSES = (1.008, 15.999, 22.99, 35.453)
ZLANE = (0, 27, 54, 72, 99)
WIDTHS = (3, 2, 3)
EDGE = 2.0 * SIDE
TILE = (8, 128)


def iota(dim, shape=TILE):
    return lax.broadcasted_iota(i32, shape, dim)


def lane_take(row, idx):
    return jnp.take_along_axis(row, idx, axis=1)


def roll_rows(v, shift):
    return v if shift % 8 == 0 else pltpu.roll(v, shift % 8, 0)


def roll_lanes(v, shift):
    return v if shift % 128 == 0 else pltpu.roll(v, shift % 128, 1)


def inverse_mass(kind):
    out = jnp.full(kind.shape, 1.0 / MASSES[3], f32)
    for k in range(3):
        out = jnp.where(kind == float(k), 1.0 / MASSES[k], out)
    return out


def start_kernel(pos, vel, frc, spec, cid, t1, t2, t3, own):
    kind = spec[...].astype(f32)
    mass = inverse_mass(kind)
    kick = vel[...] + (0.5 * STEP) * frc[...] * mass
    own[0:3, :] = pos[...] + STEP * kick
    own[3:6, :] = kick
    own[6:7, :] = kind
    own[7:8, :] = jnp.zeros_like(kind)
    cuts = [own[:, 128 * h:128 * h + 128] for h in range(4)]
    outs = (t1, t2, t3)
    for r in range(9):
        ids = jnp.broadcast_to(cid[r:r + 1, :], TILE)
        lo, hi = ids & 127, ids >> 7
        acc = lane_take(cuts[0], lo)
        for h in range(1, 4):
            acc = jnp.where(hi == h, lane_take(cuts[h], lo), acc)
        outs[r // 3][r % 3] = acc


def index_kernel(neigh, cen, cid, nrow, nlane, live, crow, clane, irow, ilane):
    sub, lane = iota(0), iota(1)
    big = iota(0, (128, 128))
    left, right = [], []
    for r in range(9):
        area = WIDTHS[r // 3] * WIDTHS[r % 3]
        ids = jnp.broadcast_to(cid[r:r + 1, :], TILE)
        valid = (lane >= 27) & (lane < 27 + 3 * area)
        valid = valid | ((lane >= 54) & (lane < 54 + 2 * area))
        valid = valid | ((lane >= 72) & (lane < 72 + 3 * area))
        row = (r // 3 + 1) * 5 + r % 3 + 1
        value = jnp.where((sub & 1) == 0, row, lane)
        left.append(jnp.where(valid & ((ids >> 7) == (sub >> 1)), value, 0).astype(f32).astype(bf16))
        lo = jnp.broadcast_to(cid[r:r + 1, :], (128, 128)) & 127
        right.append(jnp.where(big == lo, 1.0, 0.0).astype(bf16))
    inv = nt(jnp.concatenate(left, 1), jnp.concatenate(right, 1))
    inv = (inv + 0.5).astype(i32)
    for h in range(4):
        irow[h:h + 1, :] = inv[2 * h:2 * h + 1, :]
        ilane[h:h + 1, :] = inv[2 * h + 1:2 * h + 2, :]

    def place(n):
        lo, hi = n & 127, n >> 7
        row = jnp.zeros(TILE, i32)
        col = jnp.zeros(TILE, i32)
        for h in range(4):
            row = jnp.where(hi == h, lane_take(jnp.broadcast_to(irow[h:h + 1, :], TILE), lo), row)
            col = jnp.where(hi == h, lane_take(jnp.broadcast_to(ilane[h:h + 1, :], TILE), lo), col)
        m = jnp.maximum(n - ATOMS, 0)
        grow = ((m.astype(f32) + 0.5) * (1.0 / 135.0)).astype(i32)
        rem = m - 135 * grow
        ez = ((rem.astype(f32) + 0.5) * (1.0 / 27.0)).astype(i32)
        first = jnp.where(ez == 0, 0, jnp.where(ez == 1, 27, jnp.where(ez == 2, 54, jnp.where(ez == 3, 72, 99))))
        glane = first + rem - 27 * ez
        return jnp.where(hi < 4, row, grow), jnp.where(hi < 4, col, glane)

    n, c = neigh[...], cen[...]
    nrow[...], nlane[...] = place(n)
    crow[...], clane[...] = place(c)
    live[...] = jnp.where(n != c, 1.0, 0.0)


def second_kernel(xlo, t1, t2, t3, xhi, up, down):
    for ex, part in enumerate((xlo, t1, t2, t3, xhi)):
        up[ex] = part[2]
        down[ex] = part[0]


def third_kernel(xlo, t1, t2, t3, xhi, ylo, yhi, table, up, down):
    lane = iota(1)
    for ex, part in enumerate((xlo, t1, t2, t3, xhi)):
        table[5 * ex] = ylo[ex]
        for ey in range(3):
            table[5 * ex + ey + 1] = part[ey]
        table[5 * ex + 4] = yhi[ex]
    for k in range(7):
        hi, lo = jnp.zeros(TILE, f32), jnp.zeros(TILE, f32)
        for p in range(min(4, ROWS - 4 * k)):
            v = table[4 * k + p]
            here = (lane >= 32 * p) & (lane < 32 * p + 32)
            hi = jnp.where(here, roll_lanes(v, 32 * p - 72), hi)
            lo = jnp.where(here, roll_lanes(v, 32 * p - 27), lo)
        up[k] = hi
        down[k] = lo


def pair_step(tab, nrow, nlane, live, crow, clane, w, s, force):
    sub, lane = iota(0), iota(1)
    zshift = jnp.where(lane < ZLANE[1], -EDGE, jnp.where(lane >= ZLANE[4], EDGE, 0.0))
    zshift = jnp.where(sub == 2, zshift, 0.0)
    nr, nl, cr, cl = nrow[...], nlane[...], crow[...], clane[...]
    near = [jnp.zeros(TILE, f32) for _ in range(4)]
    centre = [jnp.zeros(TILE, f32) for _ in range(4)]
    for r in range(ROWS):
        ex, ey = r // 5, r % 5
        shift = zshift
        if ex in (0, 4):
            shift = jnp.where(sub == 0, EDGE * (ex // 2 - 1), shift)
        if ey in (0, 4):
            shift = jnp.where(sub == 1, EDGE * (ey // 2 - 1), shift)
        s["shifted"][r] = tab[r] + shift
        mine = nr == r
        centred = cr == r
        for k, q in enumerate((0, 1, 2, 6)):
            line = jnp.broadcast_to(s["shifted"][r, q:q + 1, :], TILE)
            near[k] = jnp.where(mine, lane_take(line, nl), near[k])
            if ex in (1, 2, 3) and ey in (1, 2, 3):
                centre[k] = jnp.where(centred, lane_take(line, cl), centre[k])
    alive = live[...]
    disp = [near[k] - centre[k] for k in range(3)]
    grads = pair_grads(disp, centre[3], near[3], alive, w, s)
    spare = 1.0 / jnp.sum(1.0 - alive, 1, keepdims=True)
    for k, g in enumerate(grads):
        g = jnp.where(alive > 0.0, -g, jnp.sum(g, 1, keepdims=True) * spare)
        hi = g.astype(bf16).astype(f32)
        s["spread"][k] = hi
        s["spread"][k + 3] = g - hi
    s["spread"][6] = jnp.zeros(TILE, f32)
    s["spread"][7] = jnp.zeros(TILE, f32)
    big = iota(0, (128, 128))
    left, right = [], []
    for b in range(NB):
        g = s["spread"][:, b, :]
        rows = jnp.broadcast_to(nrow[b:b + 1, :], TILE)
        left.append(jnp.concatenate([jnp.where(rows == r, g, 0.0) for r in range(ROWS)], 0).astype(bf16))
        right.append(jnp.where(big == jnp.broadcast_to(nlane[b:b + 1, :], (128, 128)), 1.0, 0.0).astype(bf16))
    out = nt(jnp.concatenate(left, 1), jnp.concatenate(right, 1))
    for r in range(ROWS):
        v = out[8 * r:8 * r + 8]
        force[r] = jnp.where(sub < 3, v + roll_rows(v, -3), 0.0)


def pack_x(force, up, down):
    for ey in range(5):
        up[ey] = force[15 + ey] + roll_rows(force[20 + ey], 3)
        down[ey] = force[ey] + roll_rows(force[5 + ey], 3)


def weight_refs(refs):
    return dict(zip(WEIGHT_NAMES, refs))


def first_pairs(table, zlo, zhi, nrow, nlane, live, crow, clane, *refs):
    w = weight_refs(refs[:11])
    tab, force, up, down = refs[11:15]
    s = dict(zip(ALL_SCRATCH, refs[15:]))
    lane = iota(1)
    for r in range(ROWS):
        k, p = r // 4, r % 4
        v = jnp.where(lane < ZLANE[1], roll_lanes(zlo[k], -32 * p), table[r])
        tab[r] = jnp.where(lane >= ZLANE[4], roll_lanes(zhi[k], ZLANE[4] - 32 * p), v)
    pair_step(tab, nrow, nlane, live, crow, clane, w, s, force)
    pack_x(force, up, down)


def unpack_z(force, zlo, zhi, r):
    sub, lane = iota(0), iota(1)
    k, p = r // 4, r % 4
    half, side = p % 2, p // 2
    below = roll_lanes(roll_rows(zlo[k], -3 * half), -64 * side)
    above = roll_lanes(roll_rows(zhi[k], -3 * half), ZLANE[3] - 64 * side)
    add = jnp.where(lane < ZLANE[2], below, jnp.where(lane >= ZLANE[3], above, 0.0))
    return force[r] + jnp.where(sub < 3, add, 0.0)


def next_pairs(force, zlo, zhi, table, nrow, nlane, live, crow, clane, *refs):
    w = weight_refs(refs[:11])
    total, force2, up, down = refs[11:15]
    s = dict(zip(ALL_SCRATCH, refs[15:]))
    sub = iota(0)
    for r in range(ROWS):
        f = unpack_z(force, zlo, zhi, r)
        if r // 5 in (1, 2, 3) and r % 5 in (1, 2, 3):
            total[(r // 5 - 1) * 3 + r % 5 - 1] = f
        mass = inverse_mass(jnp.broadcast_to(table[r, 6:7, :], TILE))
        half = (0.5 * STEP) * f * mass
        v = table[r]
        kick = roll_rows(v, -3) + half + half
        s["table"][r] = jnp.where(sub < 3, v + STEP * kick, v)
    pair_step(s["table"], nrow, nlane, live, crow, clane, w, s, force2)
    pack_x(force2, up, down)


def fold_x(force, xlo, xhi, out, up, down):
    sub = iota(0)
    for ey in range(5):
        for ex in range(5):
            v = force[5 * ex + ey]
            if ex != 2:
                got = (xlo if ex < 2 else xhi)[ey]
                got = roll_rows(got, -3 * (ex % 3))
                v = v + jnp.where(sub < 3, got, 0.0)
            out[5 * ex + ey] = v
    for ex in range(5):
        up[ex] = out[5 * ex + 3] + roll_rows(out[5 * ex + 4], 3)
        down[ex] = out[5 * ex] + roll_rows(out[5 * ex + 1], 3)


def fold_y(force, ylo, yhi, out, up, down):
    sub, lane = iota(0), iota(1)
    for ex in range(5):
        for ey in range(5):
            v = force[5 * ex + ey]
            if ey != 2:
                got = (ylo if ey < 2 else yhi)[ex]
                got = roll_rows(got, -3 * (ey % 3))
                v = v + jnp.where(sub < 3, got, 0.0)
            out[5 * ex + ey] = v
    for k in range(7):
        hi, lo = jnp.zeros(TILE, f32), jnp.zeros(TILE, f32)
        for p in range(min(4, ROWS - 4 * k)):
            half, side = p % 2, p // 2
            v = out[4 * k + p]
            here = lane < 64 if side == 0 else lane >= 64
            here = here & (sub >= 3 * half) & (sub < 3 * half + 3)
            v = roll_rows(v, 3 * half)
            hi = jnp.where(here, roll_lanes(v, 64 * side - ZLANE[3]), hi)
            lo = jnp.where(here, roll_lanes(v, 64 * side), lo)
        up[k] = hi
        down[k] = lo


def end_kernel(force, zlo, zhi, total, irow, ilane, pos, vel, frc, spec, new_pos, new_vel, new_frc):
    rows = []
    for ex in (1, 2, 3):
        for ey in (1, 2, 3):
            rows.append(unpack_z(force, zlo, zhi, 5 * ex + ey) + roll_rows(total[(ex - 1) * 3 + ey - 1], 3))
    mass = inverse_mass(spec[...].astype(f32))
    kick = vel[...] + (0.5 * STEP) * frc[...] * mass
    moved = pos[...] + STEP * kick
    for h in range(4):
        lanes = slice(128 * h, 128 * h + 128)
        ir = jnp.broadcast_to(irow[h:h + 1, :], TILE)
        il = jnp.broadcast_to(ilane[h:h + 1, :], TILE)
        acc = jnp.zeros(TILE, f32)
        for r in range(9):
            row = (r // 3 + 1) * 5 + r % 3 + 1
            acc = jnp.where(ir == row, lane_take(rows[r], il), acc)
        last, first = acc[0:3], acc[3:6]
        m = mass[:, lanes]
        half = (0.5 * STEP) * first * m
        kick2 = kick[:, lanes] + half + half
        new_pos[:, lanes] = moved[:, lanes] + STEP * kick2
        new_vel[:, lanes] = kick2 + (0.5 * STEP) * last * m
        new_frc[:, lanes] = last


ALL_SCRATCH = dict(PAIR_SCRATCH, shifted=(ROWS, 8, 128), table=(ROWS, 8, 128), spread=(8, 8, 128))


def shape(*dims, kind=f32):
    return jax.ShapeDtypeStruct(dims, kind)


def call(kernel, outs, *args, scratch=(), limit=None):
    vm = pl.BlockSpec(memory_space=pltpu.VMEM)
    return pl.pallas_call(
        kernel,
        out_shape=tuple(outs),
        in_specs=[vm] * len(args),
        out_specs=tuple([vm] * len(outs)),
        scratch_shapes=list(scratch),
        compiler_params=pltpu.CompilerParams(vmem_limit_bytes=limit) if limit else None,
    )(*args)


def swap(up, down, axis):
    n = lax.axis_size(axis)
    ahead = [(i, (i + 1) % n) for i in range(n)]
    return lax.ppermute(up, axis, ahead), lax.ppermute(down, axis, [(j, i) for i, j in ahead])


def local(positions, velocities, forces, species, cell_ids, centers, neighbours, *params):
    spec = species.reshape(1, ATOMS)
    pad = [jnp.zeros((3, 3, n), i32) for n in (27, 29)]
    cid = jnp.concatenate([pad[0], cell_ids[:, :, 0, :], cell_ids[:, :, 1, :18], cell_ids[:, :, 2, :], pad[1]], -1).reshape(9, 128)
    cen = jnp.broadcast_to(centers[:, None], TILE)
    table_shape = shape(ROWS, 8, 128)
    five, seven = shape(5, 8, 128), shape(7, 8, 128)

    t1, t2, t3 = call(start_kernel, [shape(3, 8, 128)] * 3, positions, velocities, forces, spec, cid, scratch=[pltpu.VMEM((8, ATOMS), f32)])
    xlo, xhi = swap(t3, t1, "gx")
    int_tile, flat = shape(8, 128, kind=i32), shape(4, 128, kind=i32)
    nrow, nlane, live, crow, clane, irow, ilane = call(
        index_kernel, [int_tile, int_tile, shape(8, 128), int_tile, int_tile, flat, flat], neighbours, cen, cid)
    idx = (nrow, nlane, live, crow, clane)
    weights = prepare(*params)
    ylo, yhi = swap(*call(second_kernel, [five, five], xlo, t1, t2, t3, xhi), "gy")
    table, up, down = call(third_kernel, [table_shape, seven, seven], xlo, t1, t2, t3, xhi, ylo, yhi)
    zlo, zhi = swap(up, down, "gz")
    scratch = [pltpu.VMEM(v, f32) for v in ALL_SCRATCH.values()]
    table, force, up, down = call(
        first_pairs, [table_shape, table_shape, five, five], table, zlo, zhi, *idx, *weights, scratch=scratch, limit=24 << 20)

    def fold(force, up, down):
        xlo, xhi = swap(up, down, "gx")
        force, up, down = call(fold_x, [table_shape, five, five], force, xlo, xhi)
        ylo, yhi = swap(up, down, "gy")
        force, up, down = call(fold_y, [table_shape, seven, seven], force, ylo, yhi)
        zlo, zhi = swap(up, down, "gz")
        return force, zlo, zhi

    total, force, up, down = call(
        next_pairs, [shape(9, 8, 128), table_shape, five, five], *fold(force, up, down), table, *idx, *weights, scratch=scratch,
        limit=24 << 20)
    out = [shape(3, ATOMS)] * 3
    return call(end_kernel, out, *fold(force, up, down), total, irow, ilane, positions, velocities, forces, spec)


def solution(mesh):
    from jax.sharding import PartitionSpec as P

    axes = ("gx", "gy", "gz")
    rows = P(None, axes)
    in_specs = (rows, rows, rows, P(axes), P(*axes, None), P(axes), P(axes, None)) + (P(),) * 7
    return jax.shard_map(local, mesh=mesh, in_specs=in_specs, out_specs=(rows, rows, rows), check_vma=False)
```

```python
import math
import jax, jax.numpy as jnp
from jax import lax
from jax.experimental import pallas as pl
from jax.experimental.pallas import tpu as pltpu

f32, bf16, i32 = jnp.float32, jnp.bfloat16, jnp.int32
NB, BLK, C = 8, 128, 64
PAIRS = NB * BLK
R3, R5, R15 = math.sqrt(3.0), math.sqrt(5.0), math.sqrt(15.0)

def nt(a, b):
    return lax.dot_general(a, b, (((1,), (1,)), ((), ())), preferred_element_type=f32)

def nn(a, b):
    return jnp.dot(a, b, preferred_element_type=f32)

def split(x):
    hi = x.astype(bf16)
    return hi, (x - hi.astype(f32)).astype(bf16)

def stack3(x):
    hi, lo = split(x)
    return jnp.concatenate([hi, lo, hi], 0)

def sigmoid(z):
    return 0.5 * jnp.tanh(0.5 * z) + 0.5

def harmonic_rows(ux, uy, uz):
    return [jnp.ones_like(ux), R3 * ux, R3 * uy, R3 * uz, R15 * ux * uy, R15 * uy * uz,
            0.5 * R5 * (3.0 * uz * uz - 1.0), R15 * ux * uz, 0.5 * R15 * (ux * ux - uy * uy)]

def wide(ref, rows):
    return jnp.concatenate([jnp.broadcast_to(ref[b:b + 1, :], (rows, BLK)) for b in range(NB)], 1)

def pair_grads(disp, kc, kn, live, w, s):
    dx, dy, dz = disp
    r = jnp.sqrt(dx * dx + dy * dy + dz * dz + 0.09)
    rinv = 1.0 / r
    ux, uy, uz = dx * rinv, dy * rinv, dz * rinv
    q = jnp.minimum(r * (1.0 / 6.0), 1.0)
    q2 = q * q
    q4 = q2 * q2
    q5 = q4 * q
    q6 = q4 * q2
    f = (1.0 - 28.0 * q6 + 48.0 * (q6 * q) - 21.0 * (q6 * q2)) * live
    fp = -28.0 * q5 * (1.0 - q) * (1.0 - q) * live
    theta = math.pi * q
    s1, c1 = jnp.sin(theta), jnp.cos(theta)
    sm, cm = s1, c1
    norm = math.sqrt(1.0 / 3.0)
    rn = norm * rinv
    slopes = []
    for m in range(8):
        basis = sm * rn
        s["feat"][m] = basis
        slopes.append((cm * (math.pi / 6.0 * (m + 1)) - sm * rinv) * rn)
        sm, cm = sm * c1 + cm * s1, cm * c1 - sm * s1
    ys = harmonic_rows(ux, uy, uz)
    for n in range(9):
        s["harm"][n] = ys[n]
    for n in range(9, 16):
        s["harm"][n] = jnp.zeros((8, 128), f32)
    s["sc"][0] = f
    s["sc"][1] = kc
    s["sc"][2] = kn
    fw = wide(s["sc"].at[0], 1)

    sub8 = lax.broadcasted_iota(i32, (8, BLK), 0).astype(f32)
    feats = []
    for b in range(NB):
        hot = jnp.where(sub8 < 4.0, jnp.broadcast_to(s["sc"][1, b:b + 1, :], (8, BLK)),
                        jnp.broadcast_to(s["sc"][2, b:b + 1, :], (8, BLK)) + 4.0) == sub8
        feats.append(jnp.concatenate([s["feat"][:, b, :], hot.astype(f32)], 0))
    feat = jnp.concatenate(feats, 1)

    z1 = nn(w["emb"][...], stack3(feat))
    g1 = sigmoid(z1)
    h = z1 * g1
    s["d1"][...] = g1 + h * (1.0 - g1)
    z2 = nn(w["mix"][...], stack3(h))
    g2 = sigmoid(z2)
    a = z2 * g2
    s["d2"][...] = g2 + a * (1.0 - g2)
    s["a"][...] = a
    x = a * fw
    vw = nn(w["ve"][...], stack3(x))
    s["vw"][...] = vw

    zero = jnp.zeros((16, BLK), f32)
    bd_h, bd_l, bd3, rep = [], [], [], []
    for j in range(NB // 2):
        y0, y1 = s["harm"][:, 2 * j, :], s["harm"][:, 2 * j + 1, :]
        bd = jnp.concatenate([jnp.concatenate([y0, zero], 1), jnp.concatenate([zero, y1], 1)], 0)
        hi, lo = split(bd)
        bd3.append(jnp.concatenate([hi, lo, hi], 0))
        rh, rl = jnp.concatenate([hi, hi, hi], 0), jnp.concatenate([lo, lo, lo], 0)
        rep.append(jnp.concatenate([rh, rl, rh], 1))

    row = lax.broadcasted_iota(i32, (192, 96), 0) // C
    col = lax.broadcasted_iota(i32, (192, 96), 1)
    part = col % 16
    order = jnp.where(part == 0, 0, jnp.where(part < 4, 1, jnp.where(part < 9, 2, 3)))
    mask = jnp.where(row == order, 0.1, 0.0).astype(f32)

    def moments(val, j):
        hi, lo = split(val)
        return nt(jnp.concatenate([hi, hi, lo], 1), rep[j]) * mask

    def sharp(m):
        hi, lo = split(m)
        return jnp.where(col < 64, hi.astype(f32), lo.astype(f32)).astype(bf16)

    sums, tees = [], []
    for j in range(NB // 2):
        lanes = slice(256 * j, 256 * j + 256)
        m = moments(s["vw"][192:384, lanes], j)
        s["sums"][j] = m
        t = nn(sharp(m), bd3[j])
        s["t"][:, lanes] = t
    sc = s["vw"][0:192, :] * s["t"][...]
    z3 = nn(w["lat"][...], stack3(jnp.concatenate([x, sc], 0)))
    g3 = sigmoid(z3)
    bb = z3 * g3
    s["d3"][...] = g3 + bb * (1.0 - g3)
    x2 = x + bb * fw
    z4 = nn(w["head"][...], stack3(x2))
    g4 = sigmoid(z4)
    hh = z4 * g4
    wen = jnp.concatenate([w["energy"][...]] * NB, 1)
    e = jnp.sum(wen * hh, 0, keepdims=True)
    dz4 = wen * fw * (g4 + hh * (1.0 - g4))
    dx2 = nn(w["head_t"][...], stack3(dz4))
    df = e + jnp.sum(dx2 * bb, 0, keepdims=True)
    dz3 = dx2 * fw * s["d3"][...]
    dc = nn(w["lat_t"][...], stack3(dz3))
    dxa = dx2 + dc[0:64]
    ds = dc[64:256]
    s["dv"][...] = ds * s["t"][...]
    s["dt"][...] = ds * s["vw"][0:192, :]
    for j in range(NB // 2):
        lanes = slice(256 * j, 256 * j + 256)
        dt = s["dt"][:, lanes]
        m = moments(dt, j)
        s["dw"][:, lanes] = nn(sharp(m), bd3[j])
        acc = None
        for left, right in ((s["sums"][j], dt), (m, s["vw"][192:384, lanes])):
            lt = jnp.transpose(jnp.concatenate([left, jnp.zeros((192, 32), f32)], 1))[0:32]
            lh, ll = split(lt)
            rh, rl = split(right)
            both = nn(jnp.concatenate([lh, ll], 0), rh)
            one = both[0:32] + both[32:64] + nn(lh, rl)
            acc = one if acc is None else acc + one
        s["dy"][2 * j] = acc[0:16, 0:128]
        s["dy"][2 * j + 1] = acc[16:32, 128:256]
    dx = dxa + nn(w["ve_t"][...], stack3(jnp.concatenate([s["dv"][...], s["dw"][...]], 0)))
    df = df + jnp.sum(dx * s["a"][...], 0, keepdims=True)
    for b in range(NB):
        s["sc"][3, b:b + 1, :] = df[:, 128 * b:128 * b + 128]
    dz2 = dx * fw * s["d2"][...]
    dz1 = nn(w["mix_t"][...], stack3(dz2)) * s["d1"][...]
    dr8 = nn(w["emb_t"][...], stack3(dz1))
    for b in range(NB):
        s["dr"][b] = dr8[0:8, 128 * b:128 * b + 128]

    dr = s["sc"][3] * fp
    for m in range(8):
        dr = dr + s["dr"][:, m, :] * slopes[m]
    gy = [s["dy"][:, n, :] for n in range(9)]
    dux = R3 * gy[1] + R15 * (uy * gy[4] + uz * gy[7] + ux * gy[8])
    duy = R3 * gy[2] + R15 * (ux * gy[4] + uz * gy[5] - uy * gy[8])
    duz = R3 * gy[3] + R15 * (uy * gy[5] + ux * gy[7]) + (3.0 * R5) * uz * gy[6]
    dot = dux * ux + duy * uy + duz * uz
    along = dr - dot * rinv
    scale = 50.0
    return [scale * (du * rinv + along * u) for du, u in ((dux, ux), (duy, uy), (duz, uz))]

PAIR_SCRATCH = {
    "feat": (8, 8, 128), "harm": (16, 8, 128), "sc": (4, 8, 128), "d1": (C, PAIRS), "d2": (C, PAIRS), "a": (C, PAIRS),
    "vw": (384, PAIRS), "sums": (4, 192, 96), "t": (192, PAIRS), "d3": (C, PAIRS), "dv": (192, PAIRS), "dt": (192, PAIRS),
    "dw": (192, PAIRS), "dy": (8, 16, 128), "dr": (8, 8, 128),
}
WEIGHT_NAMES = ("emb", "mix", "ve", "lat", "head", "head_t", "lat_t", "ve_t", "mix_t", "emb_t", "energy")


SIDE = 8
ATOMS = SIDE ** 3
ROWS = 25
STEP = 0.1
MASSES = (1.008, 15.999, 22.99, 35.453)
ZLANE = (0, 27, 54, 72, 99)
WIDTHS = (3, 2, 3)
EDGE = 2.0 * SIDE
TILE = (8, 128)
AXES = ("gx", "gy", "gz")
SIZES = (16, 8, 8)
FIRST_A, FIRST_B, SUM_CHUNK = 3, 4, 7


def iota(dim, shape=TILE):
    return lax.broadcasted_iota(i32, shape, dim)


def lane_take(row, idx):
    return jnp.take_along_axis(row, idx, axis=1)


def roll_rows(v, shift):
    return v if shift % 8 == 0 else pltpu.roll(v, shift % 8, 0)


def roll_lanes(v, shift):
    return v if shift % 128 == 0 else pltpu.roll(v, shift % 128, 1)


def inverse_mass(kind):
    out = jnp.full(kind.shape, 1.0 / MASSES[3], f32)
    for k in range(3):
        out = jnp.where(kind == float(k), 1.0 / MASSES[k], out)
    return out


def parity():
    return [lax.axis_index(a) & 1 for a in AXES]


def place_in(side):
    p = parity()
    return (p[0] * 4 + p[1] * 2 + p[2]) ^ (7 if side else 0)


def pack4(rows, start):
    lane = iota(1)
    out = []
    for k in range(0, len(rows), 4):
        v = roll_lanes(rows[k], -start)
        for p in range(1, len(rows[k:k + 4])):
            v = jnp.where(lane >= 32 * p, roll_lanes(rows[k + p], 32 * p - start), v)
        out.append(v)
    return out


def start_kernel(pos, vel, frc, spec, cells, chunks, mid, cid, own, raw):
    px, py, pz = parity()
    kind = spec[...].astype(f32)
    mass = inverse_mass(kind)
    kick = vel[...] + (0.5 * STEP) * frc[...] * mass
    own[0:3, :] = pos[...] + STEP * kick
    own[3:6, :] = kick
    own[6:7, :] = kind
    own[7:8, :] = jnp.zeros_like(kind)
    raw[...] = jnp.zeros((128, 128), i32)
    for x in range(3):
        for y in range(3):
            at = 8 * (3 * x + y)
            raw[at:at + 3, 0:27] = cells[x + px * (2 - 2 * x), y + py * (2 - 2 * y)]
    z0, z1, z2 = (raw[pl.ds(k, 16, stride=8), :] for k in range(3))
    lane = iota(1, (16, 128))
    flip = jnp.full((16, 128), pz, i32) == 1
    ids = jnp.where(lane < ZLANE[2], pltpu.roll(jnp.where(flip, z2, z0), ZLANE[1], 1),
                    jnp.where(lane < ZLANE[3], pltpu.roll(z1, ZLANE[2], 1), pltpu.roll(jnp.where(flip, z0, z2), ZLANE[3], 1)))
    cid[...] = jnp.where((lane >= ZLANE[1]) & (lane < ZLANE[4]), ids, 0)
    cuts = [own[:, 128 * h:128 * h + 128] for h in range(4)]
    rows = []
    for r in range(9):
        ids = jnp.broadcast_to(cid[r:r + 1, :], TILE)
        lo, hi = ids & 127, ids >> 7
        acc = lane_take(cuts[0], lo)
        for h in range(1, 4):
            acc = jnp.where(hi == h, lane_take(cuts[h], lo), acc)
        mid[r] = acc
        rows.append(acc)
    me = place_in(0)
    zs = ZLANE[3]
    for d, tiles in ((4, rows[6:9]), (2, rows[2::3]), (6, rows[8:9]), (1, pack4(rows, zs)), (5, pack4(rows[6:9], zs)),
                     (3, pack4(rows[2::3], zs)), (7, pack4(rows[8:9], zs))):
        for k, v in enumerate(tiles):
            chunks[me ^ d, k] = v


def widen(have, got, me, face):
    lane = iota(1)
    beyond = (lambda: lane >= ZLANE[4]) if face else (lambda: lane < ZLANE[1])
    at = ZLANE[face]
    xs = sorted({x for x, _ in have})
    rows = sorted(have)

    def strip(d, keys, base):
        out = {}
        for n, key in enumerate(keys):
            v = roll_lanes(got[me ^ d, n // 4], at - 32 * (n % 4))
            out[key] = jnp.where(beyond(), v, base[key])
        return out

    new = strip(1, rows, have)
    new.update(strip(5, [(face, y) for y in xs], {(face, y): got[me ^ 4, n] for n, y in enumerate(xs)}))
    new.update(strip(3, [(x, face) for x in xs], {(x, face): got[me ^ 2, n] for n, x in enumerate(xs)}))
    new.update(strip(7, [(face, face)], {(face, face): got[me ^ 6, 0]}))
    return new


def second_kernel(got, mid, table, chunks):
    have = {(r // 3 + 1, r % 3 + 1): mid[r] for r in range(9)}
    have = widen(have, got, place_in(0), 4)
    for (x, y), v in have.items():
        table[4 * (x - 1) + y - 1] = v
    me = place_in(1)
    zs = ZLANE[1]
    along_x = [have[1, y] for y in range(1, 5)]
    along_y = [have[x, 1] for x in range(1, 5)]
    whole = [have[x, y] for x in range(1, 5) for y in range(1, 5)]
    for d, tiles in ((4, along_x), (2, along_y), (6, along_x[:1]), (1, pack4(whole, zs)), (5, pack4(along_x, zs)),
                     (3, pack4(along_y, zs)), (7, pack4(along_x[:1], zs))):
        for k, v in enumerate(tiles):
            chunks[me ^ d, k] = v


def prepare_kernel(neigh, cen, cid, emb, mix, val, env, lat, head, energy,
                   nrow, nlane, live, crow, clane, irow, ilane, *out):
    sub, lane = iota(0), iota(1)
    big = iota(0, (128, 128))
    left, right = [], []
    for r in range(9):
        area = WIDTHS[r // 3] * WIDTHS[r % 3]
        ids = jnp.broadcast_to(cid[r:r + 1, :], TILE)
        valid = (lane >= 27) & (lane < 27 + 3 * area)
        valid = valid | ((lane >= 54) & (lane < 54 + 2 * area))
        valid = valid | ((lane >= 72) & (lane < 72 + 3 * area))
        row = (r // 3 + 1) * 5 + r % 3 + 1
        value = jnp.where((sub & 1) == 0, row, lane)
        left.append(jnp.where(valid & ((ids >> 7) == (sub >> 1)), value, 0).astype(f32).astype(bf16))
        lo = jnp.broadcast_to(cid[r:r + 1, :], (128, 128)) & 127
        right.append(jnp.where(big == lo, 1.0, 0.0).astype(bf16))
    inv = nt(jnp.concatenate(left, 1), jnp.concatenate(right, 1))
    inv = (inv + 0.5).astype(i32)
    for h in range(4):
        irow[h:h + 1, :] = inv[2 * h:2 * h + 1, :]
        ilane[h:h + 1, :] = inv[2 * h + 1:2 * h + 2, :]
    px, py, pz = parity()

    def flip(e, p):
        return e + p * (4 - 2 * e)

    def place(n):
        lo, hi = n & 127, n >> 7
        row = jnp.zeros(TILE, i32)
        col = jnp.zeros(TILE, i32)
        for h in range(4):
            row = jnp.where(hi == h, lane_take(jnp.broadcast_to(irow[h:h + 1, :], TILE), lo), row)
            col = jnp.where(hi == h, lane_take(jnp.broadcast_to(ilane[h:h + 1, :], TILE), lo), col)
        m = jnp.maximum(n - ATOMS, 0)
        grow = ((m.astype(f32) + 0.5) * (1.0 / 135.0)).astype(i32)
        rem = m - 135 * grow
        ex = ((grow.astype(f32) + 0.5) * 0.2).astype(i32)
        ey = grow - 5 * ex
        ez = ((rem.astype(f32) + 0.5) * (1.0 / 27.0)).astype(i32)
        slot = rem - 27 * ez
        ex, ey, ez = flip(ex, px), flip(ey, py), flip(ez, pz)
        first = jnp.where(ez == 0, 0, jnp.where(ez == 1, 27, jnp.where(ez == 2, 54, jnp.where(ez == 3, 72, 99))))
        return jnp.where(hi < 4, row, 5 * ex + ey), jnp.where(hi < 4, col, first + slot)

    n = neigh[...]
    c = jnp.concatenate([cen[...].astype(f32), jnp.zeros((1, 120), f32)], 1)
    c = jnp.sum(jnp.where(lane == sub, jnp.broadcast_to(c, TILE), 0.0), 1, keepdims=True)
    c = (jnp.broadcast_to(c, TILE) + 0.5).astype(i32)
    nrow[...], nlane[...] = place(n)
    crow[...], clane[...] = place(c)
    live[...] = jnp.where(n != c, 1.0, 0.0)

    def stack(w):
        hi = w.astype(bf16).astype(f32)
        return jnp.concatenate([hi, hi, w - hi], 1).astype(bf16)

    ve_t = jnp.concatenate([val[...], env[...]], 1)
    emb_t = jnp.concatenate([emb[0:8, :], jnp.zeros((8, C), f32)], 0)
    wide_energy = jnp.broadcast_to(energy[...], (128, C))
    tiles = (stack(emb[...].T), stack(mix[...]), stack(ve_t.T), stack(lat[...]), stack(head[...]), stack(head[...].T),
             stack(lat[...].T), stack(ve_t), stack(mix[...].T), stack(emb_t), wide_energy.T)
    for ref, v in zip(out, tiles):
        ref[...] = v


def pair_step(tab, nrow, nlane, live, crow, clane, w, s, force):
    sub, lane = iota(0), iota(1)
    px, py, pz = (1.0 - 2.0 * p.astype(f32) for p in parity())
    zshift = jnp.where(lane < ZLANE[1], -EDGE, jnp.where(lane >= ZLANE[4], EDGE, 0.0)) * pz
    zshift = jnp.where(sub == 2, zshift, 0.0)
    xshift = jnp.where(sub == 0, EDGE, 0.0) * px
    yshift = jnp.where(sub == 1, EDGE, 0.0) * py
    nr, nl, cr, cl = nrow[...], nlane[...], crow[...], clane[...]
    near = [jnp.zeros(TILE, f32) for _ in range(4)]
    centre = [jnp.zeros(TILE, f32) for _ in range(4)]
    for r in range(ROWS):
        ex, ey = r // 5, r % 5
        shift = zshift
        if ex in (0, 4):
            shift = shift + xshift * float(ex // 2 - 1)
        if ey in (0, 4):
            shift = shift + yshift * float(ey // 2 - 1)
        s["shifted"][r] = tab(ex, ey) + shift
        mine = nr == r
        centred = cr == r
        for k, q in enumerate((0, 1, 2, 6)):
            line = jnp.broadcast_to(s["shifted"][r, q:q + 1, :], TILE)
            near[k] = jnp.where(mine, lane_take(line, nl), near[k])
            if ex in (1, 2, 3) and ey in (1, 2, 3):
                centre[k] = jnp.where(centred, lane_take(line, cl), centre[k])
    alive = live[...]
    disp = [near[k] - centre[k] for k in range(3)]
    grads = pair_grads(disp, centre[3], near[3], alive, w, s)
    spare = 1.0 / jnp.sum(1.0 - alive, 1, keepdims=True)
    for k, g in enumerate(grads):
        g = jnp.where(alive > 0.0, -g, jnp.sum(g, 1, keepdims=True) * spare)
        hi = g.astype(bf16).astype(f32)
        s["spread"][k] = hi
        s["spread"][k + 3] = g - hi
    s["spread"][6] = jnp.zeros(TILE, f32)
    s["spread"][7] = jnp.zeros(TILE, f32)
    big = iota(0, (128, 128))
    left, right = [], []
    for b in range(NB):
        g = s["spread"][:, b, :]
        rows = jnp.broadcast_to(nrow[b:b + 1, :], TILE)
        left.append(jnp.concatenate([jnp.where(rows == r, g, 0.0) for r in range(ROWS)], 0).astype(bf16))
        right.append(jnp.where(big == jnp.broadcast_to(nlane[b:b + 1, :], (128, 128)), 1.0, 0.0).astype(bf16))
    out = nt(jnp.concatenate(left, 1), jnp.concatenate(right, 1))
    for r in range(ROWS):
        v = out[8 * r:8 * r + 8]
        force[r] = jnp.where(sub < 3, v + roll_rows(v, -3), 0.0)


def sum_messages(force, chunks, side):
    lane, sub = iota(1), iota(0)
    me = place_in(side)
    near, far = (1, 0) if side else (3, 4)
    head, tail = (near, far) if side else (far, near)
    upper = sub >= 3
    twice = [force[r] + roll_rows(force[r], 3) for r in range(ROWS)]

    def two(a, b):
        return jnp.where(upper, twice[b], twice[a])

    def strips(rows):
        out = []
        for k in range(0, len(rows), 4):
            part = rows[k:k + 4]
            pairs = [two(part[i], part[min(i + 1, len(part) - 1)]) for i in range(0, len(part), 2)]
            v = None
            for n, q in enumerate(pairs):
                t = jnp.where(lane < 64 * n + 27, roll_lanes(q, 64 * n - ZLANE[head]), roll_lanes(q, 64 * n + 27 - ZLANE[tail]))
                v = t if v is None else jnp.where(lane >= 64, t, v)
            out.append(v)
        return out

    xr = [[5 * x + y for y in range(5)] for x in (far, near)]
    yr = [[5 * x + y for x in range(5)] for y in (far, near)]
    corner = [5 * x + y for x in (far, near) for y in (far, near)]
    for d, tiles in ((4, [two(xr[0][k], xr[1][k]) for k in range(5)]), (2, [two(yr[0][k], yr[1][k]) for k in range(5)]),
                     (6, [two(corner[0], corner[1]), two(corner[2], corner[3])]), (1, strips(list(range(ROWS)))),
                     (5, strips(xr[0] + xr[1])), (3, strips(yr[0] + yr[1])), (7, strips(corner))):
        for k, v in enumerate(tiles):
            chunks[me ^ d, k] = v


def add_messages(force, got, side, wanted=tuple(range(ROWS))):
    lane, sub = iota(1), iota(0)
    me = place_in(side)
    near, far = (1, 0) if side else (3, 4)
    out = {r: force[r] for r in wanted}

    def add(r, v, mask=None):
        keep = sub < 3 if mask is None else (sub < 3) & mask
        if r in out:
            out[r] = out[r] + jnp.where(keep, v, 0.0)

    def add_strips(d, rows):
        for n, r in enumerate(rows):
            if r not in out:
                continue
            v = got[me ^ d, n // 4]
            v = roll_rows(v, -3 * (n % 2))
            v = roll_lanes(v, min(ZLANE[near], ZLANE[far]) - 64 * ((n % 4) // 2))
            add(r, v, lane >= ZLANE[3] if side == 0 else lane < ZLANE[2])

    xr = [[5 * x + y for y in range(5)] for x in (near, far)]
    yr = [[5 * x + y for x in range(5)] for y in (near, far)]
    corner = [5 * x + y for x in (near, far) for y in (near, far)]
    for k in range(5):
        for half in range(2):
            add(xr[half][k], roll_rows(got[me ^ 4, k], -3 * half))
            add(yr[half][k], roll_rows(got[me ^ 2, k], -3 * half))
    for n, r in enumerate(corner):
        add(r, roll_rows(got[me ^ 6, n // 2], -3 * (n % 2)))
    add_strips(1, list(range(ROWS)))
    add_strips(5, xr[0] + xr[1])
    add_strips(3, yr[0] + yr[1])
    add_strips(7, corner)
    return out


def weight_refs(refs):
    return dict(zip(WEIGHT_NAMES, refs))


def first_pairs(part, got, nrow, nlane, live, crow, clane, *refs):
    w = weight_refs(refs[:11])
    tab, force, chunks = refs[11:14]
    s = dict(zip(ALL_SCRATCH, refs[14:]))
    have = {(x, y): part[4 * (x - 1) + y - 1] for x in range(1, 5) for y in range(1, 5)}
    for (x, y), v in widen(have, got, place_in(1), 0).items():
        tab[5 * x + y] = v
    pair_step(lambda x, y: tab[5 * x + y], nrow, nlane, live, crow, clane, w, s, force)
    sum_messages(force, chunks, 0)


def next_pairs(force, got, table, nrow, nlane, live, crow, clane, *refs):
    w = weight_refs(refs[:11])
    total, force2, chunks = refs[11:14]
    s = dict(zip(ALL_SCRATCH, refs[14:]))
    sub = iota(0)
    for r, f in add_messages(force, got, 1).items():
        if r // 5 in (1, 2, 3) and r % 5 in (1, 2, 3):
            total[(r // 5 - 1) * 3 + r % 5 - 1] = f
        mass = inverse_mass(jnp.broadcast_to(table[r, 6:7, :], TILE))
        half = (0.5 * STEP) * f * mass
        v = table[r]
        kick = roll_rows(v, -3) + half + half
        s["table"][r] = jnp.where(sub < 3, v + STEP * kick, v)
    pair_step(lambda x, y: s["table"][5 * x + y], nrow, nlane, live, crow, clane, w, s, force2)
    sum_messages(force2, chunks, 0)


def fold_kernel(force, got, out, chunks):
    for r, v in add_messages(force, got, 0).items():
        out[r] = v
    sum_messages(out, chunks, 1)


def end_kernel(force, got, total, irow, ilane, pos, vel, frc, spec, new_pos, new_vel, new_frc):
    middle = [5 * x + y for x in (1, 2, 3) for y in (1, 2, 3)]
    summed = add_messages(force, got, 1, tuple(middle))
    rows = [summed[r] + roll_rows(total[k], 3) for k, r in enumerate(middle)]
    mass = inverse_mass(spec[...].astype(f32))
    kick = vel[...] + (0.5 * STEP) * frc[...] * mass
    moved = pos[...] + STEP * kick
    for h in range(4):
        lanes = slice(128 * h, 128 * h + 128)
        ir = jnp.broadcast_to(irow[h:h + 1, :], TILE)
        il = jnp.broadcast_to(ilane[h:h + 1, :], TILE)
        acc = jnp.zeros(TILE, f32)
        for k, r in enumerate(middle):
            acc = jnp.where(ir == r, lane_take(rows[k], il), acc)
        last, first = acc[0:3], acc[3:6]
        m = mass[:, lanes]
        half = (0.5 * STEP) * first * m
        kick2 = kick[:, lanes] + half + half
        new_pos[:, lanes] = moved[:, lanes] + STEP * kick2
        new_vel[:, lanes] = kick2 + (0.5 * STEP) * last * m
        new_frc[:, lanes] = last


ALL_SCRATCH = dict(PAIR_SCRATCH, shifted=(ROWS, 8, 128), table=(ROWS, 8, 128), spread=(8, 8, 128))


def shape(*dims, kind=f32):
    return jax.ShapeDtypeStruct(dims, kind)


def call(kernel, outs, *args, scratch=(), limit=4 << 20, flops=1 << 20):
    vm = pl.BlockSpec(memory_space=pltpu.VMEM)
    return pl.pallas_call(
        kernel,
        out_shape=tuple(outs),
        in_specs=[vm] * len(args),
        out_specs=tuple([vm] * len(outs)),
        scratch_shapes=list(scratch),
        compiler_params=pltpu.CompilerParams(vmem_limit_bytes=limit),
        cost_estimate=pl.CostEstimate(flops=flops, bytes_accessed=1 << 18, transcendentals=0),
    )(*args)


def groups(side):
    out = []
    for x in range(side, SIZES[0] + side, 2):
        for y in range(side, SIZES[1] + side, 2):
            for z in range(side, SIZES[2] + side, 2):
                out.append([(((x + a) % SIZES[0]) * SIZES[1] + (y + b) % SIZES[1]) * SIZES[2] + (z + c) % SIZES[2]
                            for a in range(2) for b in range(2) for c in range(2)])
    return out


def trade(chunks, side):
    return lax.all_to_all(chunks, AXES, 0, 0, axis_index_groups=groups(side), tiled=True)


def local(positions, velocities, forces, species, cell_ids, centers, neighbours,
          w_embed, w_mix, w_value, w_env, w_latent, w_head, w_energy):
    spec = species.reshape(1, ATOMS)
    table_shape = shape(ROWS, 8, 128)
    sums = shape(8, SUM_CHUNK, 8, 128)
    int_tile, flat = shape(8, 128, kind=i32), shape(4, 128, kind=i32)

    chunks, mid, cid = call(
        start_kernel, [shape(8, FIRST_A, 8, 128), shape(9, 8, 128), shape(16, 128, kind=i32)],
        positions, velocities, forces, spec, cell_ids, scratch=[pltpu.VMEM((8, ATOMS), f32), pltpu.VMEM((128, 128), i32)])
    got = trade(chunks, 0)
    weight_shapes = [shape(m, k, kind=bf16) for m, k in (
        (C, 48), (C, 192), (384, 192), (C, 768), (C, 192), (C, 192), (256, 192), (C, 1152), (C, 192), (16, 192))]
    prepared = call(
        prepare_kernel, [int_tile, int_tile, shape(8, 128), int_tile, int_tile, flat, flat] + weight_shapes + [shape(C, 128)],
        neighbours, centers.reshape(1, NB), cid, w_embed.T, w_mix, w_value[0].T, w_env[0].T, w_latent[0], w_head, w_energy.reshape(1, C))
    idx, (irow, ilane), weights = prepared[:5], prepared[5:7], prepared[7:]
    part, chunks = call(second_kernel, [shape(16, 8, 128), shape(8, FIRST_B, 8, 128)], got, mid)
    got = trade(chunks, 1)
    scratch = [pltpu.VMEM(v, f32) for v in ALL_SCRATCH.values()]
    table, force, chunks = call(
        first_pairs, [table_shape, table_shape, sums], part, got, *idx, *weights, scratch=scratch, limit=24 << 20, flops=1 << 30)

    def fold(force, chunks):
        force, chunks = call(fold_kernel, [table_shape, sums], force, trade(chunks, 0))
        return force, trade(chunks, 1)

    total, force, chunks = call(
        next_pairs, [shape(9, 8, 128), table_shape, sums], *fold(force, chunks), table, *idx, *weights, scratch=scratch,
        limit=24 << 20, flops=1 << 30)
    out = [shape(3, ATOMS)] * 3
    return call(end_kernel, out, *fold(force, chunks), total, irow, ilane, positions, velocities, forces, spec)


def solution(mesh):
    from jax.sharding import PartitionSpec as P

    rows = P(None, AXES)
    in_specs = (rows, rows, rows, P(AXES), P(*AXES, None), P(AXES), P(AXES, None)) + (P(),) * 7
    return jax.shard_map(local, mesh=mesh, in_specs=in_specs, out_specs=(rows, rows, rows), check_vma=False)
```

```python
import math
import jax, jax.numpy as jnp
from jax import lax
from jax.experimental import pallas as pl
from jax.experimental.pallas import tpu as pltpu

f32, bf16, i32 = jnp.float32, jnp.bfloat16, jnp.int32
NB, BLK, C = 8, 128, 64
PAIRS = NB * BLK
R3, R5, R15 = math.sqrt(3.0), math.sqrt(5.0), math.sqrt(15.0)

def nt(a, b):
    return lax.dot_general(a, b, (((1,), (1,)), ((), ())), preferred_element_type=f32)

def nn(a, b):
    return jnp.dot(a, b, preferred_element_type=f32)

def split(x):
    hi = x.astype(bf16)
    return hi, (x - hi.astype(f32)).astype(bf16)

def stack3(x):
    hi, lo = split(x)
    return jnp.concatenate([hi, lo, hi], 0)

def sigmoid(z):
    return 0.5 * jnp.tanh(0.5 * z) + 0.5

def harmonic_rows(ux, uy, uz):
    return [jnp.ones_like(ux), R3 * ux, R3 * uy, R3 * uz, R15 * ux * uy, R15 * uy * uz,
            0.5 * R5 * (3.0 * uz * uz - 1.0), R15 * ux * uz, 0.5 * R15 * (ux * ux - uy * uy)]

def wide(ref, rows):
    return jnp.concatenate([jnp.broadcast_to(ref[b:b + 1, :], (rows, BLK)) for b in range(NB)], 1)

def pair_grads(disp, kc, kn, live, w, s):
    dx, dy, dz = disp
    r = jnp.sqrt(dx * dx + dy * dy + dz * dz + 0.09)
    rinv = 1.0 / r
    ux, uy, uz = dx * rinv, dy * rinv, dz * rinv
    q = jnp.minimum(r * (1.0 / 6.0), 1.0)
    q2 = q * q
    q4 = q2 * q2
    q5 = q4 * q
    q6 = q4 * q2
    f = (1.0 - 28.0 * q6 + 48.0 * (q6 * q) - 21.0 * (q6 * q2)) * live
    fp = -28.0 * q5 * (1.0 - q) * (1.0 - q) * live
    theta = math.pi * q
    s1, c1 = jnp.sin(theta), jnp.cos(theta)
    sm, cm = s1, c1
    norm = math.sqrt(1.0 / 3.0)
    rn = norm * rinv
    slopes = []
    for m in range(8):
        basis = sm * rn
        s["feat"][m] = basis
        slopes.append((cm * (math.pi / 6.0 * (m + 1)) - sm * rinv) * rn)
        sm, cm = sm * c1 + cm * s1, cm * c1 - sm * s1
    ys = harmonic_rows(ux, uy, uz)
    for n in range(9):
        s["harm"][n] = ys[n]
    for n in range(9, 16):
        s["harm"][n] = jnp.zeros((8, 128), f32)
    s["sc"][0] = f
    s["sc"][1] = kc
    s["sc"][2] = kn
    fw = wide(s["sc"].at[0], 1)

    sub8 = lax.broadcasted_iota(i32, (8, BLK), 0).astype(f32)
    feats = []
    for b in range(NB):
        hot = jnp.where(sub8 < 4.0, jnp.broadcast_to(s["sc"][1, b:b + 1, :], (8, BLK)),
                        jnp.broadcast_to(s["sc"][2, b:b + 1, :], (8, BLK)) + 4.0) == sub8
        feats.append(jnp.concatenate([s["feat"][:, b, :], hot.astype(f32)], 0))
    feat = jnp.concatenate(feats, 1)

    z1 = nn(w["emb"][...], stack3(feat))
    g1 = sigmoid(z1)
    h = z1 * g1
    s["d1"][...] = g1 + h * (1.0 - g1)
    z2 = nn(w["mix"][...], stack3(h))
    g2 = sigmoid(z2)
    a = z2 * g2
    s["d2"][...] = g2 + a * (1.0 - g2)
    s["a"][...] = a
    x = a * fw
    vw = nn(w["ve"][...], stack3(x))
    s["vw"][...] = vw

    zero = jnp.zeros((16, BLK), f32)
    bd_h, bd_l, bd3, rep = [], [], [], []
    for j in range(NB // 2):
        y0, y1 = s["harm"][:, 2 * j, :], s["harm"][:, 2 * j + 1, :]
        bd = jnp.concatenate([jnp.concatenate([y0, zero], 1), jnp.concatenate([zero, y1], 1)], 0)
        hi, lo = split(bd)
        bd3.append(jnp.concatenate([hi, lo, hi], 0))
        rh, rl = jnp.concatenate([hi, hi, hi], 0), jnp.concatenate([lo, lo, lo], 0)
        rep.append(jnp.concatenate([rh, rl, rh], 1))

    row = lax.broadcasted_iota(i32, (192, 96), 0) // C
    col = lax.broadcasted_iota(i32, (192, 96), 1)
    part = col % 16
    order = jnp.where(part == 0, 0, jnp.where(part < 4, 1, jnp.where(part < 9, 2, 3)))
    mask = jnp.where(row == order, 0.1, 0.0).astype(f32)

    def moments(val, j):
        hi, lo = split(val)
        return nt(jnp.concatenate([hi, hi, lo], 1), rep[j]) * mask

    def sharp(m):
        hi, lo = split(m)
        return jnp.where(col < 64, hi.astype(f32), lo.astype(f32)).astype(bf16)

    sums, tees = [], []
    for j in range(NB // 2):
        lanes = slice(256 * j, 256 * j + 256)
        m = moments(s["vw"][192:384, lanes], j)
        s["sums"][j] = m
        t = nn(sharp(m), bd3[j])
        s["t"][:, lanes] = t
    sc = s["vw"][0:192, :] * s["t"][...]
    z3 = nn(w["lat"][...], stack3(jnp.concatenate([x, sc], 0)))
    g3 = sigmoid(z3)
    bb = z3 * g3
    s["d3"][...] = g3 + bb * (1.0 - g3)
    x2 = x + bb * fw
    z4 = nn(w["head"][...], stack3(x2))
    g4 = sigmoid(z4)
    hh = z4 * g4
    wen = jnp.concatenate([w["energy"][...]] * NB, 1)
    e = jnp.sum(wen * hh, 0, keepdims=True)
    dz4 = wen * fw * (g4 + hh * (1.0 - g4))
    dx2 = nn(w["head_t"][...], stack3(dz4))
    df = e + jnp.sum(dx2 * bb, 0, keepdims=True)
    dz3 = dx2 * fw * s["d3"][...]
    dc = nn(w["lat_t"][...], stack3(dz3))
    dxa = dx2 + dc[0:64]
    ds = dc[64:256]
    s["dv"][...] = ds * s["t"][...]
    s["dt"][...] = ds * s["vw"][0:192, :]
    for j in range(NB // 2):
        lanes = slice(256 * j, 256 * j + 256)
        dt = s["dt"][:, lanes]
        m = moments(dt, j)
        s["dw"][:, lanes] = nn(sharp(m), bd3[j])
        acc = None
        for left, right in ((s["sums"][j], dt), (m, s["vw"][192:384, lanes])):
            lt = jnp.transpose(jnp.concatenate([left, jnp.zeros((192, 32), f32)], 1))[0:32]
            lh, ll = split(lt)
            rh, rl = split(right)
            both = nn(jnp.concatenate([lh, ll], 0), rh)
            one = both[0:32] + both[32:64] + nn(lh, rl)
            acc = one if acc is None else acc + one
        s["dy"][2 * j] = acc[0:16, 0:128]
        s["dy"][2 * j + 1] = acc[16:32, 128:256]
    dx = dxa + nn(w["ve_t"][...], stack3(jnp.concatenate([s["dv"][...], s["dw"][...]], 0)))
    df = df + jnp.sum(dx * s["a"][...], 0, keepdims=True)
    for b in range(NB):
        s["sc"][3, b:b + 1, :] = df[:, 128 * b:128 * b + 128]
    dz2 = dx * fw * s["d2"][...]
    dz1 = nn(w["mix_t"][...], stack3(dz2)) * s["d1"][...]
    dr8 = nn(w["emb_t"][...], stack3(dz1))
    for b in range(NB):
        s["dr"][b] = dr8[0:8, 128 * b:128 * b + 128]

    dr = s["sc"][3] * fp
    for m in range(8):
        dr = dr + s["dr"][:, m, :] * slopes[m]
    gy = [s["dy"][:, n, :] for n in range(9)]
    dux = R3 * gy[1] + R15 * (uy * gy[4] + uz * gy[7] + ux * gy[8])
    duy = R3 * gy[2] + R15 * (ux * gy[4] + uz * gy[5] - uy * gy[8])
    duz = R3 * gy[3] + R15 * (uy * gy[5] + ux * gy[7]) + (3.0 * R5) * uz * gy[6]
    dot = dux * ux + duy * uy + duz * uz
    along = dr - dot * rinv
    scale = 50.0
    return [scale * (du * rinv + along * u) for du, u in ((dux, ux), (duy, uy), (duz, uz))]

PAIR_SCRATCH = {
    "feat": (8, 8, 128), "harm": (16, 8, 128), "sc": (4, 8, 128), "d1": (C, PAIRS), "d2": (C, PAIRS), "a": (C, PAIRS),
    "vw": (384, PAIRS), "sums": (4, 192, 96), "t": (192, PAIRS), "d3": (C, PAIRS), "dv": (192, PAIRS), "dt": (192, PAIRS),
    "dw": (192, PAIRS), "dy": (8, 16, 128), "dr": (8, 8, 128),
}
WEIGHT_NAMES = ("emb", "mix", "ve", "lat", "head", "head_t", "lat_t", "ve_t", "mix_t", "emb_t", "energy")


SIDE = 8
ATOMS = SIDE ** 3
ROWS = 25
STEP = 0.1
MASSES = (1.008, 15.999, 22.99, 35.453)
ZLANE = (0, 27, 54, 72, 99)
WIDTHS = (3, 2, 3)
EDGE = 2.0 * SIDE
TILE = (8, 128)
AXES = ("gx", "gy", "gz")
SIZES = (16, 8, 8)
FIRST_A, FIRST_B = 3, 4
SUM_ROWS, FAR_ROWS = 40, 16


def iota(dim, shape=TILE):
    return lax.broadcasted_iota(i32, shape, dim)


def lane_take(row, idx):
    return jnp.take_along_axis(row, idx, axis=1)


def roll_rows(v, shift):
    return v if shift % 8 == 0 else pltpu.roll(v, shift % 8, 0)


def roll_lanes(v, shift):
    return v if shift % 128 == 0 else pltpu.roll(v, shift % 128, 1)


def inverse_mass(kind):
    out = jnp.full(kind.shape, 1.0 / MASSES[3], f32)
    for k in range(3):
        out = jnp.where(kind == float(k), 1.0 / MASSES[k], out)
    return out


def parity():
    return [lax.axis_index(a) & 1 for a in AXES]


def place_in(side):
    p = parity()
    return (p[0] * 4 + p[1] * 2 + p[2]) ^ (7 if side else 0)


def pack4(rows, start):
    lane = iota(1)
    out = []
    for k in range(0, len(rows), 4):
        v = roll_lanes(rows[k], -start)
        for p in range(1, len(rows[k:k + 4])):
            v = jnp.where(lane >= 32 * p, roll_lanes(rows[k + p], 32 * p - start), v)
        out.append(v)
    return out


def start_kernel(pos_in, vel_in, frc_in, spec_in, cells_in, chunks, mid, cid, own, pos, vel, frc, spec, cells, raw, sems):
    copies = [pltpu.make_async_copy(a, b, sems.at[k]) for k, (a, b) in enumerate(
        ((pos_in, pos), (vel_in, vel), (frc_in, frc), (spec_in, spec), (cells_in, cells)))]
    for c in copies:
        c.start()
    px, py, pz = parity()
    raw[...] = jnp.zeros((128, 128), i32)
    for c in copies:
        c.wait()
    kind = spec[...].astype(f32)
    mass = inverse_mass(kind)
    kick = vel[...] + (0.5 * STEP) * frc[...] * mass
    own[0:3, :] = pos[...] + STEP * kick
    own[3:6, :] = kick
    own[6:7, :] = kind
    own[7:8, :] = jnp.zeros_like(kind)
    for x in range(3):
        for y in range(3):
            at = 8 * (3 * x + y)
            raw[at:at + 3, 0:27] = cells[x + px * (2 - 2 * x), y + py * (2 - 2 * y)]
    z0, z1, z2 = (raw[pl.ds(k, 16, stride=8), :] for k in range(3))
    lane = iota(1, (16, 128))
    flip = jnp.full((16, 128), pz, i32) == 1
    ids = jnp.where(lane < ZLANE[2], pltpu.roll(jnp.where(flip, z2, z0), ZLANE[1], 1),
                    jnp.where(lane < ZLANE[3], pltpu.roll(z1, ZLANE[2], 1), pltpu.roll(jnp.where(flip, z0, z2), ZLANE[3], 1)))
    cid[...] = jnp.where((lane >= ZLANE[1]) & (lane < ZLANE[4]), ids, 0)
    cuts = [own[:, 128 * h:128 * h + 128] for h in range(4)]
    rows = []
    for r in range(9):
        ids = jnp.broadcast_to(cid[r:r + 1, :], TILE)
        lo, hi = ids & 127, ids >> 7
        acc = lane_take(cuts[0], lo)
        for h in range(1, 4):
            acc = jnp.where(hi == h, lane_take(cuts[h], lo), acc)
        mid[r] = acc
        rows.append(acc)
    me = place_in(0)
    zs = ZLANE[3]
    for d, tiles in ((4, rows[6:9]), (2, rows[2::3]), (6, rows[8:9]), (1, pack4(rows, zs)), (5, pack4(rows[6:9], zs)),
                     (3, pack4(rows[2::3], zs)), (7, pack4(rows[8:9], zs))):
        for k, v in enumerate(tiles):
            chunks[me ^ d, k] = v


def widen(have, got, me, face):
    lane = iota(1)
    beyond = (lambda: lane >= ZLANE[4]) if face else (lambda: lane < ZLANE[1])
    at = ZLANE[face]
    xs = sorted({x for x, _ in have})
    rows = sorted(have)

    def strip(d, keys, base):
        out = {}
        for n, key in enumerate(keys):
            v = roll_lanes(got[me ^ d, n // 4], at - 32 * (n % 4))
            out[key] = jnp.where(beyond(), v, base[key])
        return out

    new = strip(1, rows, have)
    new.update(strip(5, [(face, y) for y in xs], {(face, y): got[me ^ 4, n] for n, y in enumerate(xs)}))
    new.update(strip(3, [(x, face) for x in xs], {(x, face): got[me ^ 2, n] for n, x in enumerate(xs)}))
    new.update(strip(7, [(face, face)], {(face, face): got[me ^ 6, 0]}))
    return new


def second_kernel(got, mid, table, chunks):
    have = {(r // 3 + 1, r % 3 + 1): mid[r] for r in range(9)}
    have = widen(have, got, place_in(0), 4)
    for (x, y), v in have.items():
        table[4 * (x - 1) + y - 1] = v
    me = place_in(1)
    zs = ZLANE[1]
    along_x = [have[1, y] for y in range(1, 5)]
    along_y = [have[x, 1] for x in range(1, 5)]
    whole = [have[x, y] for x in range(1, 5) for y in range(1, 5)]
    for d, tiles in ((4, along_x), (2, along_y), (6, along_x[:1]), (1, pack4(whole, zs)), (5, pack4(along_x, zs)),
                     (3, pack4(along_y, zs)), (7, pack4(along_x[:1], zs))):
        for k, v in enumerate(tiles):
            chunks[me ^ d, k] = v


def prepare_kernel(neigh, cen, cid, emb, mix, val, env, lat, head, energy,
                   nrow, nlane, live, crow, clane, irow, ilane, *out):
    sub, lane = iota(0), iota(1)
    big = iota(0, (128, 128))
    left, right = [], []
    for r in range(9):
        area = WIDTHS[r // 3] * WIDTHS[r % 3]
        ids = jnp.broadcast_to(cid[r:r + 1, :], TILE)
        valid = (lane >= 27) & (lane < 27 + 3 * area)
        valid = valid | ((lane >= 54) & (lane < 54 + 2 * area))
        valid = valid | ((lane >= 72) & (lane < 72 + 3 * area))
        row = (r // 3 + 1) * 5 + r % 3 + 1
        value = jnp.where((sub & 1) == 0, row, lane)
        left.append(jnp.where(valid & ((ids >> 7) == (sub >> 1)), value, 0).astype(f32).astype(bf16))
        lo = jnp.broadcast_to(cid[r:r + 1, :], (128, 128)) & 127
        right.append(jnp.where(big == lo, 1.0, 0.0).astype(bf16))
    inv = nt(jnp.concatenate(left, 1), jnp.concatenate(right, 1))
    inv = (inv + 0.5).astype(i32)
    for h in range(4):
        irow[h:h + 1, :] = inv[2 * h:2 * h + 1, :]
        ilane[h:h + 1, :] = inv[2 * h + 1:2 * h + 2, :]
    px, py, pz = parity()

    def flip(e, p):
        return e + p * (4 - 2 * e)

    def place(n):
        lo, hi = n & 127, n >> 7
        row = jnp.zeros(TILE, i32)
        col = jnp.zeros(TILE, i32)
        for h in range(4):
            row = jnp.where(hi == h, lane_take(jnp.broadcast_to(irow[h:h + 1, :], TILE), lo), row)
            col = jnp.where(hi == h, lane_take(jnp.broadcast_to(ilane[h:h + 1, :], TILE), lo), col)
        m = jnp.maximum(n - ATOMS, 0)
        grow = ((m.astype(f32) + 0.5) * (1.0 / 135.0)).astype(i32)
        rem = m - 135 * grow
        ex = ((grow.astype(f32) + 0.5) * 0.2).astype(i32)
        ey = grow - 5 * ex
        ez = ((rem.astype(f32) + 0.5) * (1.0 / 27.0)).astype(i32)
        slot = rem - 27 * ez
        ex, ey, ez = flip(ex, px), flip(ey, py), flip(ez, pz)
        first = jnp.where(ez == 0, 0, jnp.where(ez == 1, 27, jnp.where(ez == 2, 54, jnp.where(ez == 3, 72, 99))))
        return jnp.where(hi < 4, row, 5 * ex + ey), jnp.where(hi < 4, col, first + slot)

    n = neigh[...]
    c = jnp.concatenate([cen[...].astype(f32), jnp.zeros((1, 120), f32)], 1)
    c = jnp.sum(jnp.where(lane == sub, jnp.broadcast_to(c, TILE), 0.0), 1, keepdims=True)
    c = (jnp.broadcast_to(c, TILE) + 0.5).astype(i32)
    nrow[...], nlane[...] = place(n)
    crow[...], clane[...] = place(c)
    live[...] = jnp.where(n != c, 1.0, 0.0)

    def stack(w):
        hi = w.astype(bf16).astype(f32)
        return jnp.concatenate([hi, hi, w - hi], 1).astype(bf16)

    ve_t = jnp.concatenate([val[...], env[...]], 1)
    emb_t = jnp.concatenate([emb[0:8, :], jnp.zeros((8, C), f32)], 0)
    wide_energy = jnp.broadcast_to(energy[...], (128, C))
    tiles = (stack(emb[...].T), stack(mix[...]), stack(ve_t.T), stack(lat[...]), stack(head[...]), stack(head[...].T),
             stack(lat[...].T), stack(ve_t), stack(mix[...].T), stack(emb_t), wide_energy.T)
    for ref, v in zip(out, tiles):
        ref[...] = v


def pair_step(tab, nrow, nlane, live, crow, clane, w, s, force):
    sub, lane = iota(0), iota(1)
    px, py, pz = (1.0 - 2.0 * p.astype(f32) for p in parity())
    zshift = jnp.where(lane < ZLANE[1], -EDGE, jnp.where(lane >= ZLANE[4], EDGE, 0.0)) * pz
    zshift = jnp.where(sub == 2, zshift, 0.0)
    xshift = jnp.where(sub == 0, EDGE, 0.0) * px
    yshift = jnp.where(sub == 1, EDGE, 0.0) * py
    nr, nl, cr, cl = nrow[...], nlane[...], crow[...], clane[...]
    near = [jnp.zeros(TILE, f32) for _ in range(4)]
    centre = [jnp.zeros(TILE, f32) for _ in range(4)]
    for r in range(ROWS):
        ex, ey = r // 5, r % 5
        shift = zshift
        if ex in (0, 4):
            shift = shift + xshift * float(ex // 2 - 1)
        if ey in (0, 4):
            shift = shift + yshift * float(ey // 2 - 1)
        s["shifted"][r] = tab(ex, ey) + shift
        mine = nr == r
        centred = cr == r
        for k, q in enumerate((0, 1, 2, 6)):
            line = jnp.broadcast_to(s["shifted"][r, q:q + 1, :], TILE)
            near[k] = jnp.where(mine, lane_take(line, nl), near[k])
            if ex in (1, 2, 3) and ey in (1, 2, 3):
                centre[k] = jnp.where(centred, lane_take(line, cl), centre[k])
    alive = live[...]
    disp = [near[k] - centre[k] for k in range(3)]
    grads = pair_grads(disp, centre[3], near[3], alive, w, s)
    spare = 1.0 / jnp.sum(1.0 - alive, 1, keepdims=True)
    for k, g in enumerate(grads):
        g = jnp.where(alive > 0.0, -g, jnp.sum(g, 1, keepdims=True) * spare)
        hi = g.astype(bf16).astype(f32)
        s["spread"][k] = hi
        s["spread"][k + 3] = g - hi
    s["spread"][6] = jnp.zeros(TILE, f32)
    s["spread"][7] = jnp.zeros(TILE, f32)
    big = iota(0, (128, 128))
    left, right = [], []
    for b in range(NB):
        g = s["spread"][:, b, :]
        rows = jnp.broadcast_to(nrow[b:b + 1, :], TILE)
        left.append(jnp.concatenate([jnp.where(rows == r, g, 0.0) for r in range(ROWS)], 0).astype(bf16))
        right.append(jnp.where(big == jnp.broadcast_to(nlane[b:b + 1, :], (128, 128)), 1.0, 0.0).astype(bf16))
    out = nt(jnp.concatenate(left, 1), jnp.concatenate(right, 1))
    for r in range(ROWS):
        v = out[8 * r:8 * r + 8]
        force[r] = jnp.where(sub < 3, v + roll_rows(v, -3), 0.0)


def far_rows(side):
    far = 0 if side else 4
    rest = (1, 2, 3) if side else (0, 1, 2, 3)
    return [5 * far + y for y in rest], [5 * x + far for x in rest], [5 * x + y for x in rest for y in rest], [5 * far + far]


def put(chunks, d, values):
    for m, v in enumerate(values):
        chunks[d, 3 * m:3 * m + 3, :] = v[0:3]


def strips4(rows, at):
    return pack4(rows, at)


def strips2(rows, head, tail):
    lane = iota(1)
    out = []
    for k in range(0, len(rows), 2):
        v = None
        for n, q in enumerate(rows[k:k + 2]):
            t = jnp.where(lane < 64 * n + 27, roll_lanes(q, 64 * n - head), roll_lanes(q, 64 * n + 27 - tail))
            v = t if v is None else jnp.where(lane >= 64, t, v)
        out.append(v)
    return out


def sum_messages(force, chunks, side):
    me = place_in(side)
    near, far = (1, 0) if side else (3, 4)
    head, tail = (ZLANE[near], ZLANE[far]) if side else (ZLANE[far], ZLANE[near])
    f = [force[r] for r in range(ROWS)]
    xs = [f[5 * x + y] for x in (far, near) for y in range(5)]
    ys = [f[5 * x + y] for y in (far, near) for x in range(5)]
    corner = [f[5 * x + y] for x in (far, near) for y in (far, near)]
    for d, tiles in ((4, xs), (2, ys), (6, corner), (1, strips2(f, head, tail)), (5, strips2(xs, head, tail)),
                     (3, strips2(ys, head, tail)), (7, strips2(corner, head, tail))):
        put(chunks, me ^ d, tiles)


def add_messages(force, got, side):
    lane = iota(1, (3, 128))
    me = place_in(side)
    near, far = (1, 0) if side else (3, 4)
    inside = lane >= ZLANE[3] if side == 0 else lane < ZLANE[2]
    first = min(ZLANE[near], ZLANE[far])
    out = {r: force[r, 0:3, :] for r in range(ROWS)}
    xs = [5 * x + y for x in (near, far) for y in range(5)]
    ys = [5 * x + y for y in (near, far) for x in range(5)]
    corner = [5 * x + y for x in (near, far) for y in (near, far)]
    for d, rows in ((4, xs), (2, ys), (6, corner)):
        for m, r in enumerate(rows):
            out[r] = out[r] + got[me ^ d, 3 * m:3 * m + 3, :]
    for d, rows in ((1, list(range(ROWS))), (5, xs), (3, ys), (7, corner)):
        for n, r in enumerate(rows):
            v = got[me ^ d, 3 * (n // 2):3 * (n // 2) + 3, :]
            out[r] = out[r] + jnp.where(inside, roll_lanes(v, first - 64 * (n % 2)), 0.0)
    return out


def far_messages(force, chunks, side):
    me = place_in(side)
    at = ZLANE[0 if side else 4]
    xs, ys, whole, corner = ([force[r] for r in rows] for rows in far_rows(side))
    for d, tiles in ((4, xs), (2, ys), (6, corner), (1, strips4(whole, at)), (5, strips4(xs, at)), (3, strips4(ys, at)),
                     (7, strips4(corner, at))):
        put(chunks, me ^ d, tiles)


def add_far(force, got, side):
    lane = iota(1, (3, 128))
    me = place_in(side)
    near, far = (1, 0) if side else (3, 4)
    at = ZLANE[near]
    inside = (lane >= at) & (lane < at + 27)
    xs, ys, whole, corner = far_rows(side)
    out = {r: force[r, 0:3, :] for r in whole}
    xs = [r + 5 * (near - far) for r in xs]
    ys = [r + near - far for r in ys]
    corner = [5 * near + near]
    for d, rows in ((4, xs), (2, ys), (6, corner)):
        for m, r in enumerate(rows):
            out[r] = out[r] + got[me ^ d, 3 * m:3 * m + 3, :]
    for d, rows in ((1, whole), (5, xs), (3, ys), (7, corner)):
        for n, r in enumerate(rows):
            v = got[me ^ d, 3 * (n // 4):3 * (n // 4) + 3, :]
            out[r] = out[r] + jnp.where(inside, roll_lanes(v, at - 32 * (n % 4)), 0.0)
    return out


def weight_refs(refs):
    return dict(zip(WEIGHT_NAMES, refs))


def first_pairs(part, got, nrow, nlane, live, crow, clane, *refs):
    w = weight_refs(refs[:11])
    tab, force, chunks = refs[11:14]
    s = dict(zip(ALL_SCRATCH, refs[14:]))
    have = {(x, y): part[4 * (x - 1) + y - 1] for x in range(1, 5) for y in range(1, 5)}
    for (x, y), v in widen(have, got, place_in(1), 0).items():
        tab[5 * x + y] = v
    pair_step(lambda x, y: tab[5 * x + y], nrow, nlane, live, crow, clane, w, s, force)
    sum_messages(force, chunks, 0)


def next_pairs(force, got, table, nrow, nlane, live, crow, clane, *refs):
    w = weight_refs(refs[:11])
    total, force2, chunks = refs[11:14]
    s = dict(zip(ALL_SCRATCH, refs[14:]))
    for r, f in add_messages(force, got, 1).items():
        if r // 5 in (1, 2, 3) and r % 5 in (1, 2, 3):
            total[(r // 5 - 1) * 3 + r % 5 - 1, 0:3, :] = f
        mass = inverse_mass(jnp.broadcast_to(table[r, 6:7, :], (3, 128)))
        half = (0.5 * STEP) * f * mass
        kick = table[r, 3:6, :] + half + half
        s["table"][r, 0:3, :] = table[r, 0:3, :] + STEP * kick
        s["table"][r, 3:8, :] = table[r, 3:8, :]
    pair_step(lambda x, y: s["table"][5 * x + y], nrow, nlane, live, crow, clane, w, s, force2)
    far_messages(force2, chunks, 0)


def sum_kernel(force, got, out, chunks):
    for r, v in add_messages(force, got, 0).items():
        out[r, 0:3, :] = v
    sum_messages(out, chunks, 1)


def far_kernel(force, got, out, chunks):
    for r, v in add_far(force, got, 0).items():
        out[r, 0:3, :] = v
    far_messages(out, chunks, 1)


def end_kernel(force, got, total, irow, ilane, own, new_pos, new_vel, new_frc, both):
    summed = add_far(force, got, 1)
    middle = [5 * x + y for x in (1, 2, 3) for y in (1, 2, 3)]
    for k, r in enumerate(middle):
        both[k, 0:3, :] = summed[r]
        both[k, 3:6, :] = total[k, 0:3, :]
        both[k, 6:8, :] = jnp.zeros((2, 128), f32)
    mass = inverse_mass(own[6:7, :])
    for h in range(4):
        lanes = slice(128 * h, 128 * h + 128)
        ir = jnp.broadcast_to(irow[h:h + 1, :], TILE)
        il = jnp.broadcast_to(ilane[h:h + 1, :], TILE)
        acc = jnp.zeros(TILE, f32)
        for k, r in enumerate(middle):
            acc = jnp.where(ir == r, lane_take(both[k], il), acc)
        last, first = acc[0:3], acc[3:6]
        m = mass[:, lanes]
        half = (0.5 * STEP) * first * m
        kick = own[3:6, lanes] + half + half
        new_pos[:, lanes] = own[0:3, lanes] + STEP * kick
        new_vel[:, lanes] = kick + (0.5 * STEP) * last * m
        new_frc[:, lanes] = last


ALL_SCRATCH = dict(PAIR_SCRATCH, shifted=(ROWS, 8, 128), table=(ROWS, 8, 128), spread=(8, 8, 128))


def shape(*dims, kind=f32):
    return jax.ShapeDtypeStruct(dims, kind)


def call(kernel, outs, *args, scratch=(), limit=4 << 20, flops=1 << 20, space=pltpu.VMEM):
    vm = pl.BlockSpec(memory_space=pltpu.VMEM)
    return pl.pallas_call(
        kernel,
        out_shape=tuple(outs),
        in_specs=[pl.BlockSpec(memory_space=space)] * len(args),
        out_specs=tuple([vm] * len(outs)),
        scratch_shapes=list(scratch),
        compiler_params=pltpu.CompilerParams(vmem_limit_bytes=limit),
        cost_estimate=pl.CostEstimate(flops=flops, bytes_accessed=1 << 18, transcendentals=0),
    )(*args)


def groups(side):
    out = []
    for x in range(side, SIZES[0] + side, 2):
        for y in range(side, SIZES[1] + side, 2):
            for z in range(side, SIZES[2] + side, 2):
                out.append([(((x + a) % SIZES[0]) * SIZES[1] + (y + b) % SIZES[1]) * SIZES[2] + (z + c) % SIZES[2]
                            for a in range(2) for b in range(2) for c in range(2)])
    return out


def trade(chunks, side):
    return lax.all_to_all(chunks, AXES, 0, 0, axis_index_groups=groups(side), tiled=True)


def local(positions, velocities, forces, species, cell_ids, centers, neighbours,
          w_embed, w_mix, w_value, w_env, w_latent, w_head, w_energy):
    table_shape = shape(ROWS, 8, 128)
    sums, fars = shape(8, SUM_ROWS, 128), shape(8, FAR_ROWS, 128)
    int_tile, flat = shape(8, 128, kind=i32), shape(4, 128, kind=i32)
    scratch = [pltpu.VMEM(v, f32) for v in ALL_SCRATCH.values()]

    chunks, mid, cid, own = call(
        start_kernel, [shape(8, FIRST_A, 8, 128), shape(9, 8, 128), shape(16, 128, kind=i32), shape(8, ATOMS)],
        positions, velocities, forces, species.reshape(1, ATOMS), cell_ids, space=pl.ANY,
        scratch=[pltpu.VMEM((3, ATOMS), f32)] * 3 + [pltpu.VMEM((1, ATOMS), i32), pltpu.VMEM((3, 3, 3, 27), i32),
                                                     pltpu.VMEM((128, 128), i32), pltpu.SemaphoreType.DMA((5,))])
    got = trade(chunks, 0)
    weight_shapes = [shape(m, k, kind=bf16) for m, k in (
        (C, 48), (C, 192), (384, 192), (C, 768), (C, 192), (C, 192), (256, 192), (C, 1152), (C, 192), (16, 192))]
    prepared = call(
        prepare_kernel, [int_tile, int_tile, shape(8, 128), int_tile, int_tile, flat, flat] + weight_shapes + [shape(C, 128)],
        neighbours, centers.reshape(1, NB), cid, w_embed.T, w_mix, w_value[0].T, w_env[0].T, w_latent[0], w_head, w_energy.reshape(1, C))
    idx, (irow, ilane), weights = prepared[:5], prepared[5:7], prepared[7:]
    part, chunks = call(second_kernel, [shape(16, 8, 128), shape(8, FIRST_B, 8, 128)], got, mid)
    got = trade(chunks, 1)
    table, force, chunks = call(
        first_pairs, [table_shape, table_shape, sums], part, got, *idx, *weights, scratch=scratch, limit=24 << 20, flops=1 << 30)
    force, chunks = call(sum_kernel, [table_shape, sums], force, trade(chunks, 0))
    total, force, chunks = call(
        next_pairs, [shape(9, 8, 128), table_shape, fars], force, trade(chunks, 1), table, *idx, *weights, scratch=scratch,
        limit=24 << 20, flops=1 << 30)
    force, chunks = call(far_kernel, [table_shape, fars], force, trade(chunks, 0))
    return call(end_kernel, [shape(3, ATOMS)] * 3, force, trade(chunks, 1), total, irow, ilane, own,
                scratch=[pltpu.VMEM((9, 8, 128), f32)])


def solution(mesh):
    from jax.sharding import PartitionSpec as P

    rows = P(None, AXES)
    in_specs = (rows, rows, rows, P(AXES), P(*AXES, None), P(AXES), P(AXES, None)) + (P(),) * 7
    return jax.shard_map(local, mesh=mesh, in_specs=in_specs, out_specs=(rows, rows, rows), check_vma=False)
```

```python
import math
import jax, jax.numpy as jnp
from jax import lax
from jax.experimental import pallas as pl
from jax.experimental.pallas import tpu as pltpu

f32, bf16, i32 = jnp.float32, jnp.bfloat16, jnp.int32
NB, BLK, C = 8, 128, 64
PAIRS = NB * BLK
PARTS = NB // 2
WIDE = 2 * BLK
R3, R5, R15 = math.sqrt(3.0), math.sqrt(5.0), math.sqrt(15.0)


def nt(a, b):
    return lax.dot_general(a, b, (((1,), (1,)), ((), ())), preferred_element_type=f32)


def nn(a, b):
    return jnp.dot(a, b, preferred_element_type=f32)


def split(x):
    hi = x.astype(bf16)
    return hi, (x - hi.astype(f32)).astype(bf16)


def stack3(x):
    hi, lo = split(x)
    return jnp.concatenate([hi, lo, hi], 0)


def sigmoid(z):
    return 0.5 * jnp.tanh(0.5 * z) + 0.5


def harmonic_rows(ux, uy, uz):
    return [jnp.ones_like(ux), R3 * ux, R3 * uy, R3 * uz, R15 * ux * uy, R15 * uy * uz,
            0.5 * R5 * (3.0 * uz * uz - 1.0), R15 * ux * uz, 0.5 * R15 * (ux * ux - uy * uy)]


def pair_grads(disp, kc, kn, live, w, s):
    dx, dy, dz = disp
    r = jnp.sqrt(dx * dx + dy * dy + dz * dz + 0.09)
    rinv = 1.0 / r
    ux, uy, uz = dx * rinv, dy * rinv, dz * rinv
    q = jnp.minimum(r * (1.0 / 6.0), 1.0)
    q2 = q * q
    q4 = q2 * q2
    q5 = q4 * q
    q6 = q4 * q2
    f = (1.0 - 28.0 * q6 + 48.0 * (q6 * q) - 21.0 * (q6 * q2)) * live
    fp = -28.0 * q5 * (1.0 - q) * (1.0 - q) * live
    theta = math.pi * q
    s1, c1 = jnp.sin(theta), jnp.cos(theta)
    sm, cm = s1, c1
    norm = math.sqrt(1.0 / 3.0)
    rn = norm * rinv
    slopes = []
    for m in range(8):
        s["feat"][m] = sm * rn
        slopes.append((cm * (math.pi / 6.0 * (m + 1)) - sm * rinv) * rn)
        sm, cm = sm * c1 + cm * s1, cm * c1 - sm * s1
    ys = harmonic_rows(ux, uy, uz)
    for n in range(9):
        s["harm"][n] = ys[n]
    for n in range(9, 16):
        s["harm"][n] = jnp.zeros((8, 128), f32)
    s["sc"][0] = f
    s["sc"][1] = kc
    s["sc"][2] = kn

    parts = range(PARTS)
    sub8 = lax.broadcasted_iota(i32, (8, BLK), 0).astype(f32)

    def features(b):
        hot = jnp.where(sub8 < 4.0, jnp.broadcast_to(s["sc"][1, b:b + 1, :], (8, BLK)),
                        jnp.broadcast_to(s["sc"][2, b:b + 1, :], (8, BLK)) + 4.0) == sub8
        return jnp.concatenate([s["feat"][:, b, :], hot.astype(f32)], 0)

    def envelope(j):
        return jnp.concatenate([s["sc"][0, b:b + 1, :] for b in (2 * j, 2 * j + 1)], 1)

    fw = [envelope(j) for j in parts]
    d1, d2, d3, a, x, sums, t = ([None] * PARTS for _ in range(7))
    h = [None] * PARTS
    for j in parts:
        feat = jnp.concatenate([features(2 * j), features(2 * j + 1)], 1)
        z = nn(w["emb"][...], stack3(feat))
        g = sigmoid(z)
        h[j] = z * g
        d1[j] = g + h[j] * (1.0 - g)
    for j in parts:
        z = nn(w["mix"][...], stack3(h[j]))
        g = sigmoid(z)
        a[j] = z * g
        d2[j] = g + a[j] * (1.0 - g)
        x[j] = a[j] * fw[j]
    for j in parts:
        s["vw"][j] = nn(w["ve"][...], stack3(x[j]))

    zero = jnp.zeros((16, BLK), f32)
    bd3, rep = [], []
    for j in parts:
        y0, y1 = s["harm"][:, 2 * j, :], s["harm"][:, 2 * j + 1, :]
        bd = jnp.concatenate([jnp.concatenate([y0, zero], 1), jnp.concatenate([zero, y1], 1)], 0)
        hi, lo = split(bd)
        bd3.append(jnp.concatenate([hi, lo, hi], 0))
        rh, rl = jnp.concatenate([hi, hi, hi], 0), jnp.concatenate([lo, lo, lo], 0)
        rep.append(jnp.concatenate([rh, rl, rh], 1))

    row = lax.broadcasted_iota(i32, (192, 96), 0) // C
    col = lax.broadcasted_iota(i32, (192, 96), 1)
    part = col % 16
    order = jnp.where(part == 0, 0, jnp.where(part < 4, 1, jnp.where(part < 9, 2, 3)))
    mask = jnp.where(row == order, 0.1, 0.0).astype(f32)

    def moments(val, j):
        hi, lo = split(val)
        return nt(jnp.concatenate([hi, hi, lo], 1), rep[j]) * mask

    def sharp(m):
        hi, lo = split(m)
        return jnp.where(col < 64, hi.astype(f32), lo.astype(f32)).astype(bf16)

    for j in parts:
        sums[j] = moments(s["vw"][j, 192:384, :], j)
    for j in parts:
        s["t"][j] = nn(sharp(sums[j]), bd3[j])
    bb, x2 = [None] * PARTS, [None] * PARTS
    for j in parts:
        sc = s["vw"][j, 0:192, :] * s["t"][j]
        z = nn(w["lat"][...], stack3(jnp.concatenate([x[j], sc], 0)))
        g = sigmoid(z)
        bb[j] = z * g
        d3[j] = g + bb[j] * (1.0 - g)
        x2[j] = x[j] + bb[j] * fw[j]
    wen = jnp.concatenate([w["energy"][...]] * 2, 1)
    df, dx2, dxa = ([None] * PARTS for _ in range(3))
    dz = [None] * PARTS
    for j in parts:
        z = nn(w["head"][...], stack3(x2[j]))
        g = sigmoid(z)
        hh = z * g
        df[j] = jnp.sum(wen * hh, 0, keepdims=True)
        dz[j] = wen * fw[j] * (g + hh * (1.0 - g))
    for j in parts:
        dx2[j] = nn(w["head_t"][...], stack3(dz[j]))
        df[j] = df[j] + jnp.sum(dx2[j] * bb[j], 0, keepdims=True)
        dz[j] = dx2[j] * fw[j] * d3[j]
    for j in parts:
        dc = nn(w["lat_t"][...], stack3(dz[j]))
        dxa[j] = dx2[j] + dc[0:64]
        ds = dc[64:256]
        s["dv"][j] = ds * s["t"][j]
        s["dt"][j] = ds * s["vw"][j, 0:192, :]
    m = [None] * PARTS
    for j in parts:
        m[j] = moments(s["dt"][j], j)
    for j in parts:
        s["dw"][j] = nn(sharp(m[j]), bd3[j])
    for j in parts:
        acc = None
        for left, right in ((sums[j], s["dt"][j]), (m[j], s["vw"][j, 192:384, :])):
            lt = jnp.transpose(jnp.concatenate([left, jnp.zeros((192, 32), f32)], 1))[0:32]
            lh, ll = split(lt)
            rh, rl = split(right)
            both = nn(jnp.concatenate([lh, ll], 0), rh)
            one = both[0:32] + both[32:64] + nn(lh, rl)
            acc = one if acc is None else acc + one
        s["dy"][2 * j] = acc[0:16, 0:128]
        s["dy"][2 * j + 1] = acc[16:32, 128:256]
    for j in parts:
        dx = dxa[j] + nn(w["ve_t"][...], stack3(jnp.concatenate([s["dv"][j], s["dw"][j]], 0)))
        df[j] = df[j] + jnp.sum(dx * a[j], 0, keepdims=True)
        dz[j] = dx * fw[j] * d2[j]
        for k in range(2):
            s["sc"][3, 2 * j + k:2 * j + k + 1, :] = df[j][:, 128 * k:128 * k + 128]
    for j in parts:
        dz[j] = nn(w["mix_t"][...], stack3(dz[j])) * d1[j]
    for j in parts:
        dr8 = nn(w["emb_t"][...], stack3(dz[j]))
        for k in range(2):
            s["dr"][2 * j + k] = dr8[0:8, 128 * k:128 * k + 128]

    dr = s["sc"][3] * fp
    for k in range(8):
        dr = dr + s["dr"][:, k, :] * slopes[k]
    gy = [s["dy"][:, n, :] for n in range(9)]
    dux = R3 * gy[1] + R15 * (uy * gy[4] + uz * gy[7] + ux * gy[8])
    duy = R3 * gy[2] + R15 * (ux * gy[4] + uz * gy[5] - uy * gy[8])
    duz = R3 * gy[3] + R15 * (uy * gy[5] + ux * gy[7]) + (3.0 * R5) * uz * gy[6]
    dot = dux * ux + duy * uy + duz * uz
    along = dr - dot * rinv
    scale = 50.0
    return [scale * (du * rinv + along * u) for du, u in ((dux, ux), (duy, uy), (duz, uz))]


PAIR_SCRATCH = {
    "feat": (8, 8, 128), "harm": (16, 8, 128), "sc": (4, 8, 128), "vw": (PARTS, 384, WIDE), "t": (PARTS, 192, WIDE),
    "dv": (PARTS, 192, WIDE), "dt": (PARTS, 192, WIDE), "dw": (PARTS, 192, WIDE), "dy": (8, 16, 128), "dr": (8, 8, 128),
}
WEIGHT_NAMES = ("emb", "mix", "ve", "lat", "head", "head_t", "lat_t", "ve_t", "mix_t", "emb_t", "energy")


SIDE = 8
ATOMS = SIDE ** 3
ROWS = 25
STEP = 0.1
MASSES = (1.008, 15.999, 22.99, 35.453)
ZLANE = (0, 27, 54, 72, 99)
WIDTHS = (3, 2, 3)
EDGE = 2.0 * SIDE
TILE = (8, 128)
AXES = ("gx", "gy", "gz")
SIZES = (16, 8, 8)
FIRST_A, FIRST_B = 3, 4
SUM_ROWS, FAR_ROWS = 40, 16


def iota(dim, shape=TILE):
    return lax.broadcasted_iota(i32, shape, dim)


def lane_take(row, idx):
    return jnp.take_along_axis(row, idx, axis=1)


def roll_rows(v, shift):
    return v if shift % 8 == 0 else pltpu.roll(v, shift % 8, 0)


def roll_lanes(v, shift):
    return v if shift % 128 == 0 else pltpu.roll(v, shift % 128, 1)


def inverse_mass(kind):
    out = jnp.full(kind.shape, 1.0 / MASSES[3], f32)
    for k in range(3):
        out = jnp.where(kind == float(k), 1.0 / MASSES[k], out)
    return out


def parity():
    return [lax.axis_index(a) & 1 for a in AXES]


def place_in(side):
    p = parity()
    return (p[0] * 4 + p[1] * 2 + p[2]) ^ (7 if side else 0)


def pack4(rows, start):
    lane = iota(1)
    out = []
    for k in range(0, len(rows), 4):
        v = roll_lanes(rows[k], -start)
        for p in range(1, len(rows[k:k + 4])):
            v = jnp.where(lane >= 32 * p, roll_lanes(rows[k + p], 32 * p - start), v)
        out.append(v)
    return out


def start_kernel(pos_in, vel_in, frc_in, spec_in, cells_in, chunks, mid, cid, own, pos, vel, frc, spec, cells, raw, sems):
    copies = [pltpu.make_async_copy(a, b, sems.at[k]) for k, (a, b) in enumerate(
        ((pos_in, pos), (vel_in, vel), (frc_in, frc), (spec_in, spec), (cells_in, cells)))]
    for c in copies:
        c.start()
    px, py, pz = parity()
    raw[...] = jnp.zeros((128, 128), i32)
    for c in copies:
        c.wait()
    kind = spec[...].astype(f32)
    mass = inverse_mass(kind)
    kick = vel[...] + (0.5 * STEP) * frc[...] * mass
    own[0:3, :] = pos[...] + STEP * kick
    own[3:6, :] = kick
    own[6:7, :] = kind
    own[7:8, :] = jnp.zeros_like(kind)
    for x in range(3):
        for y in range(3):
            at = 8 * (3 * x + y)
            raw[at:at + 3, 0:27] = cells[x + px * (2 - 2 * x), y + py * (2 - 2 * y)]
    z0, z1, z2 = (raw[pl.ds(k, 16, stride=8), :] for k in range(3))
    lane = iota(1, (16, 128))
    flip = jnp.full((16, 128), pz, i32) == 1
    ids = jnp.where(lane < ZLANE[2], pltpu.roll(jnp.where(flip, z2, z0), ZLANE[1], 1),
                    jnp.where(lane < ZLANE[3], pltpu.roll(z1, ZLANE[2], 1), pltpu.roll(jnp.where(flip, z0, z2), ZLANE[3], 1)))
    cid[...] = jnp.where((lane >= ZLANE[1]) & (lane < ZLANE[4]), ids, 0)
    cuts = [own[:, 128 * h:128 * h + 128] for h in range(4)]
    rows = []
    for r in range(9):
        ids = jnp.broadcast_to(cid[r:r + 1, :], TILE)
        lo, hi = ids & 127, ids >> 7
        acc = lane_take(cuts[0], lo)
        for h in range(1, 4):
            acc = jnp.where(hi == h, lane_take(cuts[h], lo), acc)
        mid[r] = acc
        rows.append(acc)
    me = place_in(0)
    zs = ZLANE[3]
    for d, tiles in ((4, rows[6:9]), (2, rows[2::3]), (6, rows[8:9]), (1, pack4(rows, zs)), (5, pack4(rows[6:9], zs)),
                     (3, pack4(rows[2::3], zs)), (7, pack4(rows[8:9], zs))):
        for k, v in enumerate(tiles):
            chunks[me ^ d, k] = v


def widen(have, got, me, face):
    lane = iota(1)
    beyond = (lambda: lane >= ZLANE[4]) if face else (lambda: lane < ZLANE[1])
    at = ZLANE[face]
    xs = sorted({x for x, _ in have})
    rows = sorted(have)

    def strip(d, keys, base):
        out = {}
        for n, key in enumerate(keys):
            v = roll_lanes(got[me ^ d, n // 4], at - 32 * (n % 4))
            out[key] = jnp.where(beyond(), v, base[key])
        return out

    new = strip(1, rows, have)
    new.update(strip(5, [(face, y) for y in xs], {(face, y): got[me ^ 4, n] for n, y in enumerate(xs)}))
    new.update(strip(3, [(x, face) for x in xs], {(x, face): got[me ^ 2, n] for n, x in enumerate(xs)}))
    new.update(strip(7, [(face, face)], {(face, face): got[me ^ 6, 0]}))
    return new


def widened(got, mid, table, chunks):
    have = {(r // 3 + 1, r % 3 + 1): mid[r] for r in range(9)}
    have = widen(have, got, place_in(0), 4)
    for (x, y), v in have.items():
        table[4 * (x - 1) + y - 1] = v
    me = place_in(1)
    zs = ZLANE[1]
    along_x = [have[1, y] for y in range(1, 5)]
    along_y = [have[x, 1] for x in range(1, 5)]
    whole = [have[x, y] for x in range(1, 5) for y in range(1, 5)]
    for d, tiles in ((4, along_x), (2, along_y), (6, along_x[:1]), (1, pack4(whole, zs)), (5, pack4(along_x, zs)),
                     (3, pack4(along_y, zs)), (7, pack4(along_x[:1], zs))):
        for k, v in enumerate(tiles):
            chunks[me ^ d, k] = v


def second_kernel(got, mid, neigh, cen, cid, emb, mix, val, env, lat, head, energy,
                  table, chunks, nrow, nlane, live, crow, clane, irow, ilane, *out):
    widened(got, mid, table, chunks)
    sub, lane = iota(0), iota(1)
    big = iota(0, (128, 128))
    left, right = [], []
    for r in range(9):
        area = WIDTHS[r // 3] * WIDTHS[r % 3]
        ids = jnp.broadcast_to(cid[r:r + 1, :], TILE)
        valid = (lane >= 27) & (lane < 27 + 3 * area)
        valid = valid | ((lane >= 54) & (lane < 54 + 2 * area))
        valid = valid | ((lane >= 72) & (lane < 72 + 3 * area))
        row = (r // 3 + 1) * 5 + r % 3 + 1
        value = jnp.where((sub & 1) == 0, row, lane)
        left.append(jnp.where(valid & ((ids >> 7) == (sub >> 1)), value, 0).astype(f32).astype(bf16))
        lo = jnp.broadcast_to(cid[r:r + 1, :], (128, 128)) & 127
        right.append(jnp.where(big == lo, 1.0, 0.0).astype(bf16))
    inv = nt(jnp.concatenate(left, 1), jnp.concatenate(right, 1))
    inv = (inv + 0.5).astype(i32)
    for h in range(4):
        irow[h:h + 1, :] = inv[2 * h:2 * h + 1, :]
        ilane[h:h + 1, :] = inv[2 * h + 1:2 * h + 2, :]
    px, py, pz = parity()

    def flip(e, p):
        return e + p * (4 - 2 * e)

    def place(n):
        lo, hi = n & 127, n >> 7
        row = jnp.zeros(TILE, i32)
        col = jnp.zeros(TILE, i32)
        for h in range(4):
            row = jnp.where(hi == h, lane_take(jnp.broadcast_to(irow[h:h + 1, :], TILE), lo), row)
            col = jnp.where(hi == h, lane_take(jnp.broadcast_to(ilane[h:h + 1, :], TILE), lo), col)
        m = jnp.maximum(n - ATOMS, 0)
        grow = ((m.astype(f32) + 0.5) * (1.0 / 135.0)).astype(i32)
        rem = m - 135 * grow
        ex = ((grow.astype(f32) + 0.5) * 0.2).astype(i32)
        ey = grow - 5 * ex
        ez = ((rem.astype(f32) + 0.5) * (1.0 / 27.0)).astype(i32)
        slot = rem - 27 * ez
        ex, ey, ez = flip(ex, px), flip(ey, py), flip(ez, pz)
        first = jnp.where(ez == 0, 0, jnp.where(ez == 1, 27, jnp.where(ez == 2, 54, jnp.where(ez == 3, 72, 99))))
        return jnp.where(hi < 4, row, 5 * ex + ey), jnp.where(hi < 4, col, first + slot)

    n = neigh[...]
    c = jnp.concatenate([cen[...].astype(f32), jnp.zeros((1, 120), f32)], 1)
    c = jnp.sum(jnp.where(lane == sub, jnp.broadcast_to(c, TILE), 0.0), 1, keepdims=True)
    c = (jnp.broadcast_to(c, TILE) + 0.5).astype(i32)
    nrow[...], nlane[...] = place(n)
    crow[...], clane[...] = place(c)
    live[...] = jnp.where(n != c, 1.0, 0.0)

    def stack(w):
        hi = w.astype(bf16).astype(f32)
        return jnp.concatenate([hi, hi, w - hi], 1).astype(bf16)

    ve_t = jnp.concatenate([val[...], env[...]], 1)
    emb_t = jnp.concatenate([emb[0:8, :], jnp.zeros((8, C), f32)], 0)
    wide_energy = jnp.broadcast_to(energy[...], (128, C))
    tiles = (stack(emb[...].T), stack(mix[...]), stack(ve_t.T), stack(lat[...]), stack(head[...]), stack(head[...].T),
             stack(lat[...].T), stack(ve_t), stack(mix[...].T), stack(emb_t), wide_energy.T)
    for ref, v in zip(out, tiles):
        ref[...] = v


def pair_step(tab, nrow, nlane, live, crow, clane, w, s, force):
    sub, lane = iota(0), iota(1)
    px, py, pz = (1.0 - 2.0 * p.astype(f32) for p in parity())
    zshift = jnp.where(lane < ZLANE[1], -EDGE, jnp.where(lane >= ZLANE[4], EDGE, 0.0)) * pz
    zshift = jnp.where(sub == 2, zshift, 0.0)
    xshift = jnp.where(sub == 0, EDGE, 0.0) * px
    yshift = jnp.where(sub == 1, EDGE, 0.0) * py
    nr, nl, cr, cl = nrow[...], nlane[...], crow[...], clane[...]
    near = [jnp.zeros(TILE, f32) for _ in range(4)]
    centre = [jnp.zeros(TILE, f32) for _ in range(4)]
    for r in range(ROWS):
        ex, ey = r // 5, r % 5
        shift = zshift
        if ex in (0, 4):
            shift = shift + xshift * float(ex // 2 - 1)
        if ey in (0, 4):
            shift = shift + yshift * float(ey // 2 - 1)
        s["shifted"][r] = tab(ex, ey) + shift
        mine = nr == r
        centred = cr == r
        for k, q in enumerate((0, 1, 2, 6)):
            line = jnp.broadcast_to(s["shifted"][r, q:q + 1, :], TILE)
            near[k] = jnp.where(mine, lane_take(line, nl), near[k])
            if ex in (1, 2, 3) and ey in (1, 2, 3):
                centre[k] = jnp.where(centred, lane_take(line, cl), centre[k])
    alive = live[...]
    disp = [near[k] - centre[k] for k in range(3)]
    grads = pair_grads(disp, centre[3], near[3], alive, w, s)
    spare = 1.0 / jnp.sum(1.0 - alive, 1, keepdims=True)
    for k, g in enumerate(grads):
        g = jnp.where(alive > 0.0, -g, jnp.sum(g, 1, keepdims=True) * spare)
        hi = g.astype(bf16).astype(f32)
        s["spread"][k] = hi
        s["spread"][k + 3] = g - hi
    s["spread"][6] = jnp.zeros(TILE, f32)
    s["spread"][7] = jnp.zeros(TILE, f32)
    big = iota(0, (128, 128))
    left, right = [], []
    for b in range(NB):
        g = s["spread"][:, b, :]
        rows = jnp.broadcast_to(nrow[b:b + 1, :], TILE)
        left.append(jnp.concatenate([jnp.where(rows == r, g, 0.0) for r in range(ROWS)], 0).astype(bf16))
        right.append(jnp.where(big == jnp.broadcast_to(nlane[b:b + 1, :], (128, 128)), 1.0, 0.0).astype(bf16))
    out = nt(jnp.concatenate(left, 1), jnp.concatenate(right, 1))
    for r in range(ROWS):
        v = out[8 * r:8 * r + 8]
        force[r] = jnp.where(sub < 3, v + roll_rows(v, -3), 0.0)


def far_rows(side):
    far = 0 if side else 4
    rest = (1, 2, 3) if side else (0, 1, 2, 3)
    return [5 * far + y for y in rest], [5 * x + far for x in rest], [5 * x + y for x in rest for y in rest], [5 * far + far]


def put(chunks, d, values):
    for m, v in enumerate(values):
        chunks[d, 3 * m:3 * m + 3, :] = v[0:3]


def strips4(rows, at):
    return pack4(rows, at)


def strips2(rows, head, tail):
    lane = iota(1)
    out = []
    for k in range(0, len(rows), 2):
        v = None
        for n, q in enumerate(rows[k:k + 2]):
            t = jnp.where(lane < 64 * n + 27, roll_lanes(q, 64 * n - head), roll_lanes(q, 64 * n + 27 - tail))
            v = t if v is None else jnp.where(lane >= 64, t, v)
        out.append(v)
    return out


def sum_messages(force, chunks, side):
    me = place_in(side)
    near, far = (1, 0) if side else (3, 4)
    head, tail = (ZLANE[near], ZLANE[far]) if side else (ZLANE[far], ZLANE[near])
    f = [force[r] for r in range(ROWS)]
    xs = [f[5 * x + y] for x in (far, near) for y in range(5)]
    ys = [f[5 * x + y] for y in (far, near) for x in range(5)]
    corner = [f[5 * x + y] for x in (far, near) for y in (far, near)]
    for d, tiles in ((4, xs), (2, ys), (6, corner), (1, strips2(f, head, tail)), (5, strips2(xs, head, tail)),
                     (3, strips2(ys, head, tail)), (7, strips2(corner, head, tail))):
        put(chunks, me ^ d, tiles)


def add_messages(force, got, side):
    lane = iota(1, (3, 128))
    me = place_in(side)
    near, far = (1, 0) if side else (3, 4)
    inside = lane >= ZLANE[3] if side == 0 else lane < ZLANE[2]
    first = min(ZLANE[near], ZLANE[far])
    out = {r: force[r, 0:3, :] for r in range(ROWS)}
    xs = [5 * x + y for x in (near, far) for y in range(5)]
    ys = [5 * x + y for y in (near, far) for x in range(5)]
    corner = [5 * x + y for x in (near, far) for y in (near, far)]
    for d, rows in ((4, xs), (2, ys), (6, corner)):
        for m, r in enumerate(rows):
            out[r] = out[r] + got[me ^ d, 3 * m:3 * m + 3, :]
    for d, rows in ((1, list(range(ROWS))), (5, xs), (3, ys), (7, corner)):
        for n, r in enumerate(rows):
            v = got[me ^ d, 3 * (n // 2):3 * (n // 2) + 3, :]
            out[r] = out[r] + jnp.where(inside, roll_lanes(v, first - 64 * (n % 2)), 0.0)
    return out


def far_messages(force, chunks, side):
    me = place_in(side)
    at = ZLANE[0 if side else 4]
    xs, ys, whole, corner = ([force[r] for r in rows] for rows in far_rows(side))
    for d, tiles in ((4, xs), (2, ys), (6, corner), (1, strips4(whole, at)), (5, strips4(xs, at)), (3, strips4(ys, at)),
                     (7, strips4(corner, at))):
        put(chunks, me ^ d, tiles)


def add_far(force, got, side):
    lane = iota(1, (3, 128))
    me = place_in(side)
    near, far = (1, 0) if side else (3, 4)
    at = ZLANE[near]
    inside = (lane >= at) & (lane < at + 27)
    xs, ys, whole, corner = far_rows(side)
    out = {r: force[r, 0:3, :] for r in whole}
    xs = [r + 5 * (near - far) for r in xs]
    ys = [r + near - far for r in ys]
    corner = [5 * near + near]
    for d, rows in ((4, xs), (2, ys), (6, corner)):
        for m, r in enumerate(rows):
            out[r] = out[r] + got[me ^ d, 3 * m:3 * m + 3, :]
    for d, rows in ((1, whole), (5, xs), (3, ys), (7, corner)):
        for n, r in enumerate(rows):
            v = got[me ^ d, 3 * (n // 4):3 * (n // 4) + 3, :]
            out[r] = out[r] + jnp.where(inside, roll_lanes(v, at - 32 * (n % 4)), 0.0)
    return out


def weight_refs(refs):
    return dict(zip(WEIGHT_NAMES, refs))


def first_pairs(part, got, nrow, nlane, live, crow, clane, *refs):
    w = weight_refs(refs[:11])
    tab, force, chunks = refs[11:14]
    s = dict(zip(ALL_SCRATCH, refs[14:]))
    have = {(x, y): part[4 * (x - 1) + y - 1] for x in range(1, 5) for y in range(1, 5)}
    for (x, y), v in widen(have, got, place_in(1), 0).items():
        tab[5 * x + y] = v
    pair_step(lambda x, y: tab[5 * x + y], nrow, nlane, live, crow, clane, w, s, force)
    sum_messages(force, chunks, 0)


def next_pairs(force, got, table, nrow, nlane, live, crow, clane, *refs):
    w = weight_refs(refs[:11])
    total, force2, chunks = refs[11:14]
    s = dict(zip(ALL_SCRATCH, refs[14:]))
    for r, f in add_messages(force, got, 1).items():
        if r // 5 in (1, 2, 3) and r % 5 in (1, 2, 3):
            total[(r // 5 - 1) * 3 + r % 5 - 1, 0:3, :] = f
        mass = inverse_mass(jnp.broadcast_to(table[r, 6:7, :], (3, 128)))
        half = (0.5 * STEP) * f * mass
        kick = table[r, 3:6, :] + half + half
        s["table"][r, 0:3, :] = table[r, 0:3, :] + STEP * kick
        s["table"][r, 3:8, :] = table[r, 3:8, :]
    pair_step(lambda x, y: s["table"][5 * x + y], nrow, nlane, live, crow, clane, w, s, force2)
    far_messages(force2, chunks, 0)


def sum_kernel(force, got, out, chunks):
    for r, v in add_messages(force, got, 0).items():
        out[r, 0:3, :] = v
    sum_messages(out, chunks, 1)


def far_kernel(force, got, out, chunks):
    for r, v in add_far(force, got, 0).items():
        out[r, 0:3, :] = v
    far_messages(out, chunks, 1)


def end_kernel(force, got, total, irow, ilane, own, new_pos, new_vel, new_frc, both):
    summed = add_far(force, got, 1)
    middle = [5 * x + y for x in (1, 2, 3) for y in (1, 2, 3)]
    for k, r in enumerate(middle):
        both[k, 0:3, :] = summed[r]
        both[k, 3:6, :] = total[k, 0:3, :]
        both[k, 6:8, :] = jnp.zeros((2, 128), f32)
    mass = inverse_mass(own[6:7, :])
    for h in range(4):
        lanes = slice(128 * h, 128 * h + 128)
        ir = jnp.broadcast_to(irow[h:h + 1, :], TILE)
        il = jnp.broadcast_to(ilane[h:h + 1, :], TILE)
        acc = jnp.zeros(TILE, f32)
        for k, r in enumerate(middle):
            acc = jnp.where(ir == r, lane_take(both[k], il), acc)
        last, first = acc[0:3], acc[3:6]
        m = mass[:, lanes]
        half = (0.5 * STEP) * first * m
        kick = own[3:6, lanes] + half + half
        new_pos[:, lanes] = own[0:3, lanes] + STEP * kick
        new_vel[:, lanes] = kick + (0.5 * STEP) * last * m
        new_frc[:, lanes] = last


ALL_SCRATCH = dict(PAIR_SCRATCH, shifted=(ROWS, 8, 128), table=(ROWS, 8, 128), spread=(8, 8, 128))


def shape(*dims, kind=f32):
    return jax.ShapeDtypeStruct(dims, kind)


def call(kernel, outs, *args, scratch=(), limit=4 << 20, flops=1 << 20, space=pltpu.VMEM):
    vm = pl.BlockSpec(memory_space=pltpu.VMEM)
    return pl.pallas_call(
        kernel,
        out_shape=tuple(outs),
        in_specs=[pl.BlockSpec(memory_space=space)] * len(args),
        out_specs=tuple([vm] * len(outs)),
        scratch_shapes=list(scratch),
        compiler_params=pltpu.CompilerParams(vmem_limit_bytes=limit),
        cost_estimate=pl.CostEstimate(flops=flops, bytes_accessed=1 << 18, transcendentals=0),
    )(*args)


def groups(side):
    out = []
    for x in range(side, SIZES[0] + side, 2):
        for y in range(side, SIZES[1] + side, 2):
            for z in range(side, SIZES[2] + side, 2):
                out.append([(((x + a) % SIZES[0]) * SIZES[1] + (y + b) % SIZES[1]) * SIZES[2] + (z + c) % SIZES[2]
                            for a in range(2) for b in range(2) for c in range(2)])
    return out


def trade(chunks, side):
    return lax.all_to_all(chunks, AXES, 0, 0, axis_index_groups=groups(side), tiled=True)


def local(positions, velocities, forces, species, cell_ids, centers, neighbours,
          w_embed, w_mix, w_value, w_env, w_latent, w_head, w_energy):
    table_shape = shape(ROWS, 8, 128)
    sums, fars = shape(8, SUM_ROWS, 128), shape(8, FAR_ROWS, 128)
    int_tile, flat = shape(8, 128, kind=i32), shape(4, 128, kind=i32)
    scratch = [pltpu.VMEM(v, f32) for v in ALL_SCRATCH.values()]

    chunks, mid, cid, own = call(
        start_kernel, [shape(8, FIRST_A, 8, 128), shape(9, 8, 128), shape(16, 128, kind=i32), shape(8, ATOMS)],
        positions, velocities, forces, species.reshape(1, ATOMS), cell_ids, space=pl.ANY, limit=56 << 20,
        scratch=[pltpu.VMEM((3, ATOMS), f32)] * 3 + [pltpu.VMEM((1, ATOMS), i32), pltpu.VMEM((3, 3, 3, 27), i32),
                                                     pltpu.VMEM((128, 128), i32), pltpu.SemaphoreType.DMA((5,))])
    got = trade(chunks, 0)
    weight_shapes = [shape(m, k, kind=bf16) for m, k in (
        (C, 48), (C, 192), (384, 192), (C, 768), (C, 192), (C, 192), (256, 192), (C, 1152), (C, 192), (16, 192))]
    part, chunks, *prepared = call(
        second_kernel, [shape(16, 8, 128), shape(8, FIRST_B, 8, 128), int_tile, int_tile, shape(8, 128), int_tile, int_tile, flat, flat]
        + weight_shapes + [shape(C, 128)], got, mid, neighbours, centers.reshape(1, NB), cid, w_embed.T, w_mix, w_value[0].T, w_env[0].T,
        w_latent[0], w_head, w_energy.reshape(1, C))
    idx, (irow, ilane), weights = prepared[:5], prepared[5:7], prepared[7:]
    got = trade(chunks, 1)
    table, force, chunks = call(
        first_pairs, [table_shape, table_shape, sums], part, got, *idx, *weights, scratch=scratch, limit=24 << 20, flops=1 << 30)
    force, chunks = call(sum_kernel, [table_shape, sums], force, trade(chunks, 0))
    total, force, chunks = call(
        next_pairs, [shape(9, 8, 128), table_shape, fars], force, trade(chunks, 1), table, *idx, *weights, scratch=scratch,
        limit=24 << 20, flops=1 << 30)
    force, chunks = call(far_kernel, [table_shape, fars], force, trade(chunks, 0))
    return call(end_kernel, [shape(3, ATOMS)] * 3, force, trade(chunks, 1), total, irow, ilane, own,
                scratch=[pltpu.VMEM((9, 8, 128), f32)])


def solution(mesh):
    from jax.sharding import PartitionSpec as P

    rows = P(None, AXES)
    in_specs = (rows, rows, rows, P(AXES), P(*AXES, None), P(AXES), P(AXES, None)) + (P(),) * 7
    return jax.shard_map(local, mesh=mesh, in_specs=in_specs, out_specs=(rows, rows, rows), check_vma=False)
```

```python
import math
import jax, jax.numpy as jnp
from jax import lax
from jax.experimental import pallas as pl
from jax.experimental.pallas import tpu as pltpu

f32, bf16, i32 = jnp.float32, jnp.bfloat16, jnp.int32
NB, BLK, C = 8, 128, 64
PAIRS = NB * BLK
PARTS = NB // 2
WIDE = 2 * BLK
R3, R5, R15 = math.sqrt(3.0), math.sqrt(5.0), math.sqrt(15.0)


def nt(a, b):
    return lax.dot_general(a, b, (((1,), (1,)), ((), ())), preferred_element_type=f32)


def nn(a, b):
    return jnp.dot(a, b, preferred_element_type=f32)


def split(x):
    hi = x.astype(bf16)
    return hi, (x - hi.astype(f32)).astype(bf16)


def stack3(x):
    hi, lo = split(x)
    return jnp.concatenate([hi, lo, hi], 0)


def sigmoid(z):
    return 0.5 * jnp.tanh(0.5 * z) + 0.5


def harmonic_rows(ux, uy, uz):
    return [jnp.ones_like(ux), R3 * ux, R3 * uy, R3 * uz, R15 * ux * uy, R15 * uy * uz,
            0.5 * R5 * (3.0 * uz * uz - 1.0), R15 * ux * uz, 0.5 * R15 * (ux * ux - uy * uy)]


def pair_grads(disp, kc, kn, live, w, s):
    dx, dy, dz = disp
    r = jnp.sqrt(dx * dx + dy * dy + dz * dz + 0.09)
    rinv = 1.0 / r
    ux, uy, uz = dx * rinv, dy * rinv, dz * rinv
    q = jnp.minimum(r * (1.0 / 6.0), 1.0)
    q2 = q * q
    q4 = q2 * q2
    q5 = q4 * q
    q6 = q4 * q2
    f = (1.0 - 28.0 * q6 + 48.0 * (q6 * q) - 21.0 * (q6 * q2)) * live
    fp = -28.0 * q5 * (1.0 - q) * (1.0 - q) * live
    theta = math.pi * q
    s1, c1 = jnp.sin(theta), jnp.cos(theta)
    sm, cm = s1, c1
    norm = math.sqrt(1.0 / 3.0)
    rn = norm * rinv
    slopes = []
    for m in range(8):
        s["feat"][m] = sm * rn
        slopes.append((cm * (math.pi / 6.0 * (m + 1)) - sm * rinv) * rn)
        sm, cm = sm * c1 + cm * s1, cm * c1 - sm * s1
    ys = harmonic_rows(ux, uy, uz)
    for n in range(9):
        s["harm"][n] = ys[n]
    for n in range(9, 16):
        s["harm"][n] = jnp.zeros((8, 128), f32)
    s["sc"][0] = f
    s["sc"][1] = kc
    s["sc"][2] = kn

    parts = range(PARTS)
    sub8 = lax.broadcasted_iota(i32, (8, BLK), 0).astype(f32)

    def features(b):
        hot = jnp.where(sub8 < 4.0, jnp.broadcast_to(s["sc"][1, b:b + 1, :], (8, BLK)),
                        jnp.broadcast_to(s["sc"][2, b:b + 1, :], (8, BLK)) + 4.0) == sub8
        return jnp.concatenate([s["feat"][:, b, :], hot.astype(f32)], 0)

    def envelope(j):
        return jnp.concatenate([s["sc"][0, b:b + 1, :] for b in (2 * j, 2 * j + 1)], 1)

    fw = [envelope(j) for j in parts]
    d1, d2, d3, a, x, sums, t = ([None] * PARTS for _ in range(7))
    h = [None] * PARTS
    for j in parts:
        feat = jnp.concatenate([features(2 * j), features(2 * j + 1)], 1)
        z = nn(w["emb"][...], stack3(feat))
        g = sigmoid(z)
        h[j] = z * g
        d1[j] = g + h[j] * (1.0 - g)
    for j in parts:
        z = nn(w["mix"][...], stack3(h[j]))
        g = sigmoid(z)
        a[j] = z * g
        d2[j] = g + a[j] * (1.0 - g)
        x[j] = a[j] * fw[j]
    for j in parts:
        s["vw"][j] = nn(w["ve"][...], stack3(x[j]))

    zero = jnp.zeros((16, BLK), f32)
    bd3, rep = [], []
    for j in parts:
        y0, y1 = s["harm"][:, 2 * j, :], s["harm"][:, 2 * j + 1, :]
        bd = jnp.concatenate([jnp.concatenate([y0, zero], 1), jnp.concatenate([zero, y1], 1)], 0)
        hi, lo = split(bd)
        none = jnp.zeros((32, WIDE), bf16)
        bd3.append(jnp.concatenate([hi, lo, hi, none], 0))
        rep.append(jnp.concatenate([hi, hi, hi, none, lo, lo, lo, none], 0))

    row = lax.broadcasted_iota(i32, (192, 128), 0) // C
    col = lax.broadcasted_iota(i32, (192, 128), 1)
    part = col % 16
    order = jnp.where(part == 0, 0, jnp.where(part < 4, 1, jnp.where(part < 9, 2, 3)))
    mask = jnp.where(row == order, 0.1, 0.0).astype(f32)

    def moments(val, j):
        out = nt(jnp.concatenate(split(val), 0), rep[j])
        return (out[0:192, 0:128] + out[192:384, 0:128] + out[0:192, 128:256]) * mask

    def sharp(m):
        hi, lo = split(m)
        return jnp.where(col < 64, hi.astype(f32), lo.astype(f32)).astype(bf16)

    for j in parts:
        sums[j] = moments(s["vw"][j, 192:384, :], j)
    for j in parts:
        s["t"][j] = nn(sharp(sums[j]), bd3[j])
    bb, x2 = [None] * PARTS, [None] * PARTS
    for j in parts:
        sc = s["vw"][j, 0:192, :] * s["t"][j]
        z = nn(w["lat"][...], stack3(jnp.concatenate([x[j], sc], 0)))
        g = sigmoid(z)
        bb[j] = z * g
        d3[j] = g + bb[j] * (1.0 - g)
        x2[j] = x[j] + bb[j] * fw[j]
    wen = jnp.concatenate([w["energy"][...]] * 2, 1)
    df, dx2, dxa = ([None] * PARTS for _ in range(3))
    dz = [None] * PARTS
    for j in parts:
        z = nn(w["head"][...], stack3(x2[j]))
        g = sigmoid(z)
        hh = z * g
        df[j] = jnp.sum(wen * hh, 0, keepdims=True)
        dz[j] = wen * fw[j] * (g + hh * (1.0 - g))
    for j in parts:
        dx2[j] = nn(w["head_t"][...], stack3(dz[j]))
        df[j] = df[j] + jnp.sum(dx2[j] * bb[j], 0, keepdims=True)
        dz[j] = dx2[j] * fw[j] * d3[j]
    for j in parts:
        dc = nn(w["lat_t"][...], stack3(dz[j]))
        dxa[j] = dx2[j] + dc[0:64]
        ds = dc[64:256]
        s["dv"][j] = ds * s["t"][j]
        s["dt"][j] = ds * s["vw"][j, 0:192, :]
    m = [None] * PARTS
    for j in parts:
        m[j] = moments(s["dt"][j], j)
    for j in parts:
        s["dw"][j] = nn(sharp(m[j]), bd3[j])
    for j in parts:
        acc = None
        for left, right in ((sums[j], s["dt"][j]), (m[j], s["vw"][j, 192:384, :])):
            lt = jnp.transpose(left)[0:32]
            lh, ll = split(lt)
            rh, rl = split(right)
            both = nn(jnp.concatenate([lh, ll], 0), rh)
            one = both[0:32] + both[32:64] + nn(lh, rl)
            acc = one if acc is None else acc + one
        s["dy"][2 * j] = acc[0:16, 0:128]
        s["dy"][2 * j + 1] = acc[16:32, 128:256]
    for j in parts:
        dx = dxa[j] + nn(w["ve_t"][...], stack3(jnp.concatenate([s["dv"][j], s["dw"][j]], 0)))
        df[j] = df[j] + jnp.sum(dx * a[j], 0, keepdims=True)
        dz[j] = dx * fw[j] * d2[j]
        for k in range(2):
            s["sc"][3, 2 * j + k:2 * j + k + 1, :] = df[j][:, 128 * k:128 * k + 128]
    for j in parts:
        dz[j] = nn(w["mix_t"][...], stack3(dz[j])) * d1[j]
    for j in parts:
        dr8 = nn(w["emb_t"][...], stack3(dz[j]))
        for k in range(2):
            s["dr"][2 * j + k] = dr8[0:8, 128 * k:128 * k + 128]

    dr = s["sc"][3] * fp
    for k in range(8):
        dr = dr + s["dr"][:, k, :] * slopes[k]
    gy = [s["dy"][:, n, :] for n in range(9)]
    dux = R3 * gy[1] + R15 * (uy * gy[4] + uz * gy[7] + ux * gy[8])
    duy = R3 * gy[2] + R15 * (ux * gy[4] + uz * gy[5] - uy * gy[8])
    duz = R3 * gy[3] + R15 * (uy * gy[5] + ux * gy[7]) + (3.0 * R5) * uz * gy[6]
    dot = dux * ux + duy * uy + duz * uz
    along = dr - dot * rinv
    scale = 50.0
    return [scale * (du * rinv + along * u) for du, u in ((dux, ux), (duy, uy), (duz, uz))]


PAIR_SCRATCH = {
    "feat": (8, 8, 128), "harm": (16, 8, 128), "sc": (4, 8, 128), "vw": (PARTS, 384, WIDE), "t": (PARTS, 192, WIDE),
    "dv": (PARTS, 192, WIDE), "dt": (PARTS, 192, WIDE), "dw": (PARTS, 192, WIDE), "dy": (8, 16, 128), "dr": (8, 8, 128),
}
WEIGHT_NAMES = ("emb", "mix", "ve", "lat", "head", "head_t", "lat_t", "ve_t", "mix_t", "emb_t", "energy")
SIDE = 8
ATOMS = SIDE ** 3
ROWS = 25
STEP = 0.1
MASSES = (1.008, 15.999, 22.99, 35.453)
ZLANE = (0, 27, 54, 72, 99)
WIDTHS = (3, 2, 3)
EDGE = 2.0 * SIDE
TILE = (8, 128)
AXES = ("gx", "gy", "gz")
SIZES = (16, 8, 8)
FIRST_A, FIRST_B = 3, 4
SUM_ROWS, FAR_ROWS = 40, 16


def iota(dim, shape=TILE):
    return lax.broadcasted_iota(i32, shape, dim)


def lane_take(row, idx):
    return jnp.take_along_axis(row, idx, axis=1)


def roll_rows(v, shift):
    return v if shift % 8 == 0 else pltpu.roll(v, shift % 8, 0)


def roll_lanes(v, shift):
    return v if shift % 128 == 0 else pltpu.roll(v, shift % 128, 1)


def inverse_mass(kind):
    out = jnp.full(kind.shape, 1.0 / MASSES[3], f32)
    for k in range(3):
        out = jnp.where(kind == float(k), 1.0 / MASSES[k], out)
    return out


def parity():
    return [lax.axis_index(a) & 1 for a in AXES]


def place_in(side):
    p = parity()
    return (p[0] * 4 + p[1] * 2 + p[2]) ^ (7 if side else 0)


def pack4(rows, start):
    lane = iota(1)
    out = []
    for k in range(0, len(rows), 4):
        v = roll_lanes(rows[k], -start)
        for p in range(1, len(rows[k:k + 4])):
            v = jnp.where(lane >= 32 * p, roll_lanes(rows[k + p], 32 * p - start), v)
        out.append(v)
    return out


def start_kernel(given, cells, chunks, mid, cid, own, raw):
    px, py, pz = parity()
    raw[...] = jnp.zeros((128, 128), i32)
    kind = given[9:10, :]
    mass = inverse_mass(kind)
    kick = given[3:6, :] + (0.5 * STEP) * given[6:9, :] * mass
    own[0:3, :] = given[0:3, :] + STEP * kick
    own[3:6, :] = kick
    own[6:7, :] = kind
    own[7:8, :] = jnp.zeros_like(kind)
    for x in range(3):
        for y in range(3):
            at = 8 * (3 * x + y)
            raw[at:at + 3, 0:27] = cells[x + px * (2 - 2 * x), y + py * (2 - 2 * y)]
    z0, z1, z2 = (raw[pl.ds(k, 16, stride=8), :] for k in range(3))
    lane = iota(1, (16, 128))
    flip = jnp.full((16, 128), pz, i32) == 1
    ids = jnp.where(lane < ZLANE[2], pltpu.roll(jnp.where(flip, z2, z0), ZLANE[1], 1),
                    jnp.where(lane < ZLANE[3], pltpu.roll(z1, ZLANE[2], 1), pltpu.roll(jnp.where(flip, z0, z2), ZLANE[3], 1)))
    cid[...] = jnp.where((lane >= ZLANE[1]) & (lane < ZLANE[4]), ids, 0)
    cuts = [own[:, 128 * h:128 * h + 128] for h in range(4)]
    rows = []
    for r in range(9):
        ids = jnp.broadcast_to(cid[r:r + 1, :], TILE)
        lo, hi = ids & 127, ids >> 7
        acc = lane_take(cuts[0], lo)
        for h in range(1, 4):
            acc = jnp.where(hi == h, lane_take(cuts[h], lo), acc)
        mid[r] = acc
        rows.append(acc)
    me = place_in(0)
    zs = ZLANE[3]
    for d, tiles in ((4, rows[6:9]), (2, rows[2::3]), (6, rows[8:9]), (1, pack4(rows, zs)), (5, pack4(rows[6:9], zs)),
                     (3, pack4(rows[2::3], zs)), (7, pack4(rows[8:9], zs))):
        for k, v in enumerate(tiles):
            chunks[me ^ d, k] = v


def widen(have, got, me, face):
    lane = iota(1)
    beyond = (lambda: lane >= ZLANE[4]) if face else (lambda: lane < ZLANE[1])
    at = ZLANE[face]
    xs = sorted({x for x, _ in have})
    rows = sorted(have)

    def strip(d, keys, base):
        out = {}
        for n, key in enumerate(keys):
            v = roll_lanes(got[me ^ d, n // 4], at - 32 * (n % 4))
            out[key] = jnp.where(beyond(), v, base[key])
        return out

    new = strip(1, rows, have)
    new.update(strip(5, [(face, y) for y in xs], {(face, y): got[me ^ 4, n] for n, y in enumerate(xs)}))
    new.update(strip(3, [(x, face) for x in xs], {(x, face): got[me ^ 2, n] for n, x in enumerate(xs)}))
    new.update(strip(7, [(face, face)], {(face, face): got[me ^ 6, 0]}))
    return new


def widened(got, mid, table, chunks):
    have = {(r // 3 + 1, r % 3 + 1): mid[r] for r in range(9)}
    have = widen(have, got, place_in(0), 4)
    for (x, y), v in have.items():
        table[4 * (x - 1) + y - 1] = v
    me = place_in(1)
    zs = ZLANE[1]
    along_x = [have[1, y] for y in range(1, 5)]
    along_y = [have[x, 1] for x in range(1, 5)]
    whole = [have[x, y] for x in range(1, 5) for y in range(1, 5)]
    for d, tiles in ((4, along_x), (2, along_y), (6, along_x[:1]), (1, pack4(whole, zs)), (5, pack4(along_x, zs)),
                     (3, pack4(along_y, zs)), (7, pack4(along_x[:1], zs))):
        for k, v in enumerate(tiles):
            chunks[me ^ d, k] = v


def second_kernel(got, mid, neigh, cen, cid, emb, mix, val, env, lat, head, energy,
                  table, chunks, nrow, nlane, live, crow, clane, irow, ilane, *out):
    widened(got, mid, table, chunks)
    sub, lane = iota(0), iota(1)
    big = iota(0, (128, 128))
    left, right = [], []
    for r in range(9):
        area = WIDTHS[r // 3] * WIDTHS[r % 3]
        ids = jnp.broadcast_to(cid[r:r + 1, :], TILE)
        valid = (lane >= 27) & (lane < 27 + 3 * area)
        valid = valid | ((lane >= 54) & (lane < 54 + 2 * area))
        valid = valid | ((lane >= 72) & (lane < 72 + 3 * area))
        row = (r // 3 + 1) * 5 + r % 3 + 1
        value = jnp.where((sub & 1) == 0, row, lane)
        left.append(jnp.where(valid & ((ids >> 7) == (sub >> 1)), value, 0).astype(f32).astype(bf16))
        lo = jnp.broadcast_to(cid[r:r + 1, :], (128, 128)) & 127
        right.append(jnp.where(big == lo, 1.0, 0.0).astype(bf16))
    inv = nt(jnp.concatenate(left, 1), jnp.concatenate(right, 1))
    inv = (inv + 0.5).astype(i32)
    for h in range(4):
        irow[h:h + 1, :] = inv[2 * h:2 * h + 1, :]
        ilane[h:h + 1, :] = inv[2 * h + 1:2 * h + 2, :]
    px, py, pz = parity()

    def flip(e, p):
        return e + p * (4 - 2 * e)

    def place(n):
        lo, hi = n & 127, n >> 7
        row = jnp.zeros(TILE, i32)
        col = jnp.zeros(TILE, i32)
        for h in range(4):
            row = jnp.where(hi == h, lane_take(jnp.broadcast_to(irow[h:h + 1, :], TILE), lo), row)
            col = jnp.where(hi == h, lane_take(jnp.broadcast_to(ilane[h:h + 1, :], TILE), lo), col)
        m = jnp.maximum(n - ATOMS, 0)
        grow = ((m.astype(f32) + 0.5) * (1.0 / 135.0)).astype(i32)
        rem = m - 135 * grow
        ex = ((grow.astype(f32) + 0.5) * 0.2).astype(i32)
        ey = grow - 5 * ex
        ez = ((rem.astype(f32) + 0.5) * (1.0 / 27.0)).astype(i32)
        slot = rem - 27 * ez
        ex, ey, ez = flip(ex, px), flip(ey, py), flip(ez, pz)
        first = jnp.where(ez == 0, 0, jnp.where(ez == 1, 27, jnp.where(ez == 2, 54, jnp.where(ez == 3, 72, 99))))
        return jnp.where(hi < 4, row, 5 * ex + ey), jnp.where(hi < 4, col, first + slot)

    n = neigh[...]
    c = jnp.concatenate([cen[...].astype(f32), jnp.zeros((1, 120), f32)], 1)
    c = jnp.sum(jnp.where(lane == sub, jnp.broadcast_to(c, TILE), 0.0), 1, keepdims=True)
    c = (jnp.broadcast_to(c, TILE) + 0.5).astype(i32)
    nrow[...], nlane[...] = place(n)
    crow[...], clane[...] = place(c)
    live[...] = jnp.where(n != c, 1.0, 0.0)

    def stack(w):
        hi = w.astype(bf16).astype(f32)
        return jnp.concatenate([hi, hi, w - hi], 1).astype(bf16)

    ve_t = jnp.concatenate([val[...], env[...]], 1)
    emb_t = jnp.concatenate([emb[0:8, :], jnp.zeros((8, C), f32)], 0)
    wide_energy = jnp.broadcast_to(energy[...], (128, C))
    tiles = (stack(emb[...].T), stack(mix[...]), stack(ve_t.T), stack(lat[...]), stack(head[...]), stack(head[...].T),
             stack(lat[...].T), stack(ve_t), stack(mix[...].T), stack(emb_t), wide_energy.T)
    for ref, v in zip(out, tiles):
        ref[...] = v


def pair_step(tab, nrow, nlane, live, crow, clane, w, s, force):
    sub, lane = iota(0), iota(1)
    px, py, pz = (1.0 - 2.0 * p.astype(f32) for p in parity())
    zshift = jnp.where(lane < ZLANE[1], -EDGE, jnp.where(lane >= ZLANE[4], EDGE, 0.0)) * pz
    zshift = jnp.where(sub == 2, zshift, 0.0)
    xshift = jnp.where(sub == 0, EDGE, 0.0) * px
    yshift = jnp.where(sub == 1, EDGE, 0.0) * py
    nr, nl, cr, cl = nrow[...], nlane[...], crow[...], clane[...]
    near = [jnp.zeros(TILE, f32) for _ in range(4)]
    centre = [jnp.zeros(TILE, f32) for _ in range(4)]
    for r in range(ROWS):
        ex, ey = r // 5, r % 5
        shift = zshift
        if ex in (0, 4):
            shift = shift + xshift * float(ex // 2 - 1)
        if ey in (0, 4):
            shift = shift + yshift * float(ey // 2 - 1)
        s["shifted"][r] = tab(ex, ey) + shift
        mine = nr == r
        centred = cr == r
        for k, q in enumerate((0, 1, 2, 6)):
            line = jnp.broadcast_to(s["shifted"][r, q:q + 1, :], TILE)
            near[k] = jnp.where(mine, lane_take(line, nl), near[k])
            if ex in (1, 2, 3) and ey in (1, 2, 3):
                centre[k] = jnp.where(centred, lane_take(line, cl), centre[k])
    alive = live[...]
    disp = [near[k] - centre[k] for k in range(3)]
    grads = pair_grads(disp, centre[3], near[3], alive, w, s)
    spare = 1.0 / jnp.sum(1.0 - alive, 1, keepdims=True)
    for k, g in enumerate(grads):
        g = jnp.where(alive > 0.0, -g, jnp.sum(g, 1, keepdims=True) * spare)
        hi = g.astype(bf16).astype(f32)
        s["spread"][k] = hi
        s["spread"][k + 3] = g - hi
    s["spread"][6] = jnp.zeros(TILE, f32)
    s["spread"][7] = jnp.zeros(TILE, f32)
    big = iota(0, (128, 128))
    left, right = [], []
    for b in range(NB):
        g = s["spread"][:, b, :]
        rows = jnp.broadcast_to(nrow[b:b + 1, :], TILE)
        left.append(jnp.concatenate([jnp.where(rows == r, g, 0.0) for r in range(ROWS)], 0).astype(bf16))
        right.append(jnp.where(big == jnp.broadcast_to(nlane[b:b + 1, :], (128, 128)), 1.0, 0.0).astype(bf16))
    out = nt(jnp.concatenate(left, 1), jnp.concatenate(right, 1))
    for r in range(ROWS):
        v = out[8 * r:8 * r + 8]
        force[r] = jnp.where(sub < 3, v + roll_rows(v, -3), 0.0)


def far_rows(side):
    far = 0 if side else 4
    rest = (1, 2, 3) if side else (0, 1, 2, 3)
    return [5 * far + y for y in rest], [5 * x + far for x in rest], [5 * x + y for x in rest for y in rest], [5 * far + far]


def put(chunks, d, values):
    for m, v in enumerate(values):
        chunks[d, 3 * m:3 * m + 3, :] = v[0:3]


def strips4(rows, at):
    return pack4(rows, at)


def strips2(rows, head, tail):
    lane = iota(1)
    out = []
    for k in range(0, len(rows), 2):
        v = None
        for n, q in enumerate(rows[k:k + 2]):
            t = jnp.where(lane < 64 * n + 27, roll_lanes(q, 64 * n - head), roll_lanes(q, 64 * n + 27 - tail))
            v = t if v is None else jnp.where(lane >= 64, t, v)
        out.append(v)
    return out


def sum_messages(force, chunks, side):
    me = place_in(side)
    near, far = (1, 0) if side else (3, 4)
    head, tail = (ZLANE[near], ZLANE[far]) if side else (ZLANE[far], ZLANE[near])
    f = [force[r] for r in range(ROWS)]
    xs = [f[5 * x + y] for x in (far, near) for y in range(5)]
    ys = [f[5 * x + y] for y in (far, near) for x in range(5)]
    corner = [f[5 * x + y] for x in (far, near) for y in (far, near)]
    for d, tiles in ((4, xs), (2, ys), (6, corner), (1, strips2(f, head, tail)), (5, strips2(xs, head, tail)),
                     (3, strips2(ys, head, tail)), (7, strips2(corner, head, tail))):
        put(chunks, me ^ d, tiles)


def add_messages(force, got, side):
    lane = iota(1, (3, 128))
    me = place_in(side)
    near, far = (1, 0) if side else (3, 4)
    inside = lane >= ZLANE[3] if side == 0 else lane < ZLANE[2]
    first = min(ZLANE[near], ZLANE[far])
    out = {r: force[r, 0:3, :] for r in range(ROWS)}
    xs = [5 * x + y for x in (near, far) for y in range(5)]
    ys = [5 * x + y for y in (near, far) for x in range(5)]
    corner = [5 * x + y for x in (near, far) for y in (near, far)]
    for d, rows in ((4, xs), (2, ys), (6, corner)):
        for m, r in enumerate(rows):
            out[r] = out[r] + got[me ^ d, 3 * m:3 * m + 3, :]
    for d, rows in ((1, list(range(ROWS))), (5, xs), (3, ys), (7, corner)):
        for n, r in enumerate(rows):
            v = got[me ^ d, 3 * (n // 2):3 * (n // 2) + 3, :]
            out[r] = out[r] + jnp.where(inside, roll_lanes(v, first - 64 * (n % 2)), 0.0)
    return out


def far_messages(force, chunks, side):
    me = place_in(side)
    at = ZLANE[0 if side else 4]
    xs, ys, whole, corner = ([force[r] for r in rows] for rows in far_rows(side))
    for d, tiles in ((4, xs), (2, ys), (6, corner), (1, strips4(whole, at)), (5, strips4(xs, at)), (3, strips4(ys, at)),
                     (7, strips4(corner, at))):
        put(chunks, me ^ d, tiles)


def add_far(force, got, side):
    lane = iota(1, (3, 128))
    me = place_in(side)
    near, far = (1, 0) if side else (3, 4)
    at = ZLANE[near]
    inside = (lane >= at) & (lane < at + 27)
    xs, ys, whole, corner = far_rows(side)
    out = {r: force[r, 0:3, :] for r in whole}
    xs = [r + 5 * (near - far) for r in xs]
    ys = [r + near - far for r in ys]
    corner = [5 * near + near]
    for d, rows in ((4, xs), (2, ys), (6, corner)):
        for m, r in enumerate(rows):
            out[r] = out[r] + got[me ^ d, 3 * m:3 * m + 3, :]
    for d, rows in ((1, whole), (5, xs), (3, ys), (7, corner)):
        for n, r in enumerate(rows):
            v = got[me ^ d, 3 * (n // 4):3 * (n // 4) + 3, :]
            out[r] = out[r] + jnp.where(inside, roll_lanes(v, at - 32 * (n % 4)), 0.0)
    return out


def weight_refs(refs):
    return dict(zip(WEIGHT_NAMES, refs))


def first_pairs(part, got, nrow, nlane, live, crow, clane, *refs):
    w = weight_refs(refs[:11])
    tab, force, chunks = refs[11:14]
    s = dict(zip(ALL_SCRATCH, refs[14:]))
    have = {(x, y): part[4 * (x - 1) + y - 1] for x in range(1, 5) for y in range(1, 5)}
    for (x, y), v in widen(have, got, place_in(1), 0).items():
        tab[5 * x + y] = v
    pair_step(lambda x, y: tab[5 * x + y], nrow, nlane, live, crow, clane, w, s, force)
    sum_messages(force, chunks, 0)


def next_pairs(force, got, table, nrow, nlane, live, crow, clane, *refs):
    w = weight_refs(refs[:11])
    total, force2, chunks = refs[11:14]
    s = dict(zip(ALL_SCRATCH, refs[14:]))
    for r, f in add_messages(force, got, 1).items():
        if r // 5 in (1, 2, 3) and r % 5 in (1, 2, 3):
            total[(r // 5 - 1) * 3 + r % 5 - 1, 0:3, :] = f
        mass = inverse_mass(jnp.broadcast_to(table[r, 6:7, :], (3, 128)))
        half = (0.5 * STEP) * f * mass
        kick = table[r, 3:6, :] + half + half
        s["table"][r, 0:3, :] = table[r, 0:3, :] + STEP * kick
        s["table"][r, 3:8, :] = table[r, 3:8, :]
    pair_step(lambda x, y: s["table"][5 * x + y], nrow, nlane, live, crow, clane, w, s, force2)
    far_messages(force2, chunks, 0)


def sum_kernel(force, got, out, chunks):
    for r, v in add_messages(force, got, 0).items():
        out[r, 0:3, :] = v
    sum_messages(out, chunks, 1)


def far_kernel(force, got, out, chunks):
    for r, v in add_far(force, got, 0).items():
        out[r, 0:3, :] = v
    far_messages(out, chunks, 1)


def end_kernel(force, got, total, irow, ilane, own, new_pos, new_vel, new_frc, both):
    summed = add_far(force, got, 1)
    middle = [5 * x + y for x in (1, 2, 3) for y in (1, 2, 3)]
    for k, r in enumerate(middle):
        both[k, 0:3, :] = summed[r]
        both[k, 3:6, :] = total[k, 0:3, :]
        both[k, 6:8, :] = jnp.zeros((2, 128), f32)
    mass = inverse_mass(own[6:7, :])
    for h in range(4):
        lanes = slice(128 * h, 128 * h + 128)
        ir = jnp.broadcast_to(irow[h:h + 1, :], TILE)
        il = jnp.broadcast_to(ilane[h:h + 1, :], TILE)
        acc = jnp.zeros(TILE, f32)
        for k, r in enumerate(middle):
            acc = jnp.where(ir == r, lane_take(both[k], il), acc)
        last, first = acc[0:3], acc[3:6]
        m = mass[:, lanes]
        half = (0.5 * STEP) * first * m
        kick = own[3:6, lanes] + half + half
        new_pos[:, lanes] = own[0:3, lanes] + STEP * kick
        new_vel[:, lanes] = kick + (0.5 * STEP) * last * m
        new_frc[:, lanes] = last


ALL_SCRATCH = dict(PAIR_SCRATCH, shifted=(ROWS, 8, 128), table=(ROWS, 8, 128), spread=(8, 8, 128))


def shape(*dims, kind=f32):
    return jax.ShapeDtypeStruct(dims, kind)


def call(kernel, outs, *args, scratch=(), limit=4 << 20, flops=1 << 20, space=pltpu.VMEM):
    vm = pl.BlockSpec(memory_space=pltpu.VMEM)
    return pl.pallas_call(
        kernel,
        out_shape=tuple(outs),
        in_specs=[pl.BlockSpec(memory_space=space)] * len(args),
        out_specs=tuple([vm] * len(outs)),
        scratch_shapes=list(scratch),
        compiler_params=pltpu.CompilerParams(vmem_limit_bytes=limit),
        cost_estimate=pl.CostEstimate(flops=flops, bytes_accessed=1 << 18, transcendentals=0),
    )(*args)


def groups(side):
    out = []
    for x in range(side, SIZES[0] + side, 2):
        for y in range(side, SIZES[1] + side, 2):
            for z in range(side, SIZES[2] + side, 2):
                out.append([(((x + a) % SIZES[0]) * SIZES[1] + (y + b) % SIZES[1]) * SIZES[2] + (z + c) % SIZES[2]
                            for a in range(2) for b in range(2) for c in range(2)])
    return out


def trade(chunks, side):
    return lax.all_to_all(chunks, AXES, 0, 0, axis_index_groups=groups(side), tiled=True)


def local(positions, velocities, forces, species, cell_ids, centers, neighbours,
          w_embed, w_mix, w_value, w_env, w_latent, w_head, w_energy):
    table_shape = shape(ROWS, 8, 128)
    sums, fars = shape(8, SUM_ROWS, 128), shape(8, FAR_ROWS, 128)
    int_tile, flat = shape(8, 128, kind=i32), shape(4, 128, kind=i32)
    scratch = [pltpu.VMEM(v, f32) for v in ALL_SCRATCH.values()]

    chunks, mid, cid, own = call(
        start_kernel, [shape(8, FIRST_A, 8, 128), shape(9, 8, 128), shape(16, 128, kind=i32), shape(8, ATOMS)],
        jnp.concatenate([positions, velocities, forces, species.astype(f32)[None]], 0), cell_ids,
        scratch=[pltpu.VMEM((128, 128), i32)])
    got = trade(chunks, 0)
    weight_shapes = [shape(m, k, kind=bf16) for m, k in (
        (C, 48), (C, 192), (384, 192), (C, 768), (C, 192), (C, 192), (256, 192), (C, 1152), (C, 192), (16, 192))]
    part, chunks, *prepared = call(
        second_kernel, [shape(16, 8, 128), shape(8, FIRST_B, 8, 128), int_tile, int_tile, shape(8, 128), int_tile, int_tile, flat, flat]
        + weight_shapes + [shape(C, 128)], got, mid, neighbours, centers.reshape(1, NB), cid, w_embed.T, w_mix, w_value[0].T, w_env[0].T,
        w_latent[0], w_head, w_energy.reshape(1, C))
    idx, (irow, ilane), weights = prepared[:5], prepared[5:7], prepared[7:]
    got = trade(chunks, 1)
    table, force, chunks = call(
        first_pairs, [table_shape, table_shape, sums], part, got, *idx, *weights, scratch=scratch, limit=24 << 20, flops=1 << 30)
    force, chunks = call(sum_kernel, [table_shape, sums], force, trade(chunks, 0))
    total, force, chunks = call(
        next_pairs, [shape(9, 8, 128), table_shape, fars], force, trade(chunks, 1), table, *idx, *weights, scratch=scratch,
        limit=24 << 20, flops=1 << 30)
    force, chunks = call(far_kernel, [table_shape, fars], force, trade(chunks, 0))
    return call(end_kernel, [shape(3, ATOMS)] * 3, force, trade(chunks, 1), total, irow, ilane, own,
                scratch=[pltpu.VMEM((9, 8, 128), f32)])


def solution(mesh):
    from jax.sharding import PartitionSpec as P

    rows = P(None, AXES)
    in_specs = (rows, rows, rows, P(AXES), P(*AXES, None), P(AXES), P(AXES, None)) + (P(),) * 7
    return jax.shard_map(local, mesh=mesh, in_specs=in_specs, out_specs=(rows, rows, rows), check_vma=False)
```

```python
import math
import jax, jax.numpy as jnp
from jax import lax
from jax.experimental import pallas as pl
from jax.experimental.pallas import tpu as pltpu

f32, bf16, i32 = jnp.float32, jnp.bfloat16, jnp.int32
NB, BLK, C = 8, 128, 64
PAIRS = NB * BLK
PARTS = NB // 2
WIDE = 2 * BLK
R3, R5, R15 = math.sqrt(3.0), math.sqrt(5.0), math.sqrt(15.0)


def nt(a, b):
    return lax.dot_general(a, b, (((1,), (1,)), ((), ())), preferred_element_type=f32)


def nn(a, b):
    return jnp.dot(a, b, preferred_element_type=f32)


def split(x):
    hi = x.astype(bf16)
    return hi, (x - hi.astype(f32)).astype(bf16)


def stack3(x):
    hi, lo = split(x)
    return jnp.concatenate([hi, lo, hi], 0)


def sigmoid(z):
    return 0.5 * jnp.tanh(0.5 * z) + 0.5


def harmonic_rows(ux, uy, uz):
    return [jnp.ones_like(ux), R3 * ux, R3 * uy, R3 * uz, R15 * ux * uy, R15 * uy * uz,
            0.5 * R5 * (3.0 * uz * uz - 1.0), R15 * ux * uz, 0.5 * R15 * (ux * ux - uy * uy)]


def pair_grads(disp, kc, kn, live, w, s):
    dx, dy, dz = disp
    r = jnp.sqrt(dx * dx + dy * dy + dz * dz + 0.09)
    rinv = 1.0 / r
    ux, uy, uz = dx * rinv, dy * rinv, dz * rinv
    q = jnp.minimum(r * (1.0 / 6.0), 1.0)
    q2 = q * q
    q4 = q2 * q2
    q5 = q4 * q
    q6 = q4 * q2
    f = (1.0 - 28.0 * q6 + 48.0 * (q6 * q) - 21.0 * (q6 * q2)) * live
    fp = -28.0 * q5 * (1.0 - q) * (1.0 - q) * live
    theta = math.pi * q
    s1, c1 = jnp.sin(theta), jnp.cos(theta)
    sm, cm = s1, c1
    norm = math.sqrt(1.0 / 3.0)
    rn = norm * rinv
    slopes = []
    for m in range(8):
        s["feat"][m] = sm * rn
        slopes.append((cm * (math.pi / 6.0 * (m + 1)) - sm * rinv) * rn)
        sm, cm = sm * c1 + cm * s1, cm * c1 - sm * s1
    ys = harmonic_rows(ux, uy, uz)
    for n in range(9):
        s["harm"][n] = ys[n]
    for n in range(9, 16):
        s["harm"][n] = jnp.zeros((8, 128), f32)
    s["sc"][0] = f
    s["sc"][1] = kc
    s["sc"][2] = kn

    parts = range(PARTS)
    sub8 = lax.broadcasted_iota(i32, (8, BLK), 0).astype(f32)

    def features(b):
        hot = jnp.where(sub8 < 4.0, jnp.broadcast_to(s["sc"][1, b:b + 1, :], (8, BLK)),
                        jnp.broadcast_to(s["sc"][2, b:b + 1, :], (8, BLK)) + 4.0) == sub8
        return jnp.concatenate([s["feat"][:, b, :], hot.astype(f32)], 0)

    def envelope(j):
        return jnp.concatenate([s["sc"][0, b:b + 1, :] for b in (2 * j, 2 * j + 1)], 1)

    fw = [envelope(j) for j in parts]
    d1, d2, d3, a, x, sums, t = ([None] * PARTS for _ in range(7))
    h = [None] * PARTS
    for j in parts:
        feat = jnp.concatenate([features(2 * j), features(2 * j + 1)], 1)
        z = nn(w["emb"][...], stack3(feat))
        g = sigmoid(z)
        h[j] = z * g
        d1[j] = g + h[j] * (1.0 - g)
    for j in parts:
        z = nn(w["mix"][...], stack3(h[j]))
        g = sigmoid(z)
        a[j] = z * g
        d2[j] = g + a[j] * (1.0 - g)
        x[j] = a[j] * fw[j]
    for j in parts:
        s["vw"][j] = nn(w["ve"][...], stack3(x[j]))

    zero = jnp.zeros((16, BLK), f32)
    bd3, rep = [], []
    for j in parts:
        y0, y1 = s["harm"][:, 2 * j, :], s["harm"][:, 2 * j + 1, :]
        bd = jnp.concatenate([jnp.concatenate([y0, zero], 1), jnp.concatenate([zero, y1], 1)], 0)
        hi, lo = split(bd)
        none = jnp.zeros((32, WIDE), bf16)
        bd3.append(jnp.concatenate([hi, lo, hi, none], 0))
        rep.append(jnp.concatenate([hi, hi, hi, none, lo, lo, lo, none], 0))

    row = lax.broadcasted_iota(i32, (192, 128), 0) // C
    col = lax.broadcasted_iota(i32, (192, 128), 1)
    part = col % 16
    order = jnp.where(part == 0, 0, jnp.where(part < 4, 1, jnp.where(part < 9, 2, 3)))
    mask = jnp.where(row == order, 0.1, 0.0).astype(f32)

    def moments(val, j):
        out = nt(jnp.concatenate(split(val), 0), rep[j])
        return (out[0:192, 0:128] + out[192:384, 0:128] + out[0:192, 128:256]) * mask

    def sharp(m):
        hi, lo = split(m)
        return jnp.where(col < 64, hi.astype(f32), lo.astype(f32)).astype(bf16)

    for j in parts:
        sums[j] = moments(s["vw"][j, 192:384, :], j)
    for j in parts:
        s["t"][j] = nn(sharp(sums[j]), bd3[j])
    bb, x2 = [None] * PARTS, [None] * PARTS
    for j in parts:
        sc = s["vw"][j, 0:192, :] * s["t"][j]
        z = nn(w["lat"][...], stack3(jnp.concatenate([x[j], sc], 0)))
        g = sigmoid(z)
        bb[j] = z * g
        d3[j] = g + bb[j] * (1.0 - g)
        x2[j] = x[j] + bb[j] * fw[j]
    wen = jnp.concatenate([w["energy"][...]] * 2, 1)
    df, dx2, dxa = ([None] * PARTS for _ in range(3))
    dz = [None] * PARTS
    for j in parts:
        z = nn(w["head"][...], stack3(x2[j]))
        g = sigmoid(z)
        hh = z * g
        df[j] = jnp.sum(wen * hh, 0, keepdims=True)
        dz[j] = wen * fw[j] * (g + hh * (1.0 - g))
    for j in parts:
        dx2[j] = nn(w["head_t"][...], stack3(dz[j]))
        df[j] = df[j] + jnp.sum(dx2[j] * bb[j], 0, keepdims=True)
        dz[j] = dx2[j] * fw[j] * d3[j]
    for j in parts:
        dc = nn(w["lat_t"][...], stack3(dz[j]))
        dxa[j] = dx2[j] + dc[0:64]
        ds = dc[64:256]
        s["dv"][j] = ds * s["t"][j]
        s["dt"][j] = ds * s["vw"][j, 0:192, :]
    m = [None] * PARTS
    for j in parts:
        m[j] = moments(s["dt"][j], j)
    for j in parts:
        s["dw"][j] = nn(sharp(m[j]), bd3[j])
    for j in parts:
        acc = None
        for left, right in ((sums[j], s["dt"][j]), (m[j], s["vw"][j, 192:384, :])):
            lt = jnp.transpose(left)[0:32]
            lh, ll = split(lt)
            rh, rl = split(right)
            both = nn(jnp.concatenate([lh, ll], 0), rh)
            one = both[0:32] + both[32:64] + nn(lh, rl)
            acc = one if acc is None else acc + one
        s["dy"][2 * j] = acc[0:16, 0:128]
        s["dy"][2 * j + 1] = acc[16:32, 128:256]
    for j in parts:
        dx = dxa[j] + nn(w["ve_t"][...], stack3(jnp.concatenate([s["dv"][j], s["dw"][j]], 0)))
        df[j] = df[j] + jnp.sum(dx * a[j], 0, keepdims=True)
        dz[j] = dx * fw[j] * d2[j]
        for k in range(2):
            s["sc"][3, 2 * j + k:2 * j + k + 1, :] = df[j][:, 128 * k:128 * k + 128]
    for j in parts:
        dz[j] = nn(w["mix_t"][...], stack3(dz[j])) * d1[j]
    for j in parts:
        dr8 = nn(w["emb_t"][...], stack3(dz[j]))
        for k in range(2):
            s["dr"][2 * j + k] = dr8[0:8, 128 * k:128 * k + 128]

    dr = s["sc"][3] * fp
    for k in range(8):
        dr = dr + s["dr"][:, k, :] * slopes[k]
    gy = [s["dy"][:, n, :] for n in range(9)]
    dux = R3 * gy[1] + R15 * (uy * gy[4] + uz * gy[7] + ux * gy[8])
    duy = R3 * gy[2] + R15 * (ux * gy[4] + uz * gy[5] - uy * gy[8])
    duz = R3 * gy[3] + R15 * (uy * gy[5] + ux * gy[7]) + (3.0 * R5) * uz * gy[6]
    dot = dux * ux + duy * uy + duz * uz
    along = dr - dot * rinv
    scale = 50.0
    return [scale * (du * rinv + along * u) for du, u in ((dux, ux), (duy, uy), (duz, uz))]


PAIR_SCRATCH = {
    "feat": (8, 8, 128), "harm": (16, 8, 128), "sc": (4, 8, 128), "vw": (PARTS, 384, WIDE), "t": (PARTS, 192, WIDE),
    "dv": (PARTS, 192, WIDE), "dt": (PARTS, 192, WIDE), "dw": (PARTS, 192, WIDE), "dy": (8, 16, 128), "dr": (8, 8, 128),
}
WEIGHT_NAMES = ("emb", "mix", "ve", "lat", "head", "head_t", "lat_t", "ve_t", "mix_t", "emb_t", "energy")


SIDE = 8
ATOMS = SIDE ** 3
ROWS = 25
STEP = 0.1
MASSES = (1.008, 15.999, 22.99, 35.453)
ZLANE = (0, 27, 54, 72, 99)
WIDTHS = (3, 2, 3)
EDGE = 2.0 * SIDE
TILE = (8, 128)
AXES = ("gx", "gy", "gz")
SIZES = (16, 8, 8)
FIRST_A, FIRST_B = 3, 4
SUM_ROWS, FAR_ROWS = 40, 16


def iota(dim, shape=TILE):
    return lax.broadcasted_iota(i32, shape, dim)


def lane_take(row, idx):
    return jnp.take_along_axis(row, idx, axis=1)


def roll_rows(v, shift):
    return v if shift % 8 == 0 else pltpu.roll(v, shift % 8, 0)


def roll_lanes(v, shift):
    return v if shift % 128 == 0 else pltpu.roll(v, shift % 128, 1)


def inverse_mass(kind):
    out = jnp.full(kind.shape, 1.0 / MASSES[3], f32)
    for k in range(3):
        out = jnp.where(kind == float(k), 1.0 / MASSES[k], out)
    return out


def parity():
    return [lax.axis_index(a) & 1 for a in AXES]


def place_in(side):
    p = parity()
    return (p[0] * 4 + p[1] * 2 + p[2]) ^ (7 if side else 0)


def pack4(rows, start):
    lane = iota(1)
    out = []
    for k in range(0, len(rows), 4):
        v = roll_lanes(rows[k], -start)
        for p in range(1, len(rows[k:k + 4])):
            v = jnp.where(lane >= 32 * p, roll_lanes(rows[k + p], 32 * p - start), v)
        out.append(v)
    return out


def start_kernel(given, spec, cells, cen, energy, chunks, mid, cid, own, raw):
    px, py, pz = parity()
    raw[...] = jnp.zeros((128, 128), i32)
    kind = spec[...].astype(f32)
    mass = inverse_mass(kind)
    kick = given[3:6, :] + (0.5 * STEP) * given[6:9, :] * mass
    own[0:3, :] = given[0:3, :] + STEP * kick
    own[3:6, :] = kick
    own[6:7, :] = kind
    own[7:8, :] = jnp.zeros_like(kind)
    for x in range(3):
        for y in range(3):
            at = 8 * (3 * x + y)
            raw[at:at + 3, 0:27] = cells[x + px * (2 - 2 * x), y + py * (2 - 2 * y)]
    z0, z1, z2 = (raw[pl.ds(k, 16, stride=8), :] for k in range(3))
    lane = iota(1, (16, 128))
    flip = jnp.full((16, 128), pz, i32) == 1
    ids = jnp.where(lane < ZLANE[2], pltpu.roll(jnp.where(flip, z2, z0), ZLANE[1], 1),
                    jnp.where(lane < ZLANE[3], pltpu.roll(z1, ZLANE[2], 1), pltpu.roll(jnp.where(flip, z0, z2), ZLANE[3], 1)))
    cid[...] = jnp.where((lane >= ZLANE[1]) & (lane < ZLANE[4]), ids, 0)
    cuts = [own[:, 128 * h:128 * h + 128] for h in range(4)]
    rows = []
    for r in range(9):
        ids = jnp.broadcast_to(cid[r:r + 1, :], TILE)
        lo, hi = ids & 127, ids >> 7
        acc = lane_take(cuts[0], lo)
        for h in range(1, 4):
            acc = jnp.where(hi == h, lane_take(cuts[h], lo), acc)
        mid[r] = acc
        rows.append(acc)
    me = place_in(0)
    zs = ZLANE[3]
    for d, tiles in ((4, rows[6:9]), (2, rows[2::3]), (6, rows[8:9]), (1, pack4(rows, zs)), (5, pack4(rows[6:9], zs)),
                     (3, pack4(rows[2::3], zs)), (7, pack4(rows[8:9], zs))):
        for k, v in enumerate(tiles):
            chunks[me ^ d, k] = v


def widen(have, got, me, face):
    lane = iota(1)
    beyond = (lambda: lane >= ZLANE[4]) if face else (lambda: lane < ZLANE[1])
    at = ZLANE[face]
    xs = sorted({x for x, _ in have})
    rows = sorted(have)

    def strip(d, keys, base):
        out = {}
        for n, key in enumerate(keys):
            v = roll_lanes(got[me ^ d, n // 4], at - 32 * (n % 4))
            out[key] = jnp.where(beyond(), v, base[key])
        return out

    new = strip(1, rows, have)
    new.update(strip(5, [(face, y) for y in xs], {(face, y): got[me ^ 4, n] for n, y in enumerate(xs)}))
    new.update(strip(3, [(x, face) for x in xs], {(x, face): got[me ^ 2, n] for n, x in enumerate(xs)}))
    new.update(strip(7, [(face, face)], {(face, face): got[me ^ 6, 0]}))
    return new


def widened(got, mid, table, chunks):
    have = {(r // 3 + 1, r % 3 + 1): mid[r] for r in range(9)}
    have = widen(have, got, place_in(0), 4)
    for (x, y), v in have.items():
        table[4 * (x - 1) + y - 1] = v
    me = place_in(1)
    zs = ZLANE[1]
    along_x = [have[1, y] for y in range(1, 5)]
    along_y = [have[x, 1] for x in range(1, 5)]
    whole = [have[x, y] for x in range(1, 5) for y in range(1, 5)]
    for d, tiles in ((4, along_x), (2, along_y), (6, along_x[:1]), (1, pack4(whole, zs)), (5, pack4(along_x, zs)),
                     (3, pack4(along_y, zs)), (7, pack4(along_x[:1], zs))):
        for k, v in enumerate(tiles):
            chunks[me ^ d, k] = v


def second_kernel(got, mid, neigh, cen, cid, emb, mix, val, env, lat, head, energy,
                  table, chunks, nrow, nlane, live, crow, clane, irow, ilane, *out):
    widened(got, mid, table, chunks)
    sub, lane = iota(0), iota(1)
    big = iota(0, (128, 128))
    left, right = [], []
    for r in range(9):
        area = WIDTHS[r // 3] * WIDTHS[r % 3]
        ids = jnp.broadcast_to(cid[r:r + 1, :], TILE)
        valid = (lane >= 27) & (lane < 27 + 3 * area)
        valid = valid | ((lane >= 54) & (lane < 54 + 2 * area))
        valid = valid | ((lane >= 72) & (lane < 72 + 3 * area))
        row = (r // 3 + 1) * 5 + r % 3 + 1
        value = jnp.where((sub & 1) == 0, row, lane)
        left.append(jnp.where(valid & ((ids >> 7) == (sub >> 1)), value, 0).astype(f32).astype(bf16))
        lo = jnp.broadcast_to(cid[r:r + 1, :], (128, 128)) & 127
        right.append(jnp.where(big == lo, 1.0, 0.0).astype(bf16))
    inv = nt(jnp.concatenate(left, 1), jnp.concatenate(right, 1))
    inv = (inv + 0.5).astype(i32)
    for h in range(4):
        irow[h:h + 1, :] = inv[2 * h:2 * h + 1, :]
        ilane[h:h + 1, :] = inv[2 * h + 1:2 * h + 2, :]
    px, py, pz = parity()

    def flip(e, p):
        return e + p * (4 - 2 * e)

    def place(n):
        lo, hi = n & 127, n >> 7
        row = jnp.zeros(TILE, i32)
        col = jnp.zeros(TILE, i32)
        for h in range(4):
            row = jnp.where(hi == h, lane_take(jnp.broadcast_to(irow[h:h + 1, :], TILE), lo), row)
            col = jnp.where(hi == h, lane_take(jnp.broadcast_to(ilane[h:h + 1, :], TILE), lo), col)
        m = jnp.maximum(n - ATOMS, 0)
        grow = ((m.astype(f32) + 0.5) * (1.0 / 135.0)).astype(i32)
        rem = m - 135 * grow
        ex = ((grow.astype(f32) + 0.5) * 0.2).astype(i32)
        ey = grow - 5 * ex
        ez = ((rem.astype(f32) + 0.5) * (1.0 / 27.0)).astype(i32)
        slot = rem - 27 * ez
        ex, ey, ez = flip(ex, px), flip(ey, py), flip(ez, pz)
        first = jnp.where(ez == 0, 0, jnp.where(ez == 1, 27, jnp.where(ez == 2, 54, jnp.where(ez == 3, 72, 99))))
        return jnp.where(hi < 4, row, 5 * ex + ey), jnp.where(hi < 4, col, first + slot)

    n = neigh[...]
    c = jnp.concatenate([cen[...].astype(f32), jnp.zeros((1, 120), f32)], 1)
    c = jnp.sum(jnp.where(lane == sub, jnp.broadcast_to(c, TILE), 0.0), 1, keepdims=True)
    c = (jnp.broadcast_to(c, TILE) + 0.5).astype(i32)
    nrow[...], nlane[...] = place(n)
    crow[...], clane[...] = place(c)
    live[...] = jnp.where(n != c, 1.0, 0.0)

    def stack(w):
        hi = w.astype(bf16).astype(f32)
        return jnp.concatenate([hi, hi, w - hi], 1).astype(bf16)

    ve_t = jnp.concatenate([val[...], env[...]], 1)
    emb_t = jnp.concatenate([emb[0:8, :], jnp.zeros((8, C), f32)], 0)
    wide_energy = jnp.broadcast_to(energy[...], (128, C))
    tiles = (stack(emb[...].T), stack(mix[...]), stack(ve_t.T), stack(lat[...]), stack(head[...]), stack(head[...].T),
             stack(lat[...].T), stack(ve_t), stack(mix[...].T), stack(emb_t), wide_energy.T)
    for ref, v in zip(out, tiles):
        ref[...] = v


def pair_step(tab, nrow, nlane, live, crow, clane, w, s, force):
    sub, lane = iota(0), iota(1)
    px, py, pz = (1.0 - 2.0 * p.astype(f32) for p in parity())
    zshift = jnp.where(lane < ZLANE[1], -EDGE, jnp.where(lane >= ZLANE[4], EDGE, 0.0)) * pz
    zshift = jnp.where(sub == 2, zshift, 0.0)
    xshift = jnp.where(sub == 0, EDGE, 0.0) * px
    yshift = jnp.where(sub == 1, EDGE, 0.0) * py
    nr, nl, cr, cl = nrow[...], nlane[...], crow[...], clane[...]
    near = [jnp.zeros(TILE, f32) for _ in range(4)]
    centre = [jnp.zeros(TILE, f32) for _ in range(4)]
    for r in range(ROWS):
        ex, ey = r // 5, r % 5
        shift = zshift
        if ex in (0, 4):
            shift = shift + xshift * float(ex // 2 - 1)
        if ey in (0, 4):
            shift = shift + yshift * float(ey // 2 - 1)
        s["shifted"][r] = tab(ex, ey) + shift
        mine = nr == r
        centred = cr == r
        for k, q in enumerate((0, 1, 2, 6)):
            line = jnp.broadcast_to(s["shifted"][r, q:q + 1, :], TILE)
            near[k] = jnp.where(mine, lane_take(line, nl), near[k])
            if ex in (1, 2, 3) and ey in (1, 2, 3):
                centre[k] = jnp.where(centred, lane_take(line, cl), centre[k])
    alive = live[...]
    disp = [near[k] - centre[k] for k in range(3)]
    grads = pair_grads(disp, centre[3], near[3], alive, w, s)
    spare = 1.0 / jnp.sum(1.0 - alive, 1, keepdims=True)
    for k, g in enumerate(grads):
        g = jnp.where(alive > 0.0, -g, jnp.sum(g, 1, keepdims=True) * spare)
        hi = g.astype(bf16).astype(f32)
        s["spread"][k] = hi
        s["spread"][k + 3] = g - hi
    s["spread"][6] = jnp.zeros(TILE, f32)
    s["spread"][7] = jnp.zeros(TILE, f32)
    big = iota(0, (128, 128))
    left, right = [], []
    for b in range(NB):
        g = s["spread"][:, b, :]
        rows = jnp.broadcast_to(nrow[b:b + 1, :], TILE)
        left.append(jnp.concatenate([jnp.where(rows == r, g, 0.0) for r in range(ROWS)], 0).astype(bf16))
        right.append(jnp.where(big == jnp.broadcast_to(nlane[b:b + 1, :], (128, 128)), 1.0, 0.0).astype(bf16))
    out = nt(jnp.concatenate(left, 1), jnp.concatenate(right, 1))
    for r in range(ROWS):
        v = out[8 * r:8 * r + 8]
        force[r] = jnp.where(sub < 3, v + roll_rows(v, -3), 0.0)


def far_rows(side):
    far = 0 if side else 4
    rest = (1, 2, 3) if side else (0, 1, 2, 3)
    return [5 * far + y for y in rest], [5 * x + far for x in rest], [5 * x + y for x in rest for y in rest], [5 * far + far]


def put(chunks, d, values):
    for m, v in enumerate(values):
        chunks[d, 3 * m:3 * m + 3, :] = v[0:3]


def strips4(rows, at):
    return pack4(rows, at)


def strips2(rows, head, tail):
    lane = iota(1)
    out = []
    for k in range(0, len(rows), 2):
        v = None
        for n, q in enumerate(rows[k:k + 2]):
            t = jnp.where(lane < 64 * n + 27, roll_lanes(q, 64 * n - head), roll_lanes(q, 64 * n + 27 - tail))
            v = t if v is None else jnp.where(lane >= 64, t, v)
        out.append(v)
    return out


def sum_messages(force, chunks, side):
    me = place_in(side)
    near, far = (1, 0) if side else (3, 4)
    head, tail = (ZLANE[near], ZLANE[far]) if side else (ZLANE[far], ZLANE[near])
    f = [force[r] for r in range(ROWS)]
    xs = [f[5 * x + y] for x in (far, near) for y in range(5)]
    ys = [f[5 * x + y] for y in (far, near) for x in range(5)]
    corner = [f[5 * x + y] for x in (far, near) for y in (far, near)]
    for d, tiles in ((4, xs), (2, ys), (6, corner), (1, strips2(f, head, tail)), (5, strips2(xs, head, tail)),
                     (3, strips2(ys, head, tail)), (7, strips2(corner, head, tail))):
        put(chunks, me ^ d, tiles)


def add_messages(force, got, side):
    lane = iota(1, (3, 128))
    me = place_in(side)
    near, far = (1, 0) if side else (3, 4)
    inside = lane >= ZLANE[3] if side == 0 else lane < ZLANE[2]
    first = min(ZLANE[near], ZLANE[far])
    out = {r: force[r, 0:3, :] for r in range(ROWS)}
    xs = [5 * x + y for x in (near, far) for y in range(5)]
    ys = [5 * x + y for y in (near, far) for x in range(5)]
    corner = [5 * x + y for x in (near, far) for y in (near, far)]
    for d, rows in ((4, xs), (2, ys), (6, corner)):
        for m, r in enumerate(rows):
            out[r] = out[r] + got[me ^ d, 3 * m:3 * m + 3, :]
    for d, rows in ((1, list(range(ROWS))), (5, xs), (3, ys), (7, corner)):
        for n, r in enumerate(rows):
            v = got[me ^ d, 3 * (n // 2):3 * (n // 2) + 3, :]
            out[r] = out[r] + jnp.where(inside, roll_lanes(v, first - 64 * (n % 2)), 0.0)
    return out


def far_messages(force, chunks, side):
    me = place_in(side)
    at = ZLANE[0 if side else 4]
    xs, ys, whole, corner = ([force[r] for r in rows] for rows in far_rows(side))
    for d, tiles in ((4, xs), (2, ys), (6, corner), (1, strips4(whole, at)), (5, strips4(xs, at)), (3, strips4(ys, at)),
                     (7, strips4(corner, at))):
        put(chunks, me ^ d, tiles)


def add_far(force, got, side):
    lane = iota(1, (3, 128))
    me = place_in(side)
    near, far = (1, 0) if side else (3, 4)
    at = ZLANE[near]
    inside = (lane >= at) & (lane < at + 27)
    xs, ys, whole, corner = far_rows(side)
    out = {r: force[r, 0:3, :] for r in whole}
    xs = [r + 5 * (near - far) for r in xs]
    ys = [r + near - far for r in ys]
    corner = [5 * near + near]
    for d, rows in ((4, xs), (2, ys), (6, corner)):
        for m, r in enumerate(rows):
            out[r] = out[r] + got[me ^ d, 3 * m:3 * m + 3, :]
    for d, rows in ((1, whole), (5, xs), (3, ys), (7, corner)):
        for n, r in enumerate(rows):
            v = got[me ^ d, 3 * (n // 4):3 * (n // 4) + 3, :]
            out[r] = out[r] + jnp.where(inside, roll_lanes(v, at - 32 * (n % 4)), 0.0)
    return out


def weight_refs(refs):
    return dict(zip(WEIGHT_NAMES, refs))


def first_pairs(part, got, nrow, nlane, live, crow, clane, *refs):
    w = weight_refs(refs[:11])
    tab, force, chunks = refs[11:14]
    s = dict(zip(ALL_SCRATCH, refs[14:]))
    have = {(x, y): part[4 * (x - 1) + y - 1] for x in range(1, 5) for y in range(1, 5)}
    for (x, y), v in widen(have, got, place_in(1), 0).items():
        tab[5 * x + y] = v
    pair_step(lambda x, y: tab[5 * x + y], nrow, nlane, live, crow, clane, w, s, force)
    sum_messages(force, chunks, 1)


def next_pairs(force, got, table, nrow, nlane, live, crow, clane, *refs):
    w = weight_refs(refs[:11])
    total, force2, chunks = refs[11:14]
    s = dict(zip(ALL_SCRATCH, refs[14:]))
    for r, f in add_messages(force, got, 0).items():
        if r // 5 in (1, 2, 3) and r % 5 in (1, 2, 3):
            total[(r // 5 - 1) * 3 + r % 5 - 1, 0:3, :] = f
        mass = inverse_mass(jnp.broadcast_to(table[r, 6:7, :], (3, 128)))
        half = (0.5 * STEP) * f * mass
        kick = table[r, 3:6, :] + half + half
        s["table"][r, 0:3, :] = table[r, 0:3, :] + STEP * kick
        s["table"][r, 3:8, :] = table[r, 3:8, :]
    pair_step(lambda x, y: s["table"][5 * x + y], nrow, nlane, live, crow, clane, w, s, force2)
    far_messages(force2, chunks, 0)


def sum_kernel(force, got, out, chunks):
    for r, v in add_messages(force, got, 1).items():
        out[r, 0:3, :] = v
    sum_messages(out, chunks, 0)


def far_kernel(force, got, out, chunks):
    for r, v in add_far(force, got, 0).items():
        out[r, 0:3, :] = v
    far_messages(out, chunks, 1)


def end_kernel(force, got, total, irow, ilane, own, new_pos, new_vel, new_frc, both):
    summed = add_far(force, got, 1)
    middle = [5 * x + y for x in (1, 2, 3) for y in (1, 2, 3)]
    for k, r in enumerate(middle):
        both[k, 0:3, :] = summed[r]
        both[k, 3:6, :] = total[k, 0:3, :]
        both[k, 6:8, :] = jnp.zeros((2, 128), f32)
    mass = inverse_mass(own[6:7, :])
    for h in range(4):
        lanes = slice(128 * h, 128 * h + 128)
        ir = jnp.broadcast_to(irow[h:h + 1, :], TILE)
        il = jnp.broadcast_to(ilane[h:h + 1, :], TILE)
        acc = jnp.zeros(TILE, f32)
        for k, r in enumerate(middle):
            acc = jnp.where(ir == r, lane_take(both[k], il), acc)
        last, first = acc[0:3], acc[3:6]
        m = mass[:, lanes]
        half = (0.5 * STEP) * first * m
        kick = own[3:6, lanes] + half + half
        new_pos[:, lanes] = own[0:3, lanes] + STEP * kick
        new_vel[:, lanes] = kick + (0.5 * STEP) * last * m
        new_frc[:, lanes] = last


ALL_SCRATCH = dict(PAIR_SCRATCH, shifted=(ROWS, 8, 128), table=(ROWS, 8, 128), spread=(8, 8, 128))


def shape(*dims, kind=f32):
    return jax.ShapeDtypeStruct(dims, kind)


def call(kernel, outs, *args, scratch=(), limit=4 << 20, flops=1 << 20, space=pltpu.VMEM):
    vm = pl.BlockSpec(memory_space=pltpu.VMEM)
    return pl.pallas_call(
        kernel,
        out_shape=tuple(outs),
        in_specs=[pl.BlockSpec(memory_space=space)] * len(args),
        out_specs=tuple([vm] * len(outs)),
        scratch_shapes=list(scratch),
        compiler_params=pltpu.CompilerParams(vmem_limit_bytes=limit),
        cost_estimate=pl.CostEstimate(flops=flops, bytes_accessed=1 << 18, transcendentals=0),
    )(*args)


def groups(side):
    out = []
    for x in range(side, SIZES[0] + side, 2):
        for y in range(side, SIZES[1] + side, 2):
            for z in range(side, SIZES[2] + side, 2):
                out.append([(((x + a) % SIZES[0]) * SIZES[1] + (y + b) % SIZES[1]) * SIZES[2] + (z + c) % SIZES[2]
                            for a in range(2) for b in range(2) for c in range(2)])
    return out


def trade(chunks, side):
    return lax.all_to_all(chunks, AXES, 0, 0, axis_index_groups=groups(side), tiled=True)


def local(positions, velocities, forces, species, cell_ids, centers, neighbours,
          w_embed, w_mix, w_value, w_env, w_latent, w_head, w_energy):
    table_shape = shape(ROWS, 8, 128)
    cen, energy = centers.reshape(1, NB), w_energy.reshape(1, C)
    sums, fars = shape(8, SUM_ROWS, 128), shape(8, FAR_ROWS, 128)
    int_tile, flat = shape(8, 128, kind=i32), shape(4, 128, kind=i32)
    scratch = [pltpu.VMEM(v, f32) for v in ALL_SCRATCH.values()]

    chunks, mid, cid, own = call(
        start_kernel, [shape(8, FIRST_A, 8, 128), shape(9, 8, 128), shape(16, 128, kind=i32), shape(8, ATOMS)],
        jnp.concatenate([positions, velocities, forces], 0), species.reshape(1, ATOMS), cell_ids, cen, energy,
        scratch=[pltpu.VMEM((128, 128), i32)])
    got = trade(chunks, 0)
    weight_shapes = [shape(m, k, kind=bf16) for m, k in (
        (C, 48), (C, 192), (384, 192), (C, 768), (C, 192), (C, 192), (256, 192), (C, 1152), (C, 192), (16, 192))]
    part, chunks, *prepared = call(
        second_kernel, [shape(16, 8, 128), shape(8, FIRST_B, 8, 128), int_tile, int_tile, shape(8, 128), int_tile, int_tile, flat, flat]
        + weight_shapes + [shape(C, 128)], got, mid, neighbours, cen, cid, w_embed.T, w_mix, w_value[0].T, w_env[0].T,
        w_latent[0], w_head, energy)
    idx, (irow, ilane), weights = prepared[:5], prepared[5:7], prepared[7:]
    got = trade(chunks, 1)
    table, force, chunks = call(
        first_pairs, [table_shape, table_shape, sums], part, got, *idx, *weights, scratch=scratch, limit=24 << 20, flops=1 << 30)
    force, chunks = call(sum_kernel, [table_shape, sums], force, trade(chunks, 1))
    total, force, chunks = call(
        next_pairs, [shape(9, 8, 128), table_shape, fars], force, trade(chunks, 0), table, *idx, *weights, scratch=scratch,
        limit=24 << 20, flops=1 << 30)
    force, chunks = call(far_kernel, [table_shape, fars], force, trade(chunks, 0))
    return call(end_kernel, [shape(3, ATOMS)] * 3, force, trade(chunks, 1), total, irow, ilane, own,
                scratch=[pltpu.VMEM((9, 8, 128), f32)])


def solution(mesh):
    from jax.sharding import PartitionSpec as P

    rows = P(None, AXES)
    in_specs = (rows, rows, rows, P(AXES), P(*AXES, None), P(AXES), P(AXES, None)) + (P(),) * 7
    return jax.shard_map(local, mesh=mesh, in_specs=in_specs, out_specs=(rows, rows, rows), check_vma=False)
```

```python
import math
import jax, jax.numpy as jnp
from jax import lax
from jax.experimental import pallas as pl
from jax.experimental.pallas import tpu as pltpu

f32, bf16, i32 = jnp.float32, jnp.bfloat16, jnp.int32
NB, BLK, C = 8, 128, 64
PAIRS = NB * BLK
PARTS = NB // 2
WIDE = 2 * BLK
R3, R5, R15 = math.sqrt(3.0), math.sqrt(5.0), math.sqrt(15.0)


def nt(a, b):
    return lax.dot_general(a, b, (((1,), (1,)), ((), ())), preferred_element_type=f32)


def nn(a, b):
    return jnp.dot(a, b, preferred_element_type=f32)


def split(x):
    hi = x.astype(bf16)
    return hi, (x - hi.astype(f32)).astype(bf16)


def stack3(x):
    hi, lo = split(x)
    return jnp.concatenate([hi, lo, hi], 0)


def sigmoid(z):
    return 0.5 * jnp.tanh(0.5 * z) + 0.5


def harmonic_rows(ux, uy, uz):
    return [jnp.ones_like(ux), R3 * ux, R3 * uy, R3 * uz, R15 * ux * uy, R15 * uy * uz,
            0.5 * R5 * (3.0 * uz * uz - 1.0), R15 * ux * uz, 0.5 * R15 * (ux * ux - uy * uy)]


def pair_grads(disp, kc, kn, live, w, s):
    dx, dy, dz = disp
    r = jnp.sqrt(dx * dx + dy * dy + dz * dz + 0.09)
    rinv = 1.0 / r
    ux, uy, uz = dx * rinv, dy * rinv, dz * rinv
    q = jnp.minimum(r * (1.0 / 6.0), 1.0)
    q2 = q * q
    q4 = q2 * q2
    q5 = q4 * q
    q6 = q4 * q2
    f = (1.0 - 28.0 * q6 + 48.0 * (q6 * q) - 21.0 * (q6 * q2)) * live
    fp = -28.0 * q5 * (1.0 - q) * (1.0 - q) * live
    theta = math.pi * q
    s1, c1 = jnp.sin(theta), jnp.cos(theta)
    sm, cm = s1, c1
    norm = math.sqrt(1.0 / 3.0)
    rn = norm * rinv
    slopes = []
    for m in range(8):
        s["feat"][m] = sm * rn
        slopes.append((cm * (math.pi / 6.0 * (m + 1)) - sm * rinv) * rn)
        sm, cm = sm * c1 + cm * s1, cm * c1 - sm * s1
    ys = harmonic_rows(ux, uy, uz)
    for n in range(9):
        s["harm"][n] = ys[n]
    for n in range(9, 16):
        s["harm"][n] = jnp.zeros((8, 128), f32)
    s["sc"][0] = f
    s["sc"][1] = kc
    s["sc"][2] = kn

    parts = range(PARTS)
    sub8 = lax.broadcasted_iota(i32, (8, BLK), 0).astype(f32)

    def features(b):
        hot = jnp.where(sub8 < 4.0, jnp.broadcast_to(s["sc"][1, b:b + 1, :], (8, BLK)),
                        jnp.broadcast_to(s["sc"][2, b:b + 1, :], (8, BLK)) + 4.0) == sub8
        return jnp.concatenate([s["feat"][:, b, :], hot.astype(f32)], 0)

    def envelope(j):
        return jnp.concatenate([s["sc"][0, b:b + 1, :] for b in (2 * j, 2 * j + 1)], 1)

    fw = [envelope(j) for j in parts]
    d1, d2, d3, a, x, sums, t = ([None] * PARTS for _ in range(7))
    h = [None] * PARTS
    for j in parts:
        feat = jnp.concatenate([features(2 * j), features(2 * j + 1)], 1)
        z = nn(w["emb"][...], stack3(feat))
        g = sigmoid(z)
        h[j] = z * g
        d1[j] = g + h[j] * (1.0 - g)
    for j in parts:
        z = nn(w["mix"][...], stack3(h[j]))
        g = sigmoid(z)
        a[j] = z * g
        d2[j] = g + a[j] * (1.0 - g)
        x[j] = a[j] * fw[j]
    for j in parts:
        s["vw"][j] = nn(w["ve"][...], stack3(x[j]))

    zero = jnp.zeros((16, BLK), f32)
    bd3, rep = [], []
    for j in parts:
        y0, y1 = s["harm"][:, 2 * j, :], s["harm"][:, 2 * j + 1, :]
        bd = jnp.concatenate([jnp.concatenate([y0, zero], 1), jnp.concatenate([zero, y1], 1)], 0)
        hi, lo = split(bd)
        none = jnp.zeros((32, WIDE), bf16)
        bd3.append(jnp.concatenate([hi, lo, hi, none], 0))
        rep.append(jnp.concatenate([hi, hi, hi, none, lo, lo, lo, none], 0))

    row = lax.broadcasted_iota(i32, (192, 128), 0) // C
    col = lax.broadcasted_iota(i32, (192, 128), 1)
    part = col % 16
    order = jnp.where(part == 0, 0, jnp.where(part < 4, 1, jnp.where(part < 9, 2, 3)))
    mask = jnp.where(row == order, 0.1, 0.0).astype(f32)

    def moments(val, j):
        out = nt(jnp.concatenate(split(val), 0), rep[j])
        return (out[0:192, 0:128] + out[192:384, 0:128] + out[0:192, 128:256]) * mask

    def sharp(m):
        hi, lo = split(m)
        return jnp.where(col < 64, hi.astype(f32), lo.astype(f32)).astype(bf16)

    for j in parts:
        sums[j] = moments(s["vw"][j, 192:384, :], j)
    for j in parts:
        s["t"][j] = nn(sharp(sums[j]), bd3[j])
    bb, x2 = [None] * PARTS, [None] * PARTS
    for j in parts:
        sc = s["vw"][j, 0:192, :] * s["t"][j]
        z = nn(w["lat"][...], stack3(jnp.concatenate([x[j], sc], 0)))
        g = sigmoid(z)
        bb[j] = z * g
        d3[j] = g + bb[j] * (1.0 - g)
        x2[j] = x[j] + bb[j] * fw[j]
    wen = jnp.concatenate([w["energy"][...]] * 2, 1)
    df, dx2, dxa = ([None] * PARTS for _ in range(3))
    dz = [None] * PARTS
    for j in parts:
        z = nn(w["head"][...], stack3(x2[j]))
        g = sigmoid(z)
        hh = z * g
        df[j] = jnp.sum(wen * hh, 0, keepdims=True)
        dz[j] = wen * fw[j] * (g + hh * (1.0 - g))
    for j in parts:
        dx2[j] = nn(w["head_t"][...], stack3(dz[j]))
        df[j] = df[j] + jnp.sum(dx2[j] * bb[j], 0, keepdims=True)
        dz[j] = dx2[j] * fw[j] * d3[j]
    for j in parts:
        dc = nn(w["lat_t"][...], stack3(dz[j]))
        dxa[j] = dx2[j] + dc[0:64]
        ds = dc[64:256]
        s["dv"][j] = ds * s["t"][j]
        s["dt"][j] = ds * s["vw"][j, 0:192, :]
    m = [None] * PARTS
    for j in parts:
        m[j] = moments(s["dt"][j], j)
    for j in parts:
        s["dw"][j] = nn(sharp(m[j]), bd3[j])
    for j in parts:
        acc = None
        for left, right in ((sums[j], s["dt"][j]), (m[j], s["vw"][j, 192:384, :])):
            lt = jnp.transpose(left)[0:32]
            lh, ll = split(lt)
            rh, rl = split(right)
            both = nn(jnp.concatenate([lh, ll], 0), rh)
            one = both[0:32] + both[32:64] + nn(lh, rl)
            acc = one if acc is None else acc + one
        s["dy"][2 * j] = acc[0:16, 0:128]
        s["dy"][2 * j + 1] = acc[16:32, 128:256]
    for j in parts:
        dx = dxa[j] + nn(w["ve_t"][...], stack3(jnp.concatenate([s["dv"][j], s["dw"][j]], 0)))
        df[j] = df[j] + jnp.sum(dx * a[j], 0, keepdims=True)
        dz[j] = dx * fw[j] * d2[j]
        for k in range(2):
            s["sc"][3, 2 * j + k:2 * j + k + 1, :] = df[j][:, 128 * k:128 * k + 128]
    for j in parts:
        dz[j] = nn(w["mix_t"][...], stack3(dz[j])) * d1[j]
    for j in parts:
        dr8 = nn(w["emb_t"][...], stack3(dz[j]))
        for k in range(2):
            s["dr"][2 * j + k] = dr8[0:8, 128 * k:128 * k + 128]

    dr = s["sc"][3] * fp
    for k in range(8):
        dr = dr + s["dr"][:, k, :] * slopes[k]
    gy = [s["dy"][:, n, :] for n in range(9)]
    dux = R3 * gy[1] + R15 * (uy * gy[4] + uz * gy[7] + ux * gy[8])
    duy = R3 * gy[2] + R15 * (ux * gy[4] + uz * gy[5] - uy * gy[8])
    duz = R3 * gy[3] + R15 * (uy * gy[5] + ux * gy[7]) + (3.0 * R5) * uz * gy[6]
    dot = dux * ux + duy * uy + duz * uz
    along = dr - dot * rinv
    scale = 50.0
    return [scale * (du * rinv + along * u) for du, u in ((dux, ux), (duy, uy), (duz, uz))]


PAIR_SCRATCH = {
    "feat": (8, 8, 128), "harm": (16, 8, 128), "sc": (4, 8, 128), "vw": (PARTS, 384, WIDE), "t": (PARTS, 192, WIDE),
    "dv": (PARTS, 192, WIDE), "dt": (PARTS, 192, WIDE), "dw": (PARTS, 192, WIDE), "dy": (8, 16, 128), "dr": (8, 8, 128),
}
WEIGHT_NAMES = ("emb", "mix", "ve", "lat", "head", "head_t", "lat_t", "ve_t", "mix_t", "emb_t", "energy")


SIDE = 8
ATOMS = SIDE ** 3
ROWS = 25
STEP = 0.1
MASSES = (1.008, 15.999, 22.99, 35.453)
ZLANE = (0, 27, 54, 72, 99)
WIDTHS = (3, 2, 3)
EDGE = 2.0 * SIDE
TILE = (8, 128)
MIDDLE = [5 * x + y for x in (1, 2, 3) for y in (1, 2, 3)]
AXES = ("gx", "gy", "gz")
SIZES = (16, 8, 8)
FIRST = 2
SUM_ROWS, FAR_ROWS = 40, 16


def iota(dim, shape=TILE):
    return lax.broadcasted_iota(i32, shape, dim)


def lane_take(row, idx):
    return jnp.take_along_axis(row, idx, axis=1)


def roll_rows(v, shift):
    return v if shift % 8 == 0 else pltpu.roll(v, shift % 8, 0)


def roll_lanes(v, shift):
    return v if shift % 128 == 0 else pltpu.roll(v, shift % 128, 1)


def inverse_mass(kind):
    out = jnp.full(kind.shape, 1.0 / MASSES[3], f32)
    for k in range(3):
        out = jnp.where(kind == float(k), 1.0 / MASSES[k], out)
    return out


def masses(kind):
    out = jnp.full(kind.shape, MASSES[3], f32)
    for k in range(3):
        out = jnp.where(kind == float(k), MASSES[k], out)
    return out


def parity():
    return [lax.axis_index(a) & 1 for a in AXES]


def place_in(side):
    p = parity()
    return (p[0] * 4 + p[1] * 2 + p[2]) ^ (7 if side else 0)


def pack4(rows, start):
    lane = iota(1)
    out = []
    for k in range(0, len(rows), 4):
        v = roll_lanes(rows[k], -start)
        for p in range(1, len(rows[k:k + 4])):
            v = jnp.where(lane >= 32 * p, roll_lanes(rows[k + p], 32 * p - start), v)
        out.append(v)
    return out


def doubled(tiles):
    sub = iota(0)
    return [jnp.where(sub < 4, tiles[k], roll_rows(tiles[k + 1], 4)) if k + 1 < len(tiles) else tiles[k] for k in range(0, len(tiles), 2)]


def start_kernel(given, spec, cells, cen, energy, chunks, mid, cid, own, raw):
    px, py, pz = parity()
    raw[...] = jnp.zeros((128, 128), i32)
    kind = spec[...].astype(f32)
    kick = given[3:6, :] + (0.5 * STEP) * given[6:9, :] * inverse_mass(kind)
    own[0:3, :] = given[0:3, :] + STEP * kick
    own[3:4, :] = kind
    own[4:7, :] = kick
    own[7:8, :] = jnp.zeros_like(kind)
    for x in range(3):
        for y in range(3):
            at = 8 * (3 * x + y)
            raw[at:at + 3, 0:27] = cells[x + px * (2 - 2 * x), y + py * (2 - 2 * y)]
    z0, z1, z2 = (raw[pl.ds(k, 16, stride=8), :] for k in range(3))
    lane = iota(1, (16, 128))
    flip = jnp.full((16, 128), pz, i32) == 1
    ids = jnp.where(lane < ZLANE[2], pltpu.roll(jnp.where(flip, z2, z0), ZLANE[1], 1),
                    jnp.where(lane < ZLANE[3], pltpu.roll(z1, ZLANE[2], 1), pltpu.roll(jnp.where(flip, z0, z2), ZLANE[3], 1)))
    cid[...] = jnp.where((lane >= ZLANE[1]) & (lane < ZLANE[4]), ids, 0)
    cuts = [own[:, 128 * h:128 * h + 128] for h in range(4)]
    rows = []
    for r in range(9):
        ids = jnp.broadcast_to(cid[r:r + 1, :], TILE)
        lo, hi = ids & 127, ids >> 7
        acc = lane_take(cuts[0], lo)
        for h in range(1, 4):
            acc = jnp.where(hi == h, lane_take(cuts[h], lo), acc)
        mid[r] = acc
        rows.append(acc)
    me = place_in(0)
    zs = ZLANE[3]
    for d, tiles in ((4, rows[6:9]), (2, rows[2::3]), (6, rows[8:9]), (1, pack4(rows, zs)), (5, pack4(rows[6:9], zs)),
                     (3, pack4(rows[2::3], zs)), (7, pack4(rows[8:9], zs))):
        for k, v in enumerate(doubled(tiles)):
            chunks[me ^ d, k] = v


def widen(have, got, me, face):
    lane = iota(1)
    beyond = (lambda: lane >= ZLANE[4]) if face else (lambda: lane < ZLANE[1])
    at = ZLANE[face]
    xs = sorted({x for x, _ in have})
    rows = sorted(have)

    def half(d, n):
        return roll_rows(got[me ^ d, n // 2], -4 * (n % 2))

    def strip(d, keys, base):
        out = {}
        for n, key in enumerate(keys):
            v = roll_lanes(half(d, n // 4), at - 32 * (n % 4))
            out[key] = jnp.where(beyond(), v, base[key])
        return out

    new = strip(1, rows, have)
    new.update(strip(5, [(face, y) for y in xs], {(face, y): half(4, n) for n, y in enumerate(xs)}))
    new.update(strip(3, [(x, face) for x in xs], {(x, face): half(2, n) for n, x in enumerate(xs)}))
    new.update(strip(7, [(face, face)], {(face, face): half(6, 0)}))
    return new


def widened(got, mid, table, chunks):
    have = {(r // 3 + 1, r % 3 + 1): mid[r] for r in range(9)}
    have = widen(have, got, place_in(0), 4)
    for (x, y), v in have.items():
        table[4 * (x - 1) + y - 1] = v
    me = place_in(1)
    zs = ZLANE[1]
    along_x = [have[1, y] for y in range(1, 5)]
    along_y = [have[x, 1] for x in range(1, 5)]
    whole = [have[x, y] for x in range(1, 5) for y in range(1, 5)]
    for d, tiles in ((4, along_x), (2, along_y), (6, along_x[:1]), (1, pack4(whole, zs)), (5, pack4(along_x, zs)),
                     (3, pack4(along_y, zs)), (7, pack4(along_x[:1], zs))):
        for k, v in enumerate(doubled(tiles)):
            chunks[me ^ d, k] = v


def second_kernel(got, mid, neigh, cen, cid, emb, mix, val, env, lat, head, energy,
                  table, chunks, nrow, nlane, live, crow, clane, irow, ilane, *out):
    widened(got, mid, table, chunks)
    sub, lane = iota(0), iota(1)
    big = iota(0, (128, 128))
    left, right = [], []
    for r in range(9):
        area = WIDTHS[r // 3] * WIDTHS[r % 3]
        ids = jnp.broadcast_to(cid[r:r + 1, :], TILE)
        valid = (lane >= 27) & (lane < 27 + 3 * area)
        valid = valid | ((lane >= 54) & (lane < 54 + 2 * area))
        valid = valid | ((lane >= 72) & (lane < 72 + 3 * area))
        row = (r // 3 + 1) * 5 + r % 3 + 1
        value = jnp.where((sub & 1) == 0, row, lane)
        left.append(jnp.where(valid & ((ids >> 7) == (sub >> 1)), value, 0).astype(f32).astype(bf16))
        lo = jnp.broadcast_to(cid[r:r + 1, :], (128, 128)) & 127
        right.append(jnp.where(big == lo, 1.0, 0.0).astype(bf16))
    inv = nt(jnp.concatenate(left, 1), jnp.concatenate(right, 1))
    inv = (inv + 0.5).astype(i32)
    for h in range(4):
        irow[h:h + 1, :] = inv[2 * h:2 * h + 1, :]
        ilane[h:h + 1, :] = inv[2 * h + 1:2 * h + 2, :]
    px, py, pz = parity()

    def flip(e, p):
        return e + p * (4 - 2 * e)

    def place(n):
        lo, hi = n & 127, n >> 7
        row = jnp.zeros(TILE, i32)
        col = jnp.zeros(TILE, i32)
        for h in range(4):
            row = jnp.where(hi == h, lane_take(jnp.broadcast_to(irow[h:h + 1, :], TILE), lo), row)
            col = jnp.where(hi == h, lane_take(jnp.broadcast_to(ilane[h:h + 1, :], TILE), lo), col)
        m = jnp.maximum(n - ATOMS, 0)
        grow = ((m.astype(f32) + 0.5) * (1.0 / 135.0)).astype(i32)
        rem = m - 135 * grow
        ex = ((grow.astype(f32) + 0.5) * 0.2).astype(i32)
        ey = grow - 5 * ex
        ez = ((rem.astype(f32) + 0.5) * (1.0 / 27.0)).astype(i32)
        slot = rem - 27 * ez
        ex, ey, ez = flip(ex, px), flip(ey, py), flip(ez, pz)
        first = jnp.where(ez == 0, 0, jnp.where(ez == 1, 27, jnp.where(ez == 2, 54, jnp.where(ez == 3, 72, 99))))
        return jnp.where(hi < 4, row, 5 * ex + ey), jnp.where(hi < 4, col, first + slot)

    n = neigh[...]
    c = jnp.concatenate([cen[...].astype(f32), jnp.zeros((1, 120), f32)], 1)
    c = jnp.sum(jnp.where(lane == sub, jnp.broadcast_to(c, TILE), 0.0), 1, keepdims=True)
    c = (jnp.broadcast_to(c, TILE) + 0.5).astype(i32)
    nrow[...], nlane[...] = place(n)
    crow[...], clane[...] = place(c)
    live[...] = jnp.where(n != c, 1.0, 0.0)

    def stack(w):
        hi = w.astype(bf16).astype(f32)
        return jnp.concatenate([hi, hi, w - hi], 1).astype(bf16)

    ve_t = jnp.concatenate([val[...], env[...]], 1)
    emb_t = jnp.concatenate([emb[0:8, :], jnp.zeros((8, C), f32)], 0)
    wide_energy = jnp.broadcast_to(energy[...], (128, C))
    tiles = (stack(emb[...].T), stack(mix[...]), stack(ve_t.T), stack(lat[...]), stack(head[...]), stack(head[...].T),
             stack(lat[...].T), stack(ve_t), stack(mix[...].T), stack(emb_t), wide_energy.T)
    for ref, v in zip(out, tiles):
        ref[...] = v


def pair_step(tab, nrow, nlane, live, crow, clane, w, s, force):
    sub, lane = iota(0), iota(1)
    px, py, pz = (1.0 - 2.0 * p.astype(f32) for p in parity())
    zshift = jnp.where(lane < ZLANE[1], -EDGE, jnp.where(lane >= ZLANE[4], EDGE, 0.0)) * pz
    zshift = jnp.where(sub == 2, zshift, 0.0)
    xshift = jnp.where(sub == 0, EDGE, 0.0) * px
    yshift = jnp.where(sub == 1, EDGE, 0.0) * py
    nr, nl, cr, cl = nrow[...], nlane[...], crow[...], clane[...]
    near = [jnp.zeros(TILE, f32) for _ in range(4)]
    centre = [jnp.zeros(TILE, f32) for _ in range(4)]
    for r in range(ROWS):
        ex, ey = r // 5, r % 5
        shift = zshift
        if ex in (0, 4):
            shift = shift + xshift * float(ex // 2 - 1)
        if ey in (0, 4):
            shift = shift + yshift * float(ey // 2 - 1)
        s["shifted"][r] = tab(ex, ey) + shift
        mine = nr == r
        centred = cr == r
        for q in range(4):
            line = jnp.broadcast_to(s["shifted"][r, q:q + 1, :], TILE)
            near[q] = jnp.where(mine, lane_take(line, nl), near[q])
            if ex in (1, 2, 3) and ey in (1, 2, 3):
                centre[q] = jnp.where(centred, lane_take(line, cl), centre[q])
    alive = live[...]
    disp = [near[k] - centre[k] for k in range(3)]
    grads = pair_grads(disp, centre[3], near[3], alive, w, s)
    spare = 1.0 / jnp.sum(1.0 - alive, 1, keepdims=True)
    for k, g in enumerate(grads):
        g = jnp.where(alive > 0.0, -g, jnp.sum(g, 1, keepdims=True) * spare)
        hi = g.astype(bf16).astype(f32)
        s["spread"][k] = hi
        s["spread"][k + 3] = g - hi
    s["spread"][6] = jnp.zeros(TILE, f32)
    s["spread"][7] = jnp.zeros(TILE, f32)
    big = iota(0, (128, 128))
    left, right = [], []
    for b in range(NB):
        g = s["spread"][:, b, :]
        rows = jnp.broadcast_to(nrow[b:b + 1, :], TILE)
        left.append(jnp.concatenate([jnp.where(rows == r, g, 0.0) for r in range(ROWS)], 0).astype(bf16))
        right.append(jnp.where(big == jnp.broadcast_to(nlane[b:b + 1, :], (128, 128)), 1.0, 0.0).astype(bf16))
    out = nt(jnp.concatenate(left, 1), jnp.concatenate(right, 1))
    for r in range(ROWS):
        v = out[8 * r:8 * r + 8]
        force[r] = jnp.where(sub < 3, v + roll_rows(v, -3), 0.0)


def far_rows(side):
    far = 0 if side else 4
    rest = (1, 2, 3) if side else (0, 1, 2, 3)
    return [5 * far + y for y in rest], [5 * x + far for x in rest], [5 * x + y for x in rest for y in rest], [5 * far + far]


def put(chunks, d, values):
    for m, v in enumerate(values):
        chunks[d, 3 * m:3 * m + 3, :] = v[0:3]


def strips4(rows, at):
    return pack4(rows, at)


def strips2(rows, head, tail):
    lane = iota(1)
    out = []
    for k in range(0, len(rows), 2):
        v = None
        for n, q in enumerate(rows[k:k + 2]):
            t = jnp.where(lane < 64 * n + 27, roll_lanes(q, 64 * n - head), roll_lanes(q, 64 * n + 27 - tail))
            v = t if v is None else jnp.where(lane >= 64, t, v)
        out.append(v)
    return out


def sum_messages(force, base, chunks, side):
    me = place_in(side)
    near, far = (1, 0) if side else (3, 4)
    head, tail = (ZLANE[near], ZLANE[far]) if side else (ZLANE[far], ZLANE[near])
    f = [force[r] for r in range(ROWS)]
    for k, r in enumerate(MIDDLE):
        f[r] = f[r] + base[k]
    xs = [f[5 * x + y] for x in (far, near) for y in range(5)]
    ys = [f[5 * x + y] for y in (far, near) for x in range(5)]
    corner = [f[5 * x + y] for x in (far, near) for y in (far, near)]
    for d, tiles in ((4, xs), (2, ys), (6, corner), (1, strips2(f, head, tail)), (5, strips2(xs, head, tail)),
                     (3, strips2(ys, head, tail)), (7, strips2(corner, head, tail))):
        put(chunks, me ^ d, tiles)


def add_messages(force, got, side):
    lane = iota(1, (3, 128))
    me = place_in(side)
    near, far = (1, 0) if side else (3, 4)
    inside = lane >= ZLANE[3] if side == 0 else lane < ZLANE[2]
    first = min(ZLANE[near], ZLANE[far])
    out = {r: force[r, 0:3, :] for r in range(ROWS)}
    xs = [5 * x + y for x in (near, far) for y in range(5)]
    ys = [5 * x + y for y in (near, far) for x in range(5)]
    corner = [5 * x + y for x in (near, far) for y in (near, far)]
    for d, rows in ((4, xs), (2, ys), (6, corner)):
        for m, r in enumerate(rows):
            out[r] = out[r] + got[me ^ d, 3 * m:3 * m + 3, :]
    for d, rows in ((1, list(range(ROWS))), (5, xs), (3, ys), (7, corner)):
        for n, r in enumerate(rows):
            v = got[me ^ d, 3 * (n // 2):3 * (n // 2) + 3, :]
            out[r] = out[r] + jnp.where(inside, roll_lanes(v, first - 64 * (n % 2)), 0.0)
    return out


def far_messages(force, chunks, side):
    me = place_in(side)
    at = ZLANE[0 if side else 4]
    xs, ys, whole, corner = ([force[r] for r in rows] for rows in far_rows(side))
    for d, tiles in ((4, xs), (2, ys), (6, corner), (1, strips4(whole, at)), (5, strips4(xs, at)), (3, strips4(ys, at)),
                     (7, strips4(corner, at))):
        put(chunks, me ^ d, tiles)


def add_far(force, got, side):
    lane = iota(1, (3, 128))
    me = place_in(side)
    near, far = (1, 0) if side else (3, 4)
    at = ZLANE[near]
    inside = (lane >= at) & (lane < at + 27)
    xs, ys, whole, corner = far_rows(side)
    out = {r: force[r, 0:3, :] for r in whole}
    xs = [r + 5 * (near - far) for r in xs]
    ys = [r + near - far for r in ys]
    corner = [5 * near + near]
    for d, rows in ((4, xs), (2, ys), (6, corner)):
        for m, r in enumerate(rows):
            out[r] = out[r] + got[me ^ d, 3 * m:3 * m + 3, :]
    for d, rows in ((1, whole), (5, xs), (3, ys), (7, corner)):
        for n, r in enumerate(rows):
            v = got[me ^ d, 3 * (n // 4):3 * (n // 4) + 3, :]
            out[r] = out[r] + jnp.where(inside, roll_lanes(v, at - 32 * (n % 4)), 0.0)
    return out


def weight_refs(refs):
    return dict(zip(WEIGHT_NAMES, refs))


def first_pairs(part, got, nrow, nlane, live, crow, clane, *refs):
    w = weight_refs(refs[:11])
    tab, force, base, chunks = refs[11:15]
    s = dict(zip(ALL_SCRATCH, refs[15:]))
    have = {(x, y): part[4 * (x - 1) + y - 1] for x in range(1, 5) for y in range(1, 5)}
    for (x, y), v in widen(have, got, place_in(1), 0).items():
        tab[5 * x + y] = v
    pair_step(lambda x, y: tab[5 * x + y], nrow, nlane, live, crow, clane, w, s, force)
    sub, lane = iota(0), iota(1)
    mine = (sub < 3) & (lane >= ZLANE[1]) & (lane < ZLANE[4])
    for k, r in enumerate(MIDDLE):
        v = tab[r]
        rest = (v + STEP * roll_rows(v, -4)) * (1.0 / (STEP * STEP)) * masses(jnp.broadcast_to(tab[r, 3:4, :], TILE))
        base[k] = jnp.where(mine, rest, 0.0)
    sum_messages(force, base, chunks, 1)


def next_pairs(force, got, table, nrow, nlane, live, crow, clane, *refs):
    w = weight_refs(refs[:11])
    total, force2, chunks = refs[11:14]
    s = dict(zip(ALL_SCRATCH, refs[14:]))
    lane = iota(1, (3, 128))
    mine = (lane >= ZLANE[1]) & (lane < ZLANE[4])
    for r, f in add_messages(force, got, 0).items():
        mass = inverse_mass(jnp.broadcast_to(table[r, 3:4, :], (3, 128)))
        moved = (STEP * STEP) * f * mass
        if r in MIDDLE:
            total[MIDDLE.index(r), 0:3, :] = f
            half = (0.5 * STEP) * f * mass
            kick = table[r, 4:7, :] + half + half
            moved = jnp.where(mine, table[r, 0:3, :] + STEP * kick, moved)
        s["table"][r] = table[r]
        s["table"][r, 0:3, :] = moved
    pair_step(lambda x, y: s["table"][5 * x + y], nrow, nlane, live, crow, clane, w, s, force2)
    far_messages(force2, chunks, 0)


def sum_kernel(force, base, got, out, chunks):
    for r, v in add_messages(force, got, 1).items():
        out[r, 0:3, :] = v
    sum_messages(out, base, chunks, 0)


def far_kernel(force, got, out, chunks):
    for r, v in add_far(force, got, 0).items():
        out[r, 0:3, :] = v
    far_messages(out, chunks, 1)


def end_kernel(force, got, total, irow, ilane, own, new_pos, new_vel, new_frc, both):
    summed = add_far(force, got, 1)
    for k, r in enumerate(MIDDLE):
        both[k, 0:3, :] = summed[r]
        both[k, 3:6, :] = total[k, 0:3, :]
        both[k, 6:8, :] = jnp.zeros((2, 128), f32)
    mass = inverse_mass(own[3:4, :])
    for h in range(4):
        lanes = slice(128 * h, 128 * h + 128)
        ir = jnp.broadcast_to(irow[h:h + 1, :], TILE)
        il = jnp.broadcast_to(ilane[h:h + 1, :], TILE)
        acc = jnp.zeros(TILE, f32)
        for k, r in enumerate(MIDDLE):
            acc = jnp.where(ir == r, lane_take(both[k], il), acc)
        last, first = acc[0:3], acc[3:6]
        m = mass[:, lanes]
        half = (0.5 * STEP) * first * m
        kick = own[4:7, lanes] + half + half
        new_pos[:, lanes] = own[0:3, lanes] + STEP * kick
        new_vel[:, lanes] = kick + (0.5 * STEP) * last * m
        new_frc[:, lanes] = last


ALL_SCRATCH = dict(PAIR_SCRATCH, shifted=(ROWS, 8, 128), table=(ROWS, 8, 128), spread=(8, 8, 128))


def shape(*dims, kind=f32):
    return jax.ShapeDtypeStruct(dims, kind)


def call(kernel, outs, *args, scratch=(), limit=4 << 20, flops=1 << 20, space=pltpu.VMEM):
    vm = pl.BlockSpec(memory_space=pltpu.VMEM)
    return pl.pallas_call(
        kernel,
        out_shape=tuple(outs),
        in_specs=[pl.BlockSpec(memory_space=space)] * len(args),
        out_specs=tuple([vm] * len(outs)),
        scratch_shapes=list(scratch),
        compiler_params=pltpu.CompilerParams(vmem_limit_bytes=limit),
        cost_estimate=pl.CostEstimate(flops=flops, bytes_accessed=1 << 18, transcendentals=0),
    )(*args)


def groups(side):
    out = []
    for x in range(side, SIZES[0] + side, 2):
        for y in range(side, SIZES[1] + side, 2):
            for z in range(side, SIZES[2] + side, 2):
                out.append([(((x + a) % SIZES[0]) * SIZES[1] + (y + b) % SIZES[1]) * SIZES[2] + (z + c) % SIZES[2]
                            for a in range(2) for b in range(2) for c in range(2)])
    return out


def trade(chunks, side):
    return lax.all_to_all(chunks, AXES, 0, 0, axis_index_groups=groups(side), tiled=True)


def local(positions, velocities, forces, species, cell_ids, centers, neighbours,
          w_embed, w_mix, w_value, w_env, w_latent, w_head, w_energy):
    table_shape = shape(ROWS, 8, 128)
    sums, fars = shape(8, SUM_ROWS, 128), shape(8, FAR_ROWS, 128)
    int_tile, flat = shape(8, 128, kind=i32), shape(4, 128, kind=i32)
    scratch = [pltpu.VMEM(v, f32) for v in ALL_SCRATCH.values()]

    cen, energy = centers.reshape(1, NB), w_energy.reshape(1, C)
    chunks, mid, cid, own = call(
        start_kernel, [shape(8, FIRST, 8, 128), shape(9, 8, 128), shape(16, 128, kind=i32), shape(8, ATOMS)],
        jnp.concatenate([positions, velocities, forces], 0), species.reshape(1, ATOMS), cell_ids, cen, energy,
        scratch=[pltpu.VMEM((128, 128), i32)])
    got = trade(chunks, 0)
    weight_shapes = [shape(m, k, kind=bf16) for m, k in (
        (C, 48), (C, 192), (384, 192), (C, 768), (C, 192), (C, 192), (256, 192), (C, 1152), (C, 192), (16, 192))]
    part, chunks, *prepared = call(
        second_kernel, [shape(16, 8, 128), shape(8, FIRST, 8, 128), int_tile, int_tile, shape(8, 128), int_tile, int_tile, flat, flat]
        + weight_shapes + [shape(C, 128)], got, mid, neighbours, cen, cid, w_embed.T, w_mix, w_value[0].T, w_env[0].T,
        w_latent[0], w_head, energy)
    idx, (irow, ilane), weights = prepared[:5], prepared[5:7], prepared[7:]
    got = trade(chunks, 1)
    table, force, base, chunks = call(
        first_pairs, [table_shape, table_shape, shape(9, 8, 128), sums], part, got, *idx, *weights, scratch=scratch, limit=24 << 20, flops=1 << 30)
    force, chunks = call(sum_kernel, [table_shape, sums], force, base, trade(chunks, 1))
    total, force, chunks = call(
        next_pairs, [shape(9, 8, 128), table_shape, fars], force, trade(chunks, 0), table, *idx, *weights, scratch=scratch,
        limit=24 << 20, flops=1 << 30)
    force, chunks = call(far_kernel, [table_shape, fars], force, trade(chunks, 0))
    return call(end_kernel, [shape(3, ATOMS)] * 3, force, trade(chunks, 1), total, irow, ilane, own,
                scratch=[pltpu.VMEM((9, 8, 128), f32)])


def solution(mesh):
    from jax.sharding import PartitionSpec as P

    rows = P(None, AXES)
    in_specs = (rows, rows, rows, P(AXES), P(*AXES, None), P(AXES), P(AXES, None)) + (P(),) * 7
    return jax.shard_map(local, mesh=mesh, in_specs=in_specs, out_specs=(rows, rows, rows), check_vma=False)
```

```python
import math
import jax, jax.numpy as jnp
from jax import lax
from jax.experimental import pallas as pl
from jax.experimental.pallas import tpu as pltpu

f32, bf16, i32 = jnp.float32, jnp.bfloat16, jnp.int32
NB, BLK, C = 8, 128, 64
PAIRS = NB * BLK
PARTS = NB // 2
WIDE = 2 * BLK
R3, R5, R15 = math.sqrt(3.0), math.sqrt(5.0), math.sqrt(15.0)


def nt(a, b):
    return lax.dot_general(a, b, (((1,), (1,)), ((), ())), preferred_element_type=f32)


def nn(a, b):
    return jnp.dot(a, b, preferred_element_type=f32)


def split(x):
    hi = x.astype(bf16)
    return hi, (x - hi.astype(f32)).astype(bf16)


def stack3(x):
    hi, lo = split(x)
    return jnp.concatenate([hi, lo, hi], 0)


def sigmoid(z):
    return 0.5 * jnp.tanh(0.5 * z) + 0.5


def harmonic_rows(ux, uy, uz):
    return [jnp.ones_like(ux), R3 * ux, R3 * uy, R3 * uz, R15 * ux * uy, R15 * uy * uz,
            0.5 * R5 * (3.0 * uz * uz - 1.0), R15 * ux * uz, 0.5 * R15 * (ux * ux - uy * uy)]


def pair_grads(disp, kc, kn, live, w, s):
    dx, dy, dz = disp
    r = jnp.sqrt(dx * dx + dy * dy + dz * dz + 0.09)
    rinv = 1.0 / r
    ux, uy, uz = dx * rinv, dy * rinv, dz * rinv
    q = jnp.minimum(r * (1.0 / 6.0), 1.0)
    q2 = q * q
    q4 = q2 * q2
    q5 = q4 * q
    q6 = q4 * q2
    f = (1.0 - 28.0 * q6 + 48.0 * (q6 * q) - 21.0 * (q6 * q2)) * live
    fp = -28.0 * q5 * (1.0 - q) * (1.0 - q) * live
    theta = math.pi * q
    s1, c1 = jnp.sin(theta), jnp.cos(theta)
    sm, cm = s1, c1
    norm = math.sqrt(1.0 / 3.0)
    rn = norm * rinv
    slopes = []
    for m in range(8):
        s["feat"][m] = sm * rn
        slopes.append((cm * (math.pi / 6.0 * (m + 1)) - sm * rinv) * rn)
        sm, cm = sm * c1 + cm * s1, cm * c1 - sm * s1
    ys = harmonic_rows(ux, uy, uz)
    for n in range(9):
        s["harm"][n] = ys[n]
    for n in range(9, 16):
        s["harm"][n] = jnp.zeros((8, 128), f32)
    s["sc"][0] = f
    s["sc"][1] = kc
    s["sc"][2] = kn

    parts = range(PARTS)
    sub8 = lax.broadcasted_iota(i32, (8, BLK), 0).astype(f32)

    def features(b):
        hot = jnp.where(sub8 < 4.0, jnp.broadcast_to(s["sc"][1, b:b + 1, :], (8, BLK)),
                        jnp.broadcast_to(s["sc"][2, b:b + 1, :], (8, BLK)) + 4.0) == sub8
        return jnp.concatenate([s["feat"][:, b, :], hot.astype(f32)], 0)

    def envelope(j):
        return jnp.concatenate([s["sc"][0, b:b + 1, :] for b in (2 * j, 2 * j + 1)], 1)

    fw = [envelope(j) for j in parts]
    d1, d2, d3, a, x, sums, t = ([None] * PARTS for _ in range(7))
    h = [None] * PARTS
    for j in parts:
        feat = jnp.concatenate([features(2 * j), features(2 * j + 1)], 1)
        z = nn(w["emb"][...], stack3(feat))
        g = sigmoid(z)
        h[j] = z * g
        d1[j] = g + h[j] * (1.0 - g)
    for j in parts:
        z = nn(w["mix"][...], stack3(h[j]))
        g = sigmoid(z)
        a[j] = z * g
        d2[j] = g + a[j] * (1.0 - g)
        x[j] = a[j] * fw[j]
    for j in parts:
        s["vw"][j] = nn(w["ve"][...], stack3(x[j]))

    zero = jnp.zeros((16, BLK), f32)
    bd3, rep = [], []
    for j in parts:
        y0, y1 = s["harm"][:, 2 * j, :], s["harm"][:, 2 * j + 1, :]
        bd = jnp.concatenate([jnp.concatenate([y0, zero], 1), jnp.concatenate([zero, y1], 1)], 0)
        hi, lo = split(bd)
        none = jnp.zeros((32, WIDE), bf16)
        bd3.append(jnp.concatenate([hi, lo, hi, none], 0))
        rep.append(jnp.concatenate([hi, hi, hi, none, lo, lo, lo, none], 0))

    row = lax.broadcasted_iota(i32, (192, 128), 0) // C
    col = lax.broadcasted_iota(i32, (192, 128), 1)
    part = col % 16
    order = jnp.where(part == 0, 0, jnp.where(part < 4, 1, jnp.where(part < 9, 2, 3)))
    mask = jnp.where(row == order, 0.1, 0.0).astype(f32)

    def moments(val, j):
        out = nt(jnp.concatenate(split(val), 0), rep[j])
        return (out[0:192, 0:128] + out[192:384, 0:128] + out[0:192, 128:256]) * mask

    def sharp(m):
        hi, lo = split(m)
        return jnp.where(col < 64, hi.astype(f32), lo.astype(f32)).astype(bf16)

    for j in parts:
        sums[j] = moments(s["vw"][j, 192:384, :], j)
    for j in parts:
        s["t"][j] = nn(sharp(sums[j]), bd3[j])
    bb, x2 = [None] * PARTS, [None] * PARTS
    for j in parts:
        sc = s["vw"][j, 0:192, :] * s["t"][j]
        z = nn(w["lat"][...], stack3(jnp.concatenate([x[j], sc], 0)))
        g = sigmoid(z)
        bb[j] = z * g
        d3[j] = g + bb[j] * (1.0 - g)
        x2[j] = x[j] + bb[j] * fw[j]
    wen = jnp.concatenate([w["energy"][...]] * 2, 1)
    df, dx2, dxa = ([None] * PARTS for _ in range(3))
    dz = [None] * PARTS
    for j in parts:
        z = nn(w["head"][...], stack3(x2[j]))
        g = sigmoid(z)
        hh = z * g
        df[j] = jnp.sum(wen * hh, 0, keepdims=True)
        dz[j] = wen * fw[j] * (g + hh * (1.0 - g))
    for j in parts:
        dx2[j] = nn(w["head_t"][...], stack3(dz[j]))
        df[j] = df[j] + jnp.sum(dx2[j] * bb[j], 0, keepdims=True)
        dz[j] = dx2[j] * fw[j] * d3[j]
    for j in parts:
        dc = nn(w["lat_t"][...], stack3(dz[j]))
        dxa[j] = dx2[j] + dc[0:64]
        ds = dc[64:256]
        s["dv"][j] = ds * s["t"][j]
        s["dt"][j] = ds * s["vw"][j, 0:192, :]
    m = [None] * PARTS
    for j in parts:
        m[j] = moments(s["dt"][j], j)
    for j in parts:
        s["dw"][j] = nn(sharp(m[j]), bd3[j])
    for j in parts:
        acc = None
        for left, right in ((sums[j], s["dt"][j]), (m[j], s["vw"][j, 192:384, :])):
            lt = jnp.transpose(left)[0:32]
            lh, ll = split(lt)
            rh, rl = split(right)
            both = nn(jnp.concatenate([lh, ll], 0), rh)
            one = both[0:32] + both[32:64] + nn(lh, rl)
            acc = one if acc is None else acc + one
        s["dy"][2 * j] = acc[0:16, 0:128]
        s["dy"][2 * j + 1] = acc[16:32, 128:256]
    for j in parts:
        dx = dxa[j] + nn(w["ve_t"][...], stack3(jnp.concatenate([s["dv"][j], s["dw"][j]], 0)))
        df[j] = df[j] + jnp.sum(dx * a[j], 0, keepdims=True)
        dz[j] = dx * fw[j] * d2[j]
        for k in range(2):
            s["sc"][3, 2 * j + k:2 * j + k + 1, :] = df[j][:, 128 * k:128 * k + 128]
    for j in parts:
        dz[j] = nn(w["mix_t"][...], stack3(dz[j])) * d1[j]
    for j in parts:
        dr8 = nn(w["emb_t"][...], stack3(dz[j]))
        for k in range(2):
            s["dr"][2 * j + k] = dr8[0:8, 128 * k:128 * k + 128]

    dr = s["sc"][3] * fp
    for k in range(8):
        dr = dr + s["dr"][:, k, :] * slopes[k]
    gy = [s["dy"][:, n, :] for n in range(9)]
    dux = R3 * gy[1] + R15 * (uy * gy[4] + uz * gy[7] + ux * gy[8])
    duy = R3 * gy[2] + R15 * (ux * gy[4] + uz * gy[5] - uy * gy[8])
    duz = R3 * gy[3] + R15 * (uy * gy[5] + ux * gy[7]) + (3.0 * R5) * uz * gy[6]
    dot = dux * ux + duy * uy + duz * uz
    along = dr - dot * rinv
    scale = 50.0
    return [scale * (du * rinv + along * u) for du, u in ((dux, ux), (duy, uy), (duz, uz))]


PAIR_SCRATCH = {
    "feat": (8, 8, 128), "harm": (16, 8, 128), "sc": (4, 8, 128), "vw": (PARTS, 384, WIDE), "t": (PARTS, 192, WIDE),
    "dv": (PARTS, 192, WIDE), "dt": (PARTS, 192, WIDE), "dw": (PARTS, 192, WIDE), "dy": (8, 16, 128), "dr": (8, 8, 128),
}
WEIGHT_NAMES = ("emb", "mix", "ve", "lat", "head", "head_t", "lat_t", "ve_t", "mix_t", "emb_t", "energy")


SIDE = 8
ATOMS = SIDE ** 3
ROWS = 25
STEP = 0.1
MASSES = (1.008, 15.999, 22.99, 35.453)
ZLANE = (0, 27, 54, 72, 99)
WIDTHS = (3, 2, 3)
EDGE = 2.0 * SIDE
TILE = (8, 128)
MIDDLE = [5 * x + y for x in (1, 2, 3) for y in (1, 2, 3)]
AXES = ("gx", "gy", "gz")
SIZES = (16, 8, 8)
FIRST = 2
SUM_ROWS, FAR_ROWS = 40, 16


def iota(dim, shape=TILE):
    return lax.broadcasted_iota(i32, shape, dim)


def lane_take(row, idx):
    return jnp.take_along_axis(row, idx, axis=1)


def roll_rows(v, shift):
    return v if shift % 8 == 0 else pltpu.roll(v, shift % 8, 0)


def roll_lanes(v, shift):
    return v if shift % 128 == 0 else pltpu.roll(v, shift % 128, 1)


def inverse_mass(kind):
    out = jnp.full(kind.shape, 1.0 / MASSES[3], f32)
    for k in range(3):
        out = jnp.where(kind == float(k), 1.0 / MASSES[k], out)
    return out


def masses(kind):
    out = jnp.full(kind.shape, MASSES[3], f32)
    for k in range(3):
        out = jnp.where(kind == float(k), MASSES[k], out)
    return out


def parity():
    return [lax.axis_index(a) & 1 for a in AXES]


def place_in(side):
    p = parity()
    return (p[0] * 4 + p[1] * 2 + p[2]) ^ (7 if side else 0)


def pack4(rows, start):
    lane = iota(1)
    out = []
    for k in range(0, len(rows), 4):
        v = roll_lanes(rows[k], -start)
        for p in range(1, len(rows[k:k + 4])):
            v = jnp.where(lane >= 32 * p, roll_lanes(rows[k + p], 32 * p - start), v)
        out.append(v)
    return out


def doubled(tiles):
    sub = iota(0)
    return [jnp.where(sub < 4, tiles[k], roll_rows(tiles[k + 1], 4)) if k + 1 < len(tiles) else tiles[k] for k in range(0, len(tiles), 2)]


def start_kernel(given, spec, cells, chunks, mid, cid, own, raw):
    px, py, pz = parity()
    raw[...] = jnp.zeros((128, 128), i32)
    kind = spec[...].astype(f32)
    kick = given[3:6, :] + (0.5 * STEP) * given[6:9, :] * inverse_mass(kind)
    own[0:3, :] = given[0:3, :] + STEP * kick
    own[3:4, :] = kind
    own[4:7, :] = kick
    own[7:8, :] = jnp.zeros_like(kind)
    for x in range(3):
        for y in range(3):
            at = 8 * (3 * x + y)
            raw[at:at + 3, 0:27] = cells[x + px * (2 - 2 * x), y + py * (2 - 2 * y)]
    z0, z1, z2 = (raw[pl.ds(k, 16, stride=8), :] for k in range(3))
    lane = iota(1, (16, 128))
    flip = jnp.full((16, 128), pz, i32) == 1
    ids = jnp.where(lane < ZLANE[2], pltpu.roll(jnp.where(flip, z2, z0), ZLANE[1], 1),
                    jnp.where(lane < ZLANE[3], pltpu.roll(z1, ZLANE[2], 1), pltpu.roll(jnp.where(flip, z0, z2), ZLANE[3], 1)))
    cid[...] = jnp.where((lane >= ZLANE[1]) & (lane < ZLANE[4]), ids, 0)
    cuts = [own[:, 128 * h:128 * h + 128] for h in range(4)]
    rows = []
    for r in range(9):
        ids = jnp.broadcast_to(cid[r:r + 1, :], TILE)
        lo, hi = ids & 127, ids >> 7
        acc = lane_take(cuts[0], lo)
        for h in range(1, 4):
            acc = jnp.where(hi == h, lane_take(cuts[h], lo), acc)
        mid[r] = acc
        rows.append(acc)
    me = place_in(0)
    zs = ZLANE[3]
    for d, tiles in ((4, rows[6:9]), (2, rows[2::3]), (6, rows[8:9]), (1, pack4(rows, zs)), (5, pack4(rows[6:9], zs)),
                     (3, pack4(rows[2::3], zs)), (7, pack4(rows[8:9], zs))):
        for k, v in enumerate(doubled(tiles)):
            chunks[me ^ d, k] = v


def widen(have, got, me, face):
    lane = iota(1)
    beyond = (lambda: lane >= ZLANE[4]) if face else (lambda: lane < ZLANE[1])
    at = ZLANE[face]
    xs = sorted({x for x, _ in have})
    rows = sorted(have)

    def half(d, n):
        return roll_rows(got[me ^ d, n // 2], -4 * (n % 2))

    def strip(d, keys, base):
        out = {}
        for n, key in enumerate(keys):
            v = roll_lanes(half(d, n // 4), at - 32 * (n % 4))
            out[key] = jnp.where(beyond(), v, base[key])
        return out

    new = strip(1, rows, have)
    new.update(strip(5, [(face, y) for y in xs], {(face, y): half(4, n) for n, y in enumerate(xs)}))
    new.update(strip(3, [(x, face) for x in xs], {(x, face): half(2, n) for n, x in enumerate(xs)}))
    new.update(strip(7, [(face, face)], {(face, face): half(6, 0)}))
    return new


def second_kernel(got, mid, table, chunks):
    have = {(r // 3 + 1, r % 3 + 1): mid[r] for r in range(9)}
    have = widen(have, got, place_in(0), 4)
    for (x, y), v in have.items():
        table[4 * (x - 1) + y - 1] = v
    me = place_in(1)
    zs = ZLANE[1]
    along_x = [have[1, y] for y in range(1, 5)]
    along_y = [have[x, 1] for x in range(1, 5)]
    whole = [have[x, y] for x in range(1, 5) for y in range(1, 5)]
    for d, tiles in ((4, along_x), (2, along_y), (6, along_x[:1]), (1, pack4(whole, zs)), (5, pack4(along_x, zs)),
                     (3, pack4(along_y, zs)), (7, pack4(along_x[:1], zs))):
        for k, v in enumerate(doubled(tiles)):
            chunks[me ^ d, k] = v


def prepare(neigh, cen, cid, emb, mix, val, env, lat, head, energy, nrow, nlane, live, crow, clane, irow, ilane, *out):
    sub, lane = iota(0), iota(1)
    big = iota(0, (128, 128))
    left, right = [], []
    for r in range(9):
        area = WIDTHS[r // 3] * WIDTHS[r % 3]
        ids = jnp.broadcast_to(cid[r:r + 1, :], TILE)
        valid = (lane >= 27) & (lane < 27 + 3 * area)
        valid = valid | ((lane >= 54) & (lane < 54 + 2 * area))
        valid = valid | ((lane >= 72) & (lane < 72 + 3 * area))
        row = (r // 3 + 1) * 5 + r % 3 + 1
        value = jnp.where((sub & 1) == 0, row, lane)
        left.append(jnp.where(valid & ((ids >> 7) == (sub >> 1)), value, 0).astype(f32).astype(bf16))
        lo = jnp.broadcast_to(cid[r:r + 1, :], (128, 128)) & 127
        right.append(jnp.where(big == lo, 1.0, 0.0).astype(bf16))
    inv = nt(jnp.concatenate(left, 1), jnp.concatenate(right, 1))
    inv = (inv + 0.5).astype(i32)
    for h in range(4):
        irow[h:h + 1, :] = inv[2 * h:2 * h + 1, :]
        ilane[h:h + 1, :] = inv[2 * h + 1:2 * h + 2, :]
    px, py, pz = parity()

    def flip(e, p):
        return e + p * (4 - 2 * e)

    def place(n):
        lo, hi = n & 127, n >> 7
        row = jnp.zeros(TILE, i32)
        col = jnp.zeros(TILE, i32)
        for h in range(4):
            row = jnp.where(hi == h, lane_take(jnp.broadcast_to(irow[h:h + 1, :], TILE), lo), row)
            col = jnp.where(hi == h, lane_take(jnp.broadcast_to(ilane[h:h + 1, :], TILE), lo), col)
        m = jnp.maximum(n - ATOMS, 0)
        grow = ((m.astype(f32) + 0.5) * (1.0 / 135.0)).astype(i32)
        rem = m - 135 * grow
        ex = ((grow.astype(f32) + 0.5) * 0.2).astype(i32)
        ey = grow - 5 * ex
        ez = ((rem.astype(f32) + 0.5) * (1.0 / 27.0)).astype(i32)
        slot = rem - 27 * ez
        ex, ey, ez = flip(ex, px), flip(ey, py), flip(ez, pz)
        first = jnp.where(ez == 0, 0, jnp.where(ez == 1, 27, jnp.where(ez == 2, 54, jnp.where(ez == 3, 72, 99))))
        return jnp.where(hi < 4, row, 5 * ex + ey), jnp.where(hi < 4, col, first + slot)

    n = neigh[...]
    c = jnp.concatenate([cen[...].astype(f32), jnp.zeros((1, 120), f32)], 1)
    c = jnp.sum(jnp.where(lane == sub, jnp.broadcast_to(c, TILE), 0.0), 1, keepdims=True)
    c = (jnp.broadcast_to(c, TILE) + 0.5).astype(i32)
    nrow[...], nlane[...] = place(n)
    crow[...], clane[...] = place(c)
    live[...] = jnp.where(n != c, 1.0, 0.0)

    def stack(w):
        hi = w.astype(bf16).astype(f32)
        return jnp.concatenate([hi, hi, w - hi], 1).astype(bf16)

    ve_t = jnp.concatenate([val[...], env[...]], 1)
    emb_t = jnp.concatenate([emb[0:8, :], jnp.zeros((8, C), f32)], 0)
    wide_energy = jnp.broadcast_to(energy[...], (128, C))
    tiles = (stack(emb[...].T), stack(mix[...]), stack(ve_t.T), stack(lat[...]), stack(head[...]), stack(head[...].T),
             stack(lat[...].T), stack(ve_t), stack(mix[...].T), stack(emb_t), wide_energy.T)
    for ref, v in zip(out, tiles):
        ref[...] = v


def pair_step(tab, nrow, nlane, live, crow, clane, w, s, force):
    sub, lane = iota(0), iota(1)
    px, py, pz = (1.0 - 2.0 * p.astype(f32) for p in parity())
    zshift = jnp.where(lane < ZLANE[1], -EDGE, jnp.where(lane >= ZLANE[4], EDGE, 0.0)) * pz
    zshift = jnp.where(sub == 2, zshift, 0.0)
    xshift = jnp.where(sub == 0, EDGE, 0.0) * px
    yshift = jnp.where(sub == 1, EDGE, 0.0) * py
    nr, nl, cr, cl = nrow[...], nlane[...], crow[...], clane[...]
    near = [jnp.zeros(TILE, f32) for _ in range(4)]
    centre = [jnp.zeros(TILE, f32) for _ in range(4)]
    for r in range(ROWS):
        ex, ey = r // 5, r % 5
        shift = zshift
        if ex in (0, 4):
            shift = shift + xshift * float(ex // 2 - 1)
        if ey in (0, 4):
            shift = shift + yshift * float(ey // 2 - 1)
        s["shifted"][r] = tab(ex, ey) + shift
        mine = nr == r
        centred = cr == r
        for q in range(4):
            line = jnp.broadcast_to(s["shifted"][r, q:q + 1, :], TILE)
            near[q] = jnp.where(mine, lane_take(line, nl), near[q])
            if ex in (1, 2, 3) and ey in (1, 2, 3):
                centre[q] = jnp.where(centred, lane_take(line, cl), centre[q])
    alive = live[...]
    disp = [near[k] - centre[k] for k in range(3)]
    grads = pair_grads(disp, centre[3], near[3], alive, w, s)
    spare = 1.0 / jnp.sum(1.0 - alive, 1, keepdims=True)
    for k, g in enumerate(grads):
        g = jnp.where(alive > 0.0, -g, jnp.sum(g, 1, keepdims=True) * spare)
        hi = g.astype(bf16).astype(f32)
        s["spread"][k] = hi
        s["spread"][k + 3] = g - hi
    s["spread"][6] = jnp.zeros(TILE, f32)
    s["spread"][7] = jnp.zeros(TILE, f32)
    big = iota(0, (128, 128))
    left, right = [], []
    for b in range(NB):
        g = s["spread"][:, b, :]
        rows = jnp.broadcast_to(nrow[b:b + 1, :], TILE)
        left.append(jnp.concatenate([jnp.where(rows == r, g, 0.0) for r in range(ROWS)], 0).astype(bf16))
        right.append(jnp.where(big == jnp.broadcast_to(nlane[b:b + 1, :], (128, 128)), 1.0, 0.0).astype(bf16))
    out = nt(jnp.concatenate(left, 1), jnp.concatenate(right, 1))
    for r in range(ROWS):
        v = out[8 * r:8 * r + 8]
        force[r] = jnp.where(sub < 3, v + roll_rows(v, -3), 0.0)


def far_rows(side):
    far = 0 if side else 4
    rest = (1, 2, 3) if side else (0, 1, 2, 3)
    return [5 * far + y for y in rest], [5 * x + far for x in rest], [5 * x + y for x in rest for y in rest], [5 * far + far]


def put(chunks, d, values):
    for m, v in enumerate(values):
        chunks[d, 3 * m:3 * m + 3, :] = v[0:3]


def strips4(rows, at):
    return pack4(rows, at)


def strips2(rows, head, tail):
    lane = iota(1)
    out = []
    for k in range(0, len(rows), 2):
        v = None
        for n, q in enumerate(rows[k:k + 2]):
            t = jnp.where(lane < 64 * n + 27, roll_lanes(q, 64 * n - head), roll_lanes(q, 64 * n + 27 - tail))
            v = t if v is None else jnp.where(lane >= 64, t, v)
        out.append(v)
    return out


def sum_messages(force, base, chunks, side):
    me = place_in(side)
    near, far = (1, 0) if side else (3, 4)
    head, tail = (ZLANE[near], ZLANE[far]) if side else (ZLANE[far], ZLANE[near])
    f = [force[r] for r in range(ROWS)]
    for k, r in enumerate(MIDDLE):
        f[r] = f[r] + base[k]
    xs = [f[5 * x + y] for x in (far, near) for y in range(5)]
    ys = [f[5 * x + y] for y in (far, near) for x in range(5)]
    corner = [f[5 * x + y] for x in (far, near) for y in (far, near)]
    for d, tiles in ((4, xs), (2, ys), (6, corner), (1, strips2(f, head, tail)), (5, strips2(xs, head, tail)),
                     (3, strips2(ys, head, tail)), (7, strips2(corner, head, tail))):
        put(chunks, me ^ d, tiles)


def add_messages(force, got, side):
    lane = iota(1, (3, 128))
    me = place_in(side)
    near, far = (1, 0) if side else (3, 4)
    inside = lane >= ZLANE[3] if side == 0 else lane < ZLANE[2]
    first = min(ZLANE[near], ZLANE[far])
    out = {r: force[r, 0:3, :] for r in range(ROWS)}
    xs = [5 * x + y for x in (near, far) for y in range(5)]
    ys = [5 * x + y for y in (near, far) for x in range(5)]
    corner = [5 * x + y for x in (near, far) for y in (near, far)]
    for d, rows in ((4, xs), (2, ys), (6, corner)):
        for m, r in enumerate(rows):
            out[r] = out[r] + got[me ^ d, 3 * m:3 * m + 3, :]
    for d, rows in ((1, list(range(ROWS))), (5, xs), (3, ys), (7, corner)):
        for n, r in enumerate(rows):
            v = got[me ^ d, 3 * (n // 2):3 * (n // 2) + 3, :]
            out[r] = out[r] + jnp.where(inside, roll_lanes(v, first - 64 * (n % 2)), 0.0)
    return out


def far_messages(force, chunks, side):
    me = place_in(side)
    at = ZLANE[0 if side else 4]
    xs, ys, whole, corner = ([force[r] for r in rows] for rows in far_rows(side))
    for d, tiles in ((4, xs), (2, ys), (6, corner), (1, strips4(whole, at)), (5, strips4(xs, at)), (3, strips4(ys, at)),
                     (7, strips4(corner, at))):
        put(chunks, me ^ d, tiles)


def add_far(force, got, side):
    lane = iota(1, (3, 128))
    me = place_in(side)
    near, far = (1, 0) if side else (3, 4)
    at = ZLANE[near]
    inside = (lane >= at) & (lane < at + 27)
    xs, ys, whole, corner = far_rows(side)
    out = {r: force[r, 0:3, :] for r in whole}
    xs = [r + 5 * (near - far) for r in xs]
    ys = [r + near - far for r in ys]
    corner = [5 * near + near]
    for d, rows in ((4, xs), (2, ys), (6, corner)):
        for m, r in enumerate(rows):
            out[r] = out[r] + got[me ^ d, 3 * m:3 * m + 3, :]
    for d, rows in ((1, whole), (5, xs), (3, ys), (7, corner)):
        for n, r in enumerate(rows):
            v = got[me ^ d, 3 * (n // 4):3 * (n // 4) + 3, :]
            out[r] = out[r] + jnp.where(inside, roll_lanes(v, at - 32 * (n % 4)), 0.0)
    return out


def weight_refs(refs):
    return dict(zip(WEIGHT_NAMES, refs))


def first_pairs(part, got, *refs):
    tab, force, base, chunks = refs[10:14]
    prepare(*refs[:10], *refs[14:32])
    nrow, nlane, live, crow, clane = refs[14:19]
    w = weight_refs(refs[21:32])
    s = dict(zip(ALL_SCRATCH, refs[32:]))
    have = {(x, y): part[4 * (x - 1) + y - 1] for x in range(1, 5) for y in range(1, 5)}
    for (x, y), v in widen(have, got, place_in(1), 0).items():
        tab[5 * x + y] = v
    pair_step(lambda x, y: tab[5 * x + y], nrow, nlane, live, crow, clane, w, s, force)
    sub, lane = iota(0), iota(1)
    mine = (sub < 3) & (lane >= ZLANE[1]) & (lane < ZLANE[4])
    for k, r in enumerate(MIDDLE):
        v = tab[r]
        rest = (v + STEP * roll_rows(v, -4)) * (1.0 / (STEP * STEP)) * masses(jnp.broadcast_to(tab[r, 3:4, :], TILE))
        base[k] = jnp.where(mine, rest, 0.0)
    sum_messages(force, base, chunks, 1)


def next_pairs(force, got, table, nrow, nlane, live, crow, clane, *refs):
    w = weight_refs(refs[:11])
    total, force2, chunks = refs[11:14]
    s = dict(zip(ALL_SCRATCH, refs[14:]))
    lane = iota(1, (3, 128))
    mine = (lane >= ZLANE[1]) & (lane < ZLANE[4])
    for r, f in add_messages(force, got, 0).items():
        mass = inverse_mass(jnp.broadcast_to(table[r, 3:4, :], (3, 128)))
        moved = (STEP * STEP) * f * mass
        if r in MIDDLE:
            total[MIDDLE.index(r), 0:3, :] = f
            half = (0.5 * STEP) * f * mass
            kick = table[r, 4:7, :] + half + half
            moved = jnp.where(mine, table[r, 0:3, :] + STEP * kick, moved)
        s["table"][r] = table[r]
        s["table"][r, 0:3, :] = moved
    pair_step(lambda x, y: s["table"][5 * x + y], nrow, nlane, live, crow, clane, w, s, force2)
    far_messages(force2, chunks, 0)


def sum_kernel(force, base, got, out, chunks):
    for r, v in add_messages(force, got, 1).items():
        out[r, 0:3, :] = v
    sum_messages(out, base, chunks, 0)


def far_kernel(force, got, out, chunks):
    for r, v in add_far(force, got, 0).items():
        out[r, 0:3, :] = v
    far_messages(out, chunks, 1)


def end_kernel(force, got, total, irow, ilane, own, new_pos, new_vel, new_frc, both):
    summed = add_far(force, got, 1)
    for k, r in enumerate(MIDDLE):
        both[k, 0:3, :] = summed[r]
        both[k, 3:6, :] = total[k, 0:3, :]
        both[k, 6:8, :] = jnp.zeros((2, 128), f32)
    mass = inverse_mass(own[3:4, :])
    for h in range(4):
        lanes = slice(128 * h, 128 * h + 128)
        ir = jnp.broadcast_to(irow[h:h + 1, :], TILE)
        il = jnp.broadcast_to(ilane[h:h + 1, :], TILE)
        acc = jnp.zeros(TILE, f32)
        for k, r in enumerate(MIDDLE):
            acc = jnp.where(ir == r, lane_take(both[k], il), acc)
        last, first = acc[0:3], acc[3:6]
        m = mass[:, lanes]
        half = (0.5 * STEP) * first * m
        kick = own[4:7, lanes] + half + half
        new_pos[:, lanes] = own[0:3, lanes] + STEP * kick
        new_vel[:, lanes] = kick + (0.5 * STEP) * last * m
        new_frc[:, lanes] = last


ALL_SCRATCH = dict(PAIR_SCRATCH, shifted=(ROWS, 8, 128), table=(ROWS, 8, 128), spread=(8, 8, 128))


def shape(*dims, kind=f32):
    return jax.ShapeDtypeStruct(dims, kind)


def call(kernel, outs, *args, scratch=(), limit=4 << 20, flops=1 << 20, space=pltpu.VMEM):
    vm = pl.BlockSpec(memory_space=pltpu.VMEM)
    return pl.pallas_call(
        kernel,
        out_shape=tuple(outs),
        in_specs=[pl.BlockSpec(memory_space=space)] * len(args),
        out_specs=tuple([vm] * len(outs)),
        scratch_shapes=list(scratch),
        compiler_params=pltpu.CompilerParams(vmem_limit_bytes=limit),
        cost_estimate=pl.CostEstimate(flops=flops, bytes_accessed=1 << 18, transcendentals=0),
    )(*args)


def groups(side):
    out = []
    for x in range(side, SIZES[0] + side, 2):
        for y in range(side, SIZES[1] + side, 2):
            for z in range(side, SIZES[2] + side, 2):
                out.append([(((x + a) % SIZES[0]) * SIZES[1] + (y + b) % SIZES[1]) * SIZES[2] + (z + c) % SIZES[2]
                            for a in range(2) for b in range(2) for c in range(2)])
    return out


def trade(chunks, side):
    return lax.all_to_all(chunks, AXES, 0, 0, axis_index_groups=groups(side), tiled=True)


def local(positions, velocities, forces, species, cell_ids, centers, neighbours,
          w_embed, w_mix, w_value, w_env, w_latent, w_head, w_energy):
    table_shape = shape(ROWS, 8, 128)
    sums, fars = shape(8, SUM_ROWS, 128), shape(8, FAR_ROWS, 128)
    int_tile, flat = shape(8, 128, kind=i32), shape(4, 128, kind=i32)
    scratch = [pltpu.VMEM(v, f32) for v in ALL_SCRATCH.values()]

    chunks, mid, cid, own = call(
        start_kernel, [shape(8, FIRST, 8, 128), shape(9, 8, 128), shape(16, 128, kind=i32), shape(8, ATOMS)],
        jnp.concatenate([positions, velocities, forces], 0), species.reshape(1, ATOMS), cell_ids,
        scratch=[pltpu.VMEM((128, 128), i32)])
    got = trade(chunks, 0)
    weight_shapes = [shape(m, k, kind=bf16) for m, k in (
        (C, 48), (C, 192), (384, 192), (C, 768), (C, 192), (C, 192), (256, 192), (C, 1152), (C, 192), (16, 192))]
    part, chunks = call(second_kernel, [shape(16, 8, 128), shape(8, FIRST, 8, 128)], got, mid)
    got = trade(chunks, 1)
    indices = [int_tile, int_tile, shape(8, 128), int_tile, int_tile, flat, flat]
    table, force, base, chunks, *prepared = call(
        first_pairs, [table_shape, table_shape, shape(9, 8, 128), sums] + indices + weight_shapes + [shape(C, 128)],
        part, got, neighbours, centers.reshape(1, NB), cid, w_embed.T, w_mix, w_value[0].T, w_env[0].T, w_latent[0], w_head,
        w_energy.reshape(1, C), scratch=scratch, limit=24 << 20, flops=1 << 30)
    idx, (irow, ilane), weights = prepared[:5], prepared[5:7], prepared[7:]
    force, chunks = call(sum_kernel, [table_shape, sums], force, base, trade(chunks, 1))
    total, force, chunks = call(
        next_pairs, [shape(9, 8, 128), table_shape, fars], force, trade(chunks, 0), table, *idx, *weights, scratch=scratch,
        limit=24 << 20, flops=1 << 30)
    force, chunks = call(far_kernel, [table_shape, fars], force, trade(chunks, 0))
    return call(end_kernel, [shape(3, ATOMS)] * 3, force, trade(chunks, 1), total, irow, ilane, own,
                scratch=[pltpu.VMEM((9, 8, 128), f32)])


def solution(mesh):
    from jax.sharding import PartitionSpec as P

    rows = P(None, AXES)
    in_specs = (rows, rows, rows, P(AXES), P(*AXES, None), P(AXES), P(AXES, None)) + (P(),) * 7
    return jax.shard_map(local, mesh=mesh, in_specs=in_specs, out_specs=(rows, rows, rows), check_vma=False)
```

```python
import math
import jax, jax.numpy as jnp
from jax import lax
from jax.experimental import pallas as pl
from jax.experimental.pallas import tpu as pltpu

f32, bf16, i32 = jnp.float32, jnp.bfloat16, jnp.int32
NB, BLK, C = 8, 128, 64
PAIRS = NB * BLK
PARTS = NB // 2
WIDE = 2 * BLK
R3, R5, R15 = math.sqrt(3.0), math.sqrt(5.0), math.sqrt(15.0)


def nt(a, b):
    return lax.dot_general(a, b, (((1,), (1,)), ((), ())), preferred_element_type=f32)


def nn(a, b):
    return jnp.dot(a, b, preferred_element_type=f32)


def split(x):
    hi = x.astype(bf16)
    return hi, (x - hi.astype(f32)).astype(bf16)


def stack3(x):
    hi, lo = split(x)
    return jnp.concatenate([hi, lo, hi], 0)


def sigmoid(z):
    return 0.5 * jnp.tanh(0.5 * z) + 0.5


def harmonic_rows(ux, uy, uz):
    return [jnp.ones_like(ux), R3 * ux, R3 * uy, R3 * uz, R15 * ux * uy, R15 * uy * uz,
            0.5 * R5 * (3.0 * uz * uz - 1.0), R15 * ux * uz, 0.5 * R15 * (ux * ux - uy * uy)]


def pair_grads(disp, kc, kn, live, w, s):
    dx, dy, dz = disp
    r = jnp.sqrt(dx * dx + dy * dy + dz * dz + 0.09)
    rinv = 1.0 / r
    ux, uy, uz = dx * rinv, dy * rinv, dz * rinv
    q = jnp.minimum(r * (1.0 / 6.0), 1.0)
    q2 = q * q
    q4 = q2 * q2
    q5 = q4 * q
    q6 = q4 * q2
    f = (1.0 - 28.0 * q6 + 48.0 * (q6 * q) - 21.0 * (q6 * q2)) * live
    fp = -28.0 * q5 * (1.0 - q) * (1.0 - q) * live
    theta = math.pi * q
    s1, c1 = jnp.sin(theta), jnp.cos(theta)
    sm, cm = s1, c1
    norm = math.sqrt(1.0 / 3.0)
    rn = norm * rinv
    slopes = []
    for m in range(8):
        s["feat"][m] = sm * rn
        slopes.append((cm * (math.pi / 6.0 * (m + 1)) - sm * rinv) * rn)
        sm, cm = sm * c1 + cm * s1, cm * c1 - sm * s1
    ys = harmonic_rows(ux, uy, uz)
    for n in range(9):
        s["harm"][n] = ys[n]
    for n in range(9, 16):
        s["harm"][n] = jnp.zeros((8, 128), f32)
    s["sc"][0] = f
    s["sc"][1] = kc
    s["sc"][2] = kn

    parts = range(PARTS)
    sub8 = lax.broadcasted_iota(i32, (8, BLK), 0).astype(f32)

    def features(b):
        hot = jnp.where(sub8 < 4.0, jnp.broadcast_to(s["sc"][1, b:b + 1, :], (8, BLK)),
                        jnp.broadcast_to(s["sc"][2, b:b + 1, :], (8, BLK)) + 4.0) == sub8
        return jnp.concatenate([s["feat"][:, b, :], hot.astype(f32)], 0)

    def envelope(j):
        return jnp.concatenate([s["sc"][0, b:b + 1, :] for b in (2 * j, 2 * j + 1)], 1)

    fw = [envelope(j) for j in parts]
    d1, d2, d3, a, x, sums, t = ([None] * PARTS for _ in range(7))
    h = [None] * PARTS
    for j in parts:
        feat = jnp.concatenate([features(2 * j), features(2 * j + 1)], 1)
        z = nn(w["emb"][...], stack3(feat))
        g = sigmoid(z)
        h[j] = z * g
        d1[j] = g + h[j] * (1.0 - g)
    for j in parts:
        z = nn(w["mix"][...], stack3(h[j]))
        g = sigmoid(z)
        a[j] = z * g
        d2[j] = g + a[j] * (1.0 - g)
        x[j] = a[j] * fw[j]
    for j in parts:
        s["vw"][j] = nn(w["ve"][...], stack3(x[j]))

    zero = jnp.zeros((16, BLK), f32)
    bd3, rep = [], []
    for j in parts:
        y0, y1 = s["harm"][:, 2 * j, :], s["harm"][:, 2 * j + 1, :]
        bd = jnp.concatenate([jnp.concatenate([y0, zero], 1), jnp.concatenate([zero, y1], 1)], 0)
        hi, lo = split(bd)
        none = jnp.zeros((32, WIDE), bf16)
        bd3.append(jnp.concatenate([hi, lo, hi, none], 0))
        rep.append(jnp.concatenate([hi, hi, hi, none, lo, lo, lo, none], 0))

    row = lax.broadcasted_iota(i32, (192, 128), 0) // C
    col = lax.broadcasted_iota(i32, (192, 128), 1)
    part = col % 16
    order = jnp.where(part == 0, 0, jnp.where(part < 4, 1, jnp.where(part < 9, 2, 3)))
    mask = jnp.where(row == order, 0.1, 0.0).astype(f32)

    def moments(val, j):
        out = nt(jnp.concatenate(split(val), 0), rep[j])
        return (out[0:192, 0:128] + out[192:384, 0:128] + out[0:192, 128:256]) * mask

    def sharp(m):
        hi, lo = split(m)
        return jnp.where(col < 64, hi.astype(f32), lo.astype(f32)).astype(bf16)

    for j in parts:
        sums[j] = moments(s["vw"][j, 192:384, :], j)
    for j in parts:
        s["t"][j] = nn(sharp(sums[j]), bd3[j])
    bb, x2 = [None] * PARTS, [None] * PARTS
    for j in parts:
        sc = s["vw"][j, 0:192, :] * s["t"][j]
        z = nn(w["lat"][...], stack3(jnp.concatenate([x[j], sc], 0)))
        g = sigmoid(z)
        bb[j] = z * g
        d3[j] = g + bb[j] * (1.0 - g)
        x2[j] = x[j] + bb[j] * fw[j]
    wen = jnp.concatenate([w["energy"][...]] * 2, 1)
    df, dx2, dxa = ([None] * PARTS for _ in range(3))
    dz = [None] * PARTS
    for j in parts:
        z = nn(w["head"][...], stack3(x2[j]))
        g = sigmoid(z)
        hh = z * g
        df[j] = jnp.sum(wen * hh, 0, keepdims=True)
        dz[j] = wen * fw[j] * (g + hh * (1.0 - g))
    for j in parts:
        dx2[j] = nn(w["head_t"][...], stack3(dz[j]))
        df[j] = df[j] + jnp.sum(dx2[j] * bb[j], 0, keepdims=True)
        dz[j] = dx2[j] * fw[j] * d3[j]
    for j in parts:
        dc = nn(w["lat_t"][...], stack3(dz[j]))
        dxa[j] = dx2[j] + dc[0:64]
        ds = dc[64:256]
        s["dv"][j] = ds * s["t"][j]
        s["dt"][j] = ds * s["vw"][j, 0:192, :]
    m = [None] * PARTS
    for j in parts:
        m[j] = moments(s["dt"][j], j)
    for j in parts:
        s["dw"][j] = nn(sharp(m[j]), bd3[j])
    for j in parts:
        acc = None
        for left, right in ((sums[j], s["dt"][j]), (m[j], s["vw"][j, 192:384, :])):
            lt = jnp.transpose(left)[0:32]
            lh, ll = split(lt)
            rh, rl = split(right)
            both = nn(jnp.concatenate([lh, ll], 0), rh)
            one = both[0:32] + both[32:64] + nn(lh, rl)
            acc = one if acc is None else acc + one
        s["dy"][2 * j] = acc[0:16, 0:128]
        s["dy"][2 * j + 1] = acc[16:32, 128:256]
    for j in parts:
        dx = dxa[j] + nn(w["ve_t"][...], stack3(jnp.concatenate([s["dv"][j], s["dw"][j]], 0)))
        df[j] = df[j] + jnp.sum(dx * a[j], 0, keepdims=True)
        dz[j] = dx * fw[j] * d2[j]
        for k in range(2):
            s["sc"][3, 2 * j + k:2 * j + k + 1, :] = df[j][:, 128 * k:128 * k + 128]
    for j in parts:
        dz[j] = nn(w["mix_t"][...], stack3(dz[j])) * d1[j]
    for j in parts:
        dr8 = nn(w["emb_t"][...], stack3(dz[j]))
        for k in range(2):
            s["dr"][2 * j + k] = dr8[0:8, 128 * k:128 * k + 128]

    dr = s["sc"][3] * fp
    for k in range(8):
        dr = dr + s["dr"][:, k, :] * slopes[k]
    gy = [s["dy"][:, n, :] for n in range(9)]
    dux = R3 * gy[1] + R15 * (uy * gy[4] + uz * gy[7] + ux * gy[8])
    duy = R3 * gy[2] + R15 * (ux * gy[4] + uz * gy[5] - uy * gy[8])
    duz = R3 * gy[3] + R15 * (uy * gy[5] + ux * gy[7]) + (3.0 * R5) * uz * gy[6]
    dot = dux * ux + duy * uy + duz * uz
    along = dr - dot * rinv
    scale = 50.0
    return [scale * (du * rinv + along * u) for du, u in ((dux, ux), (duy, uy), (duz, uz))]


PAIR_SCRATCH = {
    "feat": (8, 8, 128), "harm": (16, 8, 128), "sc": (4, 8, 128), "vw": (PARTS, 384, WIDE), "t": (PARTS, 192, WIDE),
    "dv": (PARTS, 192, WIDE), "dt": (PARTS, 192, WIDE), "dw": (PARTS, 192, WIDE), "dy": (8, 16, 128), "dr": (8, 8, 128),
}
WEIGHT_NAMES = ("emb", "mix", "ve", "lat", "head", "head_t", "lat_t", "ve_t", "mix_t", "emb_t", "energy")


SIDE = 8
ATOMS = SIDE ** 3
ROWS = 25
STEP = 0.1
MASSES = (1.008, 15.999, 22.99, 35.453)
ZLANE = (0, 27, 54, 72, 99)
WIDTHS = (3, 2, 3)
EDGE = 2.0 * SIDE
TILE = (8, 128)
MIDDLE = [5 * x + y for x in (1, 2, 3) for y in (1, 2, 3)]
AXES = ("gx", "gy", "gz")
SIZES = (16, 8, 8)
FIRST = 2
SUM_ROWS, FAR_ROWS = 40, 16


def iota(dim, shape=TILE):
    return lax.broadcasted_iota(i32, shape, dim)


def lane_take(row, idx):
    return jnp.take_along_axis(row, idx, axis=1)


def roll_rows(v, shift):
    return v if shift % 8 == 0 else pltpu.roll(v, shift % 8, 0)


def roll_lanes(v, shift):
    return v if shift % 128 == 0 else pltpu.roll(v, shift % 128, 1)


def inverse_mass(kind):
    out = jnp.full(kind.shape, 1.0 / MASSES[3], f32)
    for k in range(3):
        out = jnp.where(kind == float(k), 1.0 / MASSES[k], out)
    return out


def masses(kind):
    out = jnp.full(kind.shape, MASSES[3], f32)
    for k in range(3):
        out = jnp.where(kind == float(k), MASSES[k], out)
    return out


def parity():
    return [lax.axis_index(a) & 1 for a in AXES]


def place_in(side):
    p = parity()
    return (p[0] * 4 + p[1] * 2 + p[2]) ^ (7 if side else 0)


def pack4(rows, start):
    lane = iota(1)
    out = []
    for k in range(0, len(rows), 4):
        v = roll_lanes(rows[k], -start)
        for p in range(1, len(rows[k:k + 4])):
            v = jnp.where(lane >= 32 * p, roll_lanes(rows[k + p], 32 * p - start), v)
        out.append(v)
    return out


def doubled(tiles):
    sub = iota(0)
    return [jnp.where(sub < 4, tiles[k], roll_rows(tiles[k + 1], 4)) if k + 1 < len(tiles) else tiles[k] for k in range(0, len(tiles), 2)]


def start_kernel(given, spec, cells, chunks, mid, cid, own, raw):
    px, py, pz = parity()
    raw[...] = jnp.zeros((128, 128), i32)
    kind = spec[...].astype(f32)
    kick = given[3:6, :] + (0.5 * STEP) * given[6:9, :] * inverse_mass(kind)
    own[0:3, :] = given[0:3, :] + STEP * kick
    own[3:4, :] = kind
    own[4:7, :] = kick
    own[7:8, :] = jnp.zeros_like(kind)
    for x in range(3):
        for y in range(3):
            at = 8 * (3 * x + y)
            raw[at:at + 3, 0:27] = cells[x + px * (2 - 2 * x), y + py * (2 - 2 * y)]
    z0, z1, z2 = (raw[pl.ds(k, 16, stride=8), :] for k in range(3))
    lane = iota(1, (16, 128))
    flip = jnp.full((16, 128), pz, i32) == 1
    ids = jnp.where(lane < ZLANE[2], pltpu.roll(jnp.where(flip, z2, z0), ZLANE[1], 1),
                    jnp.where(lane < ZLANE[3], pltpu.roll(z1, ZLANE[2], 1), pltpu.roll(jnp.where(flip, z0, z2), ZLANE[3], 1)))
    cid[...] = jnp.where((lane >= ZLANE[1]) & (lane < ZLANE[4]), ids, 0)
    cuts = [own[:, 128 * h:128 * h + 128] for h in range(4)]
    rows = []
    for r in range(9):
        ids = jnp.broadcast_to(cid[r:r + 1, :], TILE)
        lo, hi = ids & 127, ids >> 7
        acc = lane_take(cuts[0], lo)
        for h in range(1, 4):
            acc = jnp.where(hi == h, lane_take(cuts[h], lo), acc)
        mid[r] = acc
        rows.append(acc)
    me = place_in(0)
    zs = ZLANE[3]
    for d, tiles in ((4, rows[6:9]), (2, rows[2::3]), (6, rows[8:9]), (1, pack4(rows, zs)), (5, pack4(rows[6:9], zs)),
                     (3, pack4(rows[2::3], zs)), (7, pack4(rows[8:9], zs))):
        for k, v in enumerate(doubled(tiles)):
            chunks[me ^ d, k] = v


def widen(have, got, me, face):
    lane = iota(1)
    beyond = (lambda: lane >= ZLANE[4]) if face else (lambda: lane < ZLANE[1])
    at = ZLANE[face]
    xs = sorted({x for x, _ in have})
    rows = sorted(have)

    def half(d, n):
        return roll_rows(got[me ^ d, n // 2], -4 * (n % 2))

    def strip(d, keys, base):
        out = {}
        for n, key in enumerate(keys):
            v = roll_lanes(half(d, n // 4), at - 32 * (n % 4))
            out[key] = jnp.where(beyond(), v, base[key])
        return out

    new = strip(1, rows, have)
    new.update(strip(5, [(face, y) for y in xs], {(face, y): half(4, n) for n, y in enumerate(xs)}))
    new.update(strip(3, [(x, face) for x in xs], {(x, face): half(2, n) for n, x in enumerate(xs)}))
    new.update(strip(7, [(face, face)], {(face, face): half(6, 0)}))
    return new


def second_kernel(got, mid, neigh, cen, emb, energy, table, chunks):
    have = {(r // 3 + 1, r % 3 + 1): mid[r] for r in range(9)}
    have = widen(have, got, place_in(0), 4)
    for (x, y), v in have.items():
        table[4 * (x - 1) + y - 1] = v
    me = place_in(1)
    zs = ZLANE[1]
    along_x = [have[1, y] for y in range(1, 5)]
    along_y = [have[x, 1] for x in range(1, 5)]
    whole = [have[x, y] for x in range(1, 5) for y in range(1, 5)]
    for d, tiles in ((4, along_x), (2, along_y), (6, along_x[:1]), (1, pack4(whole, zs)), (5, pack4(along_x, zs)),
                     (3, pack4(along_y, zs)), (7, pack4(along_x[:1], zs))):
        for k, v in enumerate(doubled(tiles)):
            chunks[me ^ d, k] = v


def prepare(neigh, cen, cid, emb, mix, val, env, lat, head, energy, nrow, nlane, live, crow, clane, irow, ilane, *out):
    sub, lane = iota(0), iota(1)
    big = iota(0, (128, 128))
    left, right = [], []
    for r in range(9):
        area = WIDTHS[r // 3] * WIDTHS[r % 3]
        ids = jnp.broadcast_to(cid[r:r + 1, :], TILE)
        valid = (lane >= 27) & (lane < 27 + 3 * area)
        valid = valid | ((lane >= 54) & (lane < 54 + 2 * area))
        valid = valid | ((lane >= 72) & (lane < 72 + 3 * area))
        row = (r // 3 + 1) * 5 + r % 3 + 1
        value = jnp.where((sub & 1) == 0, row, lane)
        left.append(jnp.where(valid & ((ids >> 7) == (sub >> 1)), value, 0).astype(f32).astype(bf16))
        lo = jnp.broadcast_to(cid[r:r + 1, :], (128, 128)) & 127
        right.append(jnp.where(big == lo, 1.0, 0.0).astype(bf16))
    inv = nt(jnp.concatenate(left, 1), jnp.concatenate(right, 1))
    inv = (inv + 0.5).astype(i32)
    for h in range(4):
        irow[h:h + 1, :] = inv[2 * h:2 * h + 1, :]
        ilane[h:h + 1, :] = inv[2 * h + 1:2 * h + 2, :]
    px, py, pz = parity()

    def flip(e, p):
        return e + p * (4 - 2 * e)

    def place(n):
        lo, hi = n & 127, n >> 7
        row = jnp.zeros(TILE, i32)
        col = jnp.zeros(TILE, i32)
        for h in range(4):
            row = jnp.where(hi == h, lane_take(jnp.broadcast_to(irow[h:h + 1, :], TILE), lo), row)
            col = jnp.where(hi == h, lane_take(jnp.broadcast_to(ilane[h:h + 1, :], TILE), lo), col)
        m = jnp.maximum(n - ATOMS, 0)
        grow = ((m.astype(f32) + 0.5) * (1.0 / 135.0)).astype(i32)
        rem = m - 135 * grow
        ex = ((grow.astype(f32) + 0.5) * 0.2).astype(i32)
        ey = grow - 5 * ex
        ez = ((rem.astype(f32) + 0.5) * (1.0 / 27.0)).astype(i32)
        slot = rem - 27 * ez
        ex, ey, ez = flip(ex, px), flip(ey, py), flip(ez, pz)
        first = jnp.where(ez == 0, 0, jnp.where(ez == 1, 27, jnp.where(ez == 2, 54, jnp.where(ez == 3, 72, 99))))
        return jnp.where(hi < 4, row, 5 * ex + ey), jnp.where(hi < 4, col, first + slot)

    n = neigh[...]
    c = jnp.concatenate([cen[...].astype(f32), jnp.zeros((1, 120), f32)], 1)
    c = jnp.sum(jnp.where(lane == sub, jnp.broadcast_to(c, TILE), 0.0), 1, keepdims=True)
    c = (jnp.broadcast_to(c, TILE) + 0.5).astype(i32)
    nrow[...], nlane[...] = place(n)
    crow[...], clane[...] = place(c)
    live[...] = jnp.where(n != c, 1.0, 0.0)

    def stack(w):
        hi = w.astype(bf16).astype(f32)
        return jnp.concatenate([hi, hi, w - hi], 1).astype(bf16)

    ve_t = jnp.concatenate([val[...], env[...]], 1)
    emb_t = jnp.concatenate([emb[0:8, :], jnp.zeros((8, C), f32)], 0)
    wide_energy = jnp.broadcast_to(energy[...], (128, C))
    tiles = (stack(emb[...].T), stack(mix[...]), stack(ve_t.T), stack(lat[...]), stack(head[...]), stack(head[...].T),
             stack(lat[...].T), stack(ve_t), stack(mix[...].T), stack(emb_t), wide_energy.T)
    for ref, v in zip(out, tiles):
        ref[...] = v


def pair_step(tab, nrow, nlane, live, crow, clane, w, s, force):
    sub, lane = iota(0), iota(1)
    px, py, pz = (1.0 - 2.0 * p.astype(f32) for p in parity())
    zshift = jnp.where(lane < ZLANE[1], -EDGE, jnp.where(lane >= ZLANE[4], EDGE, 0.0)) * pz
    zshift = jnp.where(sub == 2, zshift, 0.0)
    xshift = jnp.where(sub == 0, EDGE, 0.0) * px
    yshift = jnp.where(sub == 1, EDGE, 0.0) * py
    nr, nl, cr, cl = nrow[...], nlane[...], crow[...], clane[...]
    near = [jnp.zeros(TILE, f32) for _ in range(4)]
    centre = [jnp.zeros(TILE, f32) for _ in range(4)]
    for r in range(ROWS):
        ex, ey = r // 5, r % 5
        shift = zshift
        if ex in (0, 4):
            shift = shift + xshift * float(ex // 2 - 1)
        if ey in (0, 4):
            shift = shift + yshift * float(ey // 2 - 1)
        s["shifted"][r] = tab(ex, ey) + shift
        mine = nr == r
        centred = cr == r
        for q in range(4):
            line = jnp.broadcast_to(s["shifted"][r, q:q + 1, :], TILE)
            near[q] = jnp.where(mine, lane_take(line, nl), near[q])
            if ex in (1, 2, 3) and ey in (1, 2, 3):
                centre[q] = jnp.where(centred, lane_take(line, cl), centre[q])
    alive = live[...]
    disp = [near[k] - centre[k] for k in range(3)]
    grads = pair_grads(disp, centre[3], near[3], alive, w, s)
    spare = 1.0 / jnp.sum(1.0 - alive, 1, keepdims=True)
    for k, g in enumerate(grads):
        g = jnp.where(alive > 0.0, -g, jnp.sum(g, 1, keepdims=True) * spare)
        hi = g.astype(bf16).astype(f32)
        s["spread"][k] = hi
        s["spread"][k + 3] = g - hi
    s["spread"][6] = jnp.zeros(TILE, f32)
    s["spread"][7] = jnp.zeros(TILE, f32)
    big = iota(0, (128, 128))
    left, right = [], []
    for b in range(NB):
        g = s["spread"][:, b, :]
        rows = jnp.broadcast_to(nrow[b:b + 1, :], TILE)
        left.append(jnp.concatenate([jnp.where(rows == r, g, 0.0) for r in range(ROWS)], 0).astype(bf16))
        right.append(jnp.where(big == jnp.broadcast_to(nlane[b:b + 1, :], (128, 128)), 1.0, 0.0).astype(bf16))
    out = nt(jnp.concatenate(left, 1), jnp.concatenate(right, 1))
    for r in range(ROWS):
        v = out[8 * r:8 * r + 8]
        force[r] = jnp.where(sub < 3, v + roll_rows(v, -3), 0.0)


def far_rows(side):
    far = 0 if side else 4
    rest = (1, 2, 3) if side else (0, 1, 2, 3)
    return [5 * far + y for y in rest], [5 * x + far for x in rest], [5 * x + y for x in rest for y in rest], [5 * far + far]


def put(chunks, d, values):
    for m, v in enumerate(values):
        chunks[d, 3 * m:3 * m + 3, :] = v[0:3]


def strips4(rows, at):
    return pack4(rows, at)


def strips2(rows, head, tail):
    lane = iota(1)
    out = []
    for k in range(0, len(rows), 2):
        v = None
        for n, q in enumerate(rows[k:k + 2]):
            t = jnp.where(lane < 64 * n + 27, roll_lanes(q, 64 * n - head), roll_lanes(q, 64 * n + 27 - tail))
            v = t if v is None else jnp.where(lane >= 64, t, v)
        out.append(v)
    return out


def sum_messages(force, base, chunks, side):
    me = place_in(side)
    near, far = (1, 0) if side else (3, 4)
    head, tail = (ZLANE[near], ZLANE[far]) if side else (ZLANE[far], ZLANE[near])
    f = [force[r] for r in range(ROWS)]
    for k, r in enumerate(MIDDLE):
        f[r] = f[r] + base[k]
    xs = [f[5 * x + y] for x in (far, near) for y in range(5)]
    ys = [f[5 * x + y] for y in (far, near) for x in range(5)]
    corner = [f[5 * x + y] for x in (far, near) for y in (far, near)]
    for d, tiles in ((4, xs), (2, ys), (6, corner), (1, strips2(f, head, tail)), (5, strips2(xs, head, tail)),
                     (3, strips2(ys, head, tail)), (7, strips2(corner, head, tail))):
        put(chunks, me ^ d, tiles)


def add_messages(force, got, side):
    lane = iota(1, (3, 128))
    me = place_in(side)
    near, far = (1, 0) if side else (3, 4)
    inside = lane >= ZLANE[3] if side == 0 else lane < ZLANE[2]
    first = min(ZLANE[near], ZLANE[far])
    out = {r: force[r, 0:3, :] for r in range(ROWS)}
    xs = [5 * x + y for x in (near, far) for y in range(5)]
    ys = [5 * x + y for y in (near, far) for x in range(5)]
    corner = [5 * x + y for x in (near, far) for y in (near, far)]
    for d, rows in ((4, xs), (2, ys), (6, corner)):
        for m, r in enumerate(rows):
            out[r] = out[r] + got[me ^ d, 3 * m:3 * m + 3, :]
    for d, rows in ((1, list(range(ROWS))), (5, xs), (3, ys), (7, corner)):
        for n, r in enumerate(rows):
            v = got[me ^ d, 3 * (n // 2):3 * (n // 2) + 3, :]
            out[r] = out[r] + jnp.where(inside, roll_lanes(v, first - 64 * (n % 2)), 0.0)
    return out


def far_messages(force, chunks, side):
    me = place_in(side)
    at = ZLANE[0 if side else 4]
    xs, ys, whole, corner = ([force[r] for r in rows] for rows in far_rows(side))
    for d, tiles in ((4, xs), (2, ys), (6, corner), (1, strips4(whole, at)), (5, strips4(xs, at)), (3, strips4(ys, at)),
                     (7, strips4(corner, at))):
        put(chunks, me ^ d, tiles)


def add_far(force, got, side):
    lane = iota(1, (3, 128))
    me = place_in(side)
    near, far = (1, 0) if side else (3, 4)
    at = ZLANE[near]
    inside = (lane >= at) & (lane < at + 27)
    xs, ys, whole, corner = far_rows(side)
    out = {r: force[r, 0:3, :] for r in whole}
    xs = [r + 5 * (near - far) for r in xs]
    ys = [r + near - far for r in ys]
    corner = [5 * near + near]
    for d, rows in ((4, xs), (2, ys), (6, corner)):
        for m, r in enumerate(rows):
            out[r] = out[r] + got[me ^ d, 3 * m:3 * m + 3, :]
    for d, rows in ((1, whole), (5, xs), (3, ys), (7, corner)):
        for n, r in enumerate(rows):
            v = got[me ^ d, 3 * (n // 4):3 * (n // 4) + 3, :]
            out[r] = out[r] + jnp.where(inside, roll_lanes(v, at - 32 * (n % 4)), 0.0)
    return out


def weight_refs(refs):
    return dict(zip(WEIGHT_NAMES, refs))


def first_pairs(part, got, *refs):
    tab, force, base, chunks = refs[10:14]
    prepare(*refs[:10], *refs[14:32])
    nrow, nlane, live, crow, clane = refs[14:19]
    w = weight_refs(refs[21:32])
    s = dict(zip(ALL_SCRATCH, refs[32:]))
    have = {(x, y): part[4 * (x - 1) + y - 1] for x in range(1, 5) for y in range(1, 5)}
    for (x, y), v in widen(have, got, place_in(1), 0).items():
        tab[5 * x + y] = v
    pair_step(lambda x, y: tab[5 * x + y], nrow, nlane, live, crow, clane, w, s, force)
    sub, lane = iota(0), iota(1)
    mine = (sub < 3) & (lane >= ZLANE[1]) & (lane < ZLANE[4])
    for k, r in enumerate(MIDDLE):
        v = tab[r]
        rest = (v + STEP * roll_rows(v, -4)) * (1.0 / (STEP * STEP)) * masses(jnp.broadcast_to(tab[r, 3:4, :], TILE))
        base[k] = jnp.where(mine, rest, 0.0)
    sum_messages(force, base, chunks, 1)


def next_pairs(force, got, table, nrow, nlane, live, crow, clane, *refs):
    w = weight_refs(refs[:11])
    total, force2, chunks = refs[11:14]
    s = dict(zip(ALL_SCRATCH, refs[14:]))
    lane = iota(1, (3, 128))
    mine = (lane >= ZLANE[1]) & (lane < ZLANE[4])
    for r, f in add_messages(force, got, 0).items():
        mass = inverse_mass(jnp.broadcast_to(table[r, 3:4, :], (3, 128)))
        moved = (STEP * STEP) * f * mass
        if r in MIDDLE:
            total[MIDDLE.index(r), 0:3, :] = f
            half = (0.5 * STEP) * f * mass
            kick = table[r, 4:7, :] + half + half
            moved = jnp.where(mine, table[r, 0:3, :] + STEP * kick, moved)
        s["table"][r] = table[r]
        s["table"][r, 0:3, :] = moved
    pair_step(lambda x, y: s["table"][5 * x + y], nrow, nlane, live, crow, clane, w, s, force2)
    far_messages(force2, chunks, 0)


def sum_kernel(force, base, got, out, chunks):
    for r, v in add_messages(force, got, 1).items():
        out[r, 0:3, :] = v
    sum_messages(out, base, chunks, 0)


def far_kernel(force, got, out, chunks):
    for r, v in add_far(force, got, 0).items():
        out[r, 0:3, :] = v
    far_messages(out, chunks, 1)


def end_kernel(force, got, total, irow, ilane, own, new_pos, new_vel, new_frc, both):
    summed = add_far(force, got, 1)
    for k, r in enumerate(MIDDLE):
        both[k, 0:3, :] = summed[r]
        both[k, 3:6, :] = total[k, 0:3, :]
        both[k, 6:8, :] = jnp.zeros((2, 128), f32)
    mass = inverse_mass(own[3:4, :])
    for h in range(4):
        lanes = slice(128 * h, 128 * h + 128)
        ir = jnp.broadcast_to(irow[h:h + 1, :], TILE)
        il = jnp.broadcast_to(ilane[h:h + 1, :], TILE)
        acc = jnp.zeros(TILE, f32)
        for k, r in enumerate(MIDDLE):
            acc = jnp.where(ir == r, lane_take(both[k], il), acc)
        last, first = acc[0:3], acc[3:6]
        m = mass[:, lanes]
        half = (0.5 * STEP) * first * m
        kick = own[4:7, lanes] + half + half
        new_pos[:, lanes] = own[0:3, lanes] + STEP * kick
        new_vel[:, lanes] = kick + (0.5 * STEP) * last * m
        new_frc[:, lanes] = last


ALL_SCRATCH = dict(PAIR_SCRATCH, shifted=(ROWS, 8, 128), table=(ROWS, 8, 128), spread=(8, 8, 128))


def shape(*dims, kind=f32):
    return jax.ShapeDtypeStruct(dims, kind)


def call(kernel, outs, *args, scratch=(), limit=4 << 20, flops=1 << 20, space=pltpu.VMEM):
    vm = pl.BlockSpec(memory_space=pltpu.VMEM)
    return pl.pallas_call(
        kernel,
        out_shape=tuple(outs),
        in_specs=[pl.BlockSpec(memory_space=space)] * len(args),
        out_specs=tuple([vm] * len(outs)),
        scratch_shapes=list(scratch),
        compiler_params=pltpu.CompilerParams(vmem_limit_bytes=limit),
        cost_estimate=pl.CostEstimate(flops=flops, bytes_accessed=1 << 18, transcendentals=0),
    )(*args)


def groups(side):
    out = []
    for x in range(side, SIZES[0] + side, 2):
        for y in range(side, SIZES[1] + side, 2):
            for z in range(side, SIZES[2] + side, 2):
                out.append([(((x + a) % SIZES[0]) * SIZES[1] + (y + b) % SIZES[1]) * SIZES[2] + (z + c) % SIZES[2]
                            for a in range(2) for b in range(2) for c in range(2)])
    return out


def trade(chunks, side):
    return lax.all_to_all(chunks, AXES, 0, 0, axis_index_groups=groups(side), tiled=True)


def local(positions, velocities, forces, species, cell_ids, centers, neighbours,
          w_embed, w_mix, w_value, w_env, w_latent, w_head, w_energy):
    table_shape = shape(ROWS, 8, 128)
    sums, fars = shape(8, SUM_ROWS, 128), shape(8, FAR_ROWS, 128)
    int_tile, flat = shape(8, 128, kind=i32), shape(4, 128, kind=i32)
    scratch = [pltpu.VMEM(v, f32) for v in ALL_SCRATCH.values()]

    chunks, mid, cid, own = call(
        start_kernel, [shape(8, FIRST, 8, 128), shape(9, 8, 128), shape(16, 128, kind=i32), shape(8, ATOMS)],
        jnp.concatenate([positions, velocities, forces], 0), species.reshape(1, ATOMS), cell_ids,
        scratch=[pltpu.VMEM((128, 128), i32)])
    got = trade(chunks, 0)
    weight_shapes = [shape(m, k, kind=bf16) for m, k in (
        (C, 48), (C, 192), (384, 192), (C, 768), (C, 192), (C, 192), (256, 192), (C, 1152), (C, 192), (16, 192))]
    small = (neighbours, centers.reshape(1, NB), w_embed.T, w_energy.reshape(1, C))
    part, chunks = call(second_kernel, [shape(16, 8, 128), shape(8, FIRST, 8, 128)], got, mid, *small)
    got = trade(chunks, 1)
    indices = [int_tile, int_tile, shape(8, 128), int_tile, int_tile, flat, flat]
    table, force, base, chunks, *prepared = call(
        first_pairs, [table_shape, table_shape, shape(9, 8, 128), sums] + indices + weight_shapes + [shape(C, 128)],
        part, got, small[0], small[1], cid, small[2], w_mix, w_value[0].T, w_env[0].T, w_latent[0], w_head, small[3], scratch=scratch, limit=24 << 20, flops=1 << 30)
    idx, (irow, ilane), weights = prepared[:5], prepared[5:7], prepared[7:]
    force, chunks = call(sum_kernel, [table_shape, sums], force, base, trade(chunks, 1))
    total, force, chunks = call(
        next_pairs, [shape(9, 8, 128), table_shape, fars], force, trade(chunks, 0), table, *idx, *weights, scratch=scratch,
        limit=24 << 20, flops=1 << 30)
    force, chunks = call(far_kernel, [table_shape, fars], force, trade(chunks, 0))
    return call(end_kernel, [shape(3, ATOMS)] * 3, force, trade(chunks, 1), total, irow, ilane, own,
                scratch=[pltpu.VMEM((9, 8, 128), f32)])


def solution(mesh):
    from jax.sharding import PartitionSpec as P

    rows = P(None, AXES)
    in_specs = (rows, rows, rows, P(AXES), P(*AXES, None), P(AXES), P(AXES, None)) + (P(),) * 7
    return jax.shard_map(local, mesh=mesh, in_specs=in_specs, out_specs=(rows, rows, rows), check_vma=False)
```

```python
import math
import jax, jax.numpy as jnp
from jax import lax
from jax.experimental import pallas as pl
from jax.experimental.pallas import tpu as pltpu

f32, bf16, i32 = jnp.float32, jnp.bfloat16, jnp.int32
NB, BLK, C = 8, 128, 64
PAIRS = NB * BLK
PARTS = NB // 2
WIDE = 2 * BLK
R3, R5, R15 = math.sqrt(3.0), math.sqrt(5.0), math.sqrt(15.0)


def nt(a, b):
    return lax.dot_general(a, b, (((1,), (1,)), ((), ())), preferred_element_type=f32)


def nn(a, b):
    return jnp.dot(a, b, preferred_element_type=f32)


def split(x):
    hi = x.astype(bf16)
    return hi, (x - hi.astype(f32)).astype(bf16)


def stack3(x):
    hi, lo = split(x)
    return jnp.concatenate([hi, lo, hi], 0)


def sigmoid(z):
    return 0.5 * jnp.tanh(0.5 * z) + 0.5


def harmonic_rows(ux, uy, uz):
    return [jnp.ones_like(ux), R3 * ux, R3 * uy, R3 * uz, R15 * ux * uy, R15 * uy * uz,
            0.5 * R5 * (3.0 * uz * uz - 1.0), R15 * ux * uz, 0.5 * R15 * (ux * ux - uy * uy)]


def pair_grads(disp, kc, kn, live, w, s):
    dx, dy, dz = disp
    r = jnp.sqrt(dx * dx + dy * dy + dz * dz + 0.09)
    rinv = 1.0 / r
    ux, uy, uz = dx * rinv, dy * rinv, dz * rinv
    q = jnp.minimum(r * (1.0 / 6.0), 1.0)
    q2 = q * q
    q4 = q2 * q2
    q5 = q4 * q
    q6 = q4 * q2
    f = (1.0 - 28.0 * q6 + 48.0 * (q6 * q) - 21.0 * (q6 * q2)) * live
    fp = -28.0 * q5 * (1.0 - q) * (1.0 - q) * live
    theta = math.pi * q
    s1, c1 = jnp.sin(theta), jnp.cos(theta)
    sm, cm = s1, c1
    norm = math.sqrt(1.0 / 3.0)
    rn = norm * rinv
    slopes = []
    for m in range(8):
        s["feat"][m] = sm * rn
        slopes.append((cm * (math.pi / 6.0 * (m + 1)) - sm * rinv) * rn)
        sm, cm = sm * c1 + cm * s1, cm * c1 - sm * s1
    ys = harmonic_rows(ux, uy, uz)
    for n in range(9):
        s["harm"][n] = ys[n]
    for n in range(9, 16):
        s["harm"][n] = jnp.zeros((8, 128), f32)
    s["sc"][0] = f
    s["sc"][1] = kc
    s["sc"][2] = kn

    parts = range(PARTS)
    sub8 = lax.broadcasted_iota(i32, (8, BLK), 0).astype(f32)

    def features(b):
        hot = jnp.where(sub8 < 4.0, jnp.broadcast_to(s["sc"][1, b:b + 1, :], (8, BLK)),
                        jnp.broadcast_to(s["sc"][2, b:b + 1, :], (8, BLK)) + 4.0) == sub8
        return jnp.concatenate([s["feat"][:, b, :], hot.astype(f32)], 0)

    def envelope(j):
        return jnp.concatenate([s["sc"][0, b:b + 1, :] for b in (2 * j, 2 * j + 1)], 1)

    fw = [envelope(j) for j in parts]
    d1, d2, d3, a, x, sums, t = ([None] * PARTS for _ in range(7))
    h = [None] * PARTS
    for j in parts:
        feat = jnp.concatenate([features(2 * j), features(2 * j + 1)], 1)
        z = nn(w["emb"][...], stack3(feat))
        g = sigmoid(z)
        h[j] = z * g
        d1[j] = g + h[j] * (1.0 - g)
    for j in parts:
        z = nn(w["mix"][...], stack3(h[j]))
        g = sigmoid(z)
        a[j] = z * g
        d2[j] = g + a[j] * (1.0 - g)
        x[j] = a[j] * fw[j]
    for j in parts:
        s["vw"][j] = nn(w["ve"][...], stack3(x[j]))

    zero = jnp.zeros((16, BLK), f32)
    bd3, rep = [], []
    for j in parts:
        y0, y1 = s["harm"][:, 2 * j, :], s["harm"][:, 2 * j + 1, :]
        bd = jnp.concatenate([jnp.concatenate([y0, zero], 1), jnp.concatenate([zero, y1], 1)], 0)
        hi, lo = split(bd)
        none = jnp.zeros((32, WIDE), bf16)
        bd3.append(jnp.concatenate([hi, lo, hi, none], 0))
        rep.append(jnp.concatenate([hi, hi, hi, none, lo, lo, lo, none], 0))

    row = lax.broadcasted_iota(i32, (192, 128), 0) // C
    col = lax.broadcasted_iota(i32, (192, 128), 1)
    part = col % 16
    order = jnp.where(part == 0, 0, jnp.where(part < 4, 1, jnp.where(part < 9, 2, 3)))
    mask = jnp.where(row == order, 0.1, 0.0).astype(f32)

    def moments(val, j):
        out = nt(jnp.concatenate(split(val), 0), rep[j])
        return (out[0:192, 0:128] + out[192:384, 0:128] + out[0:192, 128:256]) * mask

    def sharp(m):
        hi, lo = split(m)
        return jnp.where(col < 64, hi.astype(f32), lo.astype(f32)).astype(bf16)

    for j in parts:
        sums[j] = moments(s["vw"][j, 192:384, :], j)
    for j in parts:
        s["t"][j] = nn(sharp(sums[j]), bd3[j])
    bb, x2 = [None] * PARTS, [None] * PARTS
    for j in parts:
        sc = s["vw"][j, 0:192, :] * s["t"][j]
        z = nn(w["lat"][...], stack3(jnp.concatenate([x[j], sc], 0)))
        g = sigmoid(z)
        bb[j] = z * g
        d3[j] = g + bb[j] * (1.0 - g)
        x2[j] = x[j] + bb[j] * fw[j]
    wen = jnp.concatenate([w["energy"][...]] * 2, 1)
    df, dx2, dxa = ([None] * PARTS for _ in range(3))
    dz = [None] * PARTS
    for j in parts:
        z = nn(w["head"][...], stack3(x2[j]))
        g = sigmoid(z)
        hh = z * g
        df[j] = jnp.sum(wen * hh, 0, keepdims=True)
        dz[j] = wen * fw[j] * (g + hh * (1.0 - g))
    for j in parts:
        dx2[j] = nn(w["head_t"][...], stack3(dz[j]))
        df[j] = df[j] + jnp.sum(dx2[j] * bb[j], 0, keepdims=True)
        dz[j] = dx2[j] * fw[j] * d3[j]
    for j in parts:
        dc = nn(w["lat_t"][...], stack3(dz[j]))
        dxa[j] = dx2[j] + dc[0:64]
        ds = dc[64:256]
        s["dv"][j] = ds * s["t"][j]
        s["dt"][j] = ds * s["vw"][j, 0:192, :]
    m = [None] * PARTS
    for j in parts:
        m[j] = moments(s["dt"][j], j)
    for j in parts:
        s["dw"][j] = nn(sharp(m[j]), bd3[j])
    for j in parts:
        acc = None
        for left, right in ((sums[j], s["dt"][j]), (m[j], s["vw"][j, 192:384, :])):
            lt = jnp.transpose(left)[0:32]
            lh, ll = split(lt)
            rh, rl = split(right)
            both = nn(jnp.concatenate([lh, ll], 0), rh)
            one = both[0:32] + both[32:64] + nn(lh, rl)
            acc = one if acc is None else acc + one
        s["dy"][2 * j] = acc[0:16, 0:128]
        s["dy"][2 * j + 1] = acc[16:32, 128:256]
    for j in parts:
        dx = dxa[j] + nn(w["ve_t"][...], stack3(jnp.concatenate([s["dv"][j], s["dw"][j]], 0)))
        df[j] = df[j] + jnp.sum(dx * a[j], 0, keepdims=True)
        dz[j] = dx * fw[j] * d2[j]
        for k in range(2):
            s["sc"][3, 2 * j + k:2 * j + k + 1, :] = df[j][:, 128 * k:128 * k + 128]
    for j in parts:
        dz[j] = nn(w["mix_t"][...], stack3(dz[j])) * d1[j]
    for j in parts:
        dr8 = nn(w["emb_t"][...], stack3(dz[j]))
        for k in range(2):
            s["dr"][2 * j + k] = dr8[0:8, 128 * k:128 * k + 128]

    dr = s["sc"][3] * fp
    for k in range(8):
        dr = dr + s["dr"][:, k, :] * slopes[k]
    gy = [s["dy"][:, n, :] for n in range(9)]
    dux = R3 * gy[1] + R15 * (uy * gy[4] + uz * gy[7] + ux * gy[8])
    duy = R3 * gy[2] + R15 * (ux * gy[4] + uz * gy[5] - uy * gy[8])
    duz = R3 * gy[3] + R15 * (uy * gy[5] + ux * gy[7]) + (3.0 * R5) * uz * gy[6]
    dot = dux * ux + duy * uy + duz * uz
    along = dr - dot * rinv
    scale = 50.0
    return [scale * (du * rinv + along * u) for du, u in ((dux, ux), (duy, uy), (duz, uz))]


PAIR_SCRATCH = {
    "feat": (8, 8, 128), "harm": (16, 8, 128), "sc": (4, 8, 128), "vw": (PARTS, 384, WIDE), "t": (PARTS, 192, WIDE),
    "dv": (PARTS, 192, WIDE), "dt": (PARTS, 192, WIDE), "dw": (PARTS, 192, WIDE), "dy": (8, 16, 128), "dr": (8, 8, 128),
}
WEIGHT_NAMES = ("emb", "mix", "ve", "lat", "head", "head_t", "lat_t", "ve_t", "mix_t", "emb_t", "energy")


SIDE = 8
ATOMS = SIDE ** 3
ROWS = 25
STEP = 0.1
MASSES = (1.008, 15.999, 22.99, 35.453)
ZLANE = (0, 27, 54, 72, 99)
WIDTHS = (3, 2, 3)
EDGE = 2.0 * SIDE
TILE = (8, 128)
MIDDLE = [5 * x + y for x in (1, 2, 3) for y in (1, 2, 3)]
AXES = ("gx", "gy", "gz")
SIZES = (16, 8, 8)
FIRST = 2
SUM_ROWS, FAR_ROWS = 40, 16


def iota(dim, shape=TILE):
    return lax.broadcasted_iota(i32, shape, dim)


def lane_take(row, idx):
    return jnp.take_along_axis(row, idx, axis=1)


def roll_rows(v, shift):
    return v if shift % 8 == 0 else pltpu.roll(v, shift % 8, 0)


def roll_lanes(v, shift):
    return v if shift % 128 == 0 else pltpu.roll(v, shift % 128, 1)


def inverse_mass(kind):
    out = jnp.full(kind.shape, 1.0 / MASSES[3], f32)
    for k in range(3):
        out = jnp.where(kind == float(k), 1.0 / MASSES[k], out)
    return out


def masses(kind):
    out = jnp.full(kind.shape, MASSES[3], f32)
    for k in range(3):
        out = jnp.where(kind == float(k), MASSES[k], out)
    return out


def parity():
    return [lax.axis_index(a) & 1 for a in AXES]


def place_in(side):
    p = parity()
    return (p[0] * 4 + p[1] * 2 + p[2]) ^ (7 if side else 0)


def pack4(rows, start):
    lane = iota(1)
    out = []
    for k in range(0, len(rows), 4):
        v = roll_lanes(rows[k], -start)
        for p in range(1, len(rows[k:k + 4])):
            v = jnp.where(lane >= 32 * p, roll_lanes(rows[k + p], 32 * p - start), v)
        out.append(v)
    return out


def doubled(tiles):
    sub = iota(0)
    return [jnp.where(sub < 4, tiles[k], roll_rows(tiles[k + 1], 4)) if k + 1 < len(tiles) else tiles[k] for k in range(0, len(tiles), 2)]


def start_kernel(given, spec, cells, neigh, cen, emb, energy, chunks, mid, cid, own, raw):
    px, py, pz = parity()
    raw[...] = jnp.zeros((128, 128), i32)
    kind = spec[...].astype(f32)
    kick = given[3:6, :] + (0.5 * STEP) * given[6:9, :] * inverse_mass(kind)
    own[0:3, :] = given[0:3, :] + STEP * kick
    own[3:4, :] = kind
    own[4:7, :] = kick
    own[7:8, :] = jnp.zeros_like(kind)
    for x in range(3):
        for y in range(3):
            at = 8 * (3 * x + y)
            raw[at:at + 3, 0:27] = cells[x + px * (2 - 2 * x), y + py * (2 - 2 * y)]
    z0, z1, z2 = (raw[pl.ds(k, 16, stride=8), :] for k in range(3))
    lane = iota(1, (16, 128))
    flip = jnp.full((16, 128), pz, i32) == 1
    ids = jnp.where(lane < ZLANE[2], pltpu.roll(jnp.where(flip, z2, z0), ZLANE[1], 1),
                    jnp.where(lane < ZLANE[3], pltpu.roll(z1, ZLANE[2], 1), pltpu.roll(jnp.where(flip, z0, z2), ZLANE[3], 1)))
    cid[...] = jnp.where((lane >= ZLANE[1]) & (lane < ZLANE[4]), ids, 0)
    cuts = [own[:, 128 * h:128 * h + 128] for h in range(4)]
    rows = []
    for r in range(9):
        ids = jnp.broadcast_to(cid[r:r + 1, :], TILE)
        lo, hi = ids & 127, ids >> 7
        acc = lane_take(cuts[0], lo)
        for h in range(1, 4):
            acc = jnp.where(hi == h, lane_take(cuts[h], lo), acc)
        mid[r] = acc
        rows.append(acc)
    me = place_in(0)
    zs = ZLANE[3]
    for d, tiles in ((4, rows[6:9]), (2, rows[2::3]), (6, rows[8:9]), (1, pack4(rows, zs)), (5, pack4(rows[6:9], zs)),
                     (3, pack4(rows[2::3], zs)), (7, pack4(rows[8:9], zs))):
        for k, v in enumerate(doubled(tiles)):
            chunks[me ^ d, k] = v


def widen(have, got, me, face):
    lane = iota(1)
    beyond = (lambda: lane >= ZLANE[4]) if face else (lambda: lane < ZLANE[1])
    at = ZLANE[face]
    xs = sorted({x for x, _ in have})
    rows = sorted(have)

    def half(d, n):
        return roll_rows(got[me ^ d, n // 2], -4 * (n % 2))

    def strip(d, keys, base):
        out = {}
        for n, key in enumerate(keys):
            v = roll_lanes(half(d, n // 4), at - 32 * (n % 4))
            out[key] = jnp.where(beyond(), v, base[key])
        return out

    new = strip(1, rows, have)
    new.update(strip(5, [(face, y) for y in xs], {(face, y): half(4, n) for n, y in enumerate(xs)}))
    new.update(strip(3, [(x, face) for x in xs], {(x, face): half(2, n) for n, x in enumerate(xs)}))
    new.update(strip(7, [(face, face)], {(face, face): half(6, 0)}))
    return new


def second_kernel(got, mid, table, chunks):
    have = {(r // 3 + 1, r % 3 + 1): mid[r] for r in range(9)}
    have = widen(have, got, place_in(0), 4)
    for (x, y), v in have.items():
        table[4 * (x - 1) + y - 1] = v
    me = place_in(1)
    zs = ZLANE[1]
    along_x = [have[1, y] for y in range(1, 5)]
    along_y = [have[x, 1] for x in range(1, 5)]
    whole = [have[x, y] for x in range(1, 5) for y in range(1, 5)]
    for d, tiles in ((4, along_x), (2, along_y), (6, along_x[:1]), (1, pack4(whole, zs)), (5, pack4(along_x, zs)),
                     (3, pack4(along_y, zs)), (7, pack4(along_x[:1], zs))):
        for k, v in enumerate(doubled(tiles)):
            chunks[me ^ d, k] = v


def prepare(neigh, cen, cid, emb, mix, val, env, lat, head, energy, nrow, nlane, live, crow, clane, irow, ilane, *out):
    sub, lane = iota(0), iota(1)
    big = iota(0, (128, 128))
    left, right = [], []
    for r in range(9):
        area = WIDTHS[r // 3] * WIDTHS[r % 3]
        ids = jnp.broadcast_to(cid[r:r + 1, :], TILE)
        valid = (lane >= 27) & (lane < 27 + 3 * area)
        valid = valid | ((lane >= 54) & (lane < 54 + 2 * area))
        valid = valid | ((lane >= 72) & (lane < 72 + 3 * area))
        row = (r // 3 + 1) * 5 + r % 3 + 1
        value = jnp.where((sub & 1) == 0, row, lane)
        left.append(jnp.where(valid & ((ids >> 7) == (sub >> 1)), value, 0).astype(f32).astype(bf16))
        lo = jnp.broadcast_to(cid[r:r + 1, :], (128, 128)) & 127
        right.append(jnp.where(big == lo, 1.0, 0.0).astype(bf16))
    inv = nt(jnp.concatenate(left, 1), jnp.concatenate(right, 1))
    inv = (inv + 0.5).astype(i32)
    for h in range(4):
        irow[h:h + 1, :] = inv[2 * h:2 * h + 1, :]
        ilane[h:h + 1, :] = inv[2 * h + 1:2 * h + 2, :]
    px, py, pz = parity()

    def flip(e, p):
        return e + p * (4 - 2 * e)

    def place(n):
        lo, hi = n & 127, n >> 7
        row = jnp.zeros(TILE, i32)
        col = jnp.zeros(TILE, i32)
        for h in range(4):
            row = jnp.where(hi == h, lane_take(jnp.broadcast_to(irow[h:h + 1, :], TILE), lo), row)
            col = jnp.where(hi == h, lane_take(jnp.broadcast_to(ilane[h:h + 1, :], TILE), lo), col)
        m = jnp.maximum(n - ATOMS, 0)
        grow = ((m.astype(f32) + 0.5) * (1.0 / 135.0)).astype(i32)
        rem = m - 135 * grow
        ex = ((grow.astype(f32) + 0.5) * 0.2).astype(i32)
        ey = grow - 5 * ex
        ez = ((rem.astype(f32) + 0.5) * (1.0 / 27.0)).astype(i32)
        slot = rem - 27 * ez
        ex, ey, ez = flip(ex, px), flip(ey, py), flip(ez, pz)
        first = jnp.where(ez == 0, 0, jnp.where(ez == 1, 27, jnp.where(ez == 2, 54, jnp.where(ez == 3, 72, 99))))
        return jnp.where(hi < 4, row, 5 * ex + ey), jnp.where(hi < 4, col, first + slot)

    n = neigh[...]
    c = jnp.concatenate([cen[...].astype(f32), jnp.zeros((1, 120), f32)], 1)
    c = jnp.sum(jnp.where(lane == sub, jnp.broadcast_to(c, TILE), 0.0), 1, keepdims=True)
    c = (jnp.broadcast_to(c, TILE) + 0.5).astype(i32)
    nrow[...], nlane[...] = place(n)
    crow[...], clane[...] = place(c)
    live[...] = jnp.where(n != c, 1.0, 0.0)

    def stack(w):
        hi = w.astype(bf16).astype(f32)
        return jnp.concatenate([hi, hi, w - hi], 1).astype(bf16)

    ve_t = jnp.concatenate([val[...], env[...]], 1)
    emb_t = jnp.concatenate([emb[0:8, :], jnp.zeros((8, C), f32)], 0)
    wide_energy = jnp.broadcast_to(energy[...], (128, C))
    tiles = (stack(emb[...].T), stack(mix[...]), stack(ve_t.T), stack(lat[...]), stack(head[...]), stack(head[...].T),
             stack(lat[...].T), stack(ve_t), stack(mix[...].T), stack(emb_t), wide_energy.T)
    for ref, v in zip(out, tiles):
        ref[...] = v


def pair_step(tab, nrow, nlane, live, crow, clane, w, s, force):
    sub, lane = iota(0), iota(1)
    px, py, pz = (1.0 - 2.0 * p.astype(f32) for p in parity())
    zshift = jnp.where(lane < ZLANE[1], -EDGE, jnp.where(lane >= ZLANE[4], EDGE, 0.0)) * pz
    zshift = jnp.where(sub == 2, zshift, 0.0)
    xshift = jnp.where(sub == 0, EDGE, 0.0) * px
    yshift = jnp.where(sub == 1, EDGE, 0.0) * py
    nr, nl, cr, cl = nrow[...], nlane[...], crow[...], clane[...]
    near = [jnp.zeros(TILE, f32) for _ in range(4)]
    centre = [jnp.zeros(TILE, f32) for _ in range(4)]
    for r in range(ROWS):
        ex, ey = r // 5, r % 5
        shift = zshift
        if ex in (0, 4):
            shift = shift + xshift * float(ex // 2 - 1)
        if ey in (0, 4):
            shift = shift + yshift * float(ey // 2 - 1)
        s["shifted"][r] = tab(ex, ey) + shift
        mine = nr == r
        centred = cr == r
        for q in range(4):
            line = jnp.broadcast_to(s["shifted"][r, q:q + 1, :], TILE)
            near[q] = jnp.where(mine, lane_take(line, nl), near[q])
            if ex in (1, 2, 3) and ey in (1, 2, 3):
                centre[q] = jnp.where(centred, lane_take(line, cl), centre[q])
    alive = live[...]
    disp = [near[k] - centre[k] for k in range(3)]
    grads = pair_grads(disp, centre[3], near[3], alive, w, s)
    spare = 1.0 / jnp.sum(1.0 - alive, 1, keepdims=True)
    for k, g in enumerate(grads):
        g = jnp.where(alive > 0.0, -g, jnp.sum(g, 1, keepdims=True) * spare)
        hi = g.astype(bf16).astype(f32)
        s["spread"][k] = hi
        s["spread"][k + 3] = g - hi
    s["spread"][6] = jnp.zeros(TILE, f32)
    s["spread"][7] = jnp.zeros(TILE, f32)
    big = iota(0, (128, 128))
    left, right = [], []
    for b in range(NB):
        g = s["spread"][:, b, :]
        rows = jnp.broadcast_to(nrow[b:b + 1, :], TILE)
        left.append(jnp.concatenate([jnp.where(rows == r, g, 0.0) for r in range(ROWS)], 0).astype(bf16))
        right.append(jnp.where(big == jnp.broadcast_to(nlane[b:b + 1, :], (128, 128)), 1.0, 0.0).astype(bf16))
    out = nt(jnp.concatenate(left, 1), jnp.concatenate(right, 1))
    for r in range(ROWS):
        v = out[8 * r:8 * r + 8]
        force[r] = jnp.where(sub < 3, v + roll_rows(v, -3), 0.0)


def far_rows(side):
    far = 0 if side else 4
    rest = (1, 2, 3) if side else (0, 1, 2, 3)
    return [5 * far + y for y in rest], [5 * x + far for x in rest], [5 * x + y for x in rest for y in rest], [5 * far + far]


def put(chunks, d, values):
    for m, v in enumerate(values):
        chunks[d, 3 * m:3 * m + 3, :] = v[0:3]


def strips4(rows, at):
    return pack4(rows, at)


def strips2(rows, head, tail):
    lane = iota(1)
    out = []
    for k in range(0, len(rows), 2):
        v = None
        for n, q in enumerate(rows[k:k + 2]):
            t = jnp.where(lane < 64 * n + 27, roll_lanes(q, 64 * n - head), roll_lanes(q, 64 * n + 27 - tail))
            v = t if v is None else jnp.where(lane >= 64, t, v)
        out.append(v)
    return out


def sum_messages(force, base, chunks, side):
    me = place_in(side)
    near, far = (1, 0) if side else (3, 4)
    head, tail = (ZLANE[near], ZLANE[far]) if side else (ZLANE[far], ZLANE[near])
    f = [force[r] for r in range(ROWS)]
    for k, r in enumerate(MIDDLE):
        f[r] = f[r] + base[k]
    xs = [f[5 * x + y] for x in (far, near) for y in range(5)]
    ys = [f[5 * x + y] for y in (far, near) for x in range(5)]
    corner = [f[5 * x + y] for x in (far, near) for y in (far, near)]
    for d, tiles in ((4, xs), (2, ys), (6, corner), (1, strips2(f, head, tail)), (5, strips2(xs, head, tail)),
                     (3, strips2(ys, head, tail)), (7, strips2(corner, head, tail))):
        put(chunks, me ^ d, tiles)


def add_messages(force, got, side):
    lane = iota(1, (3, 128))
    me = place_in(side)
    near, far = (1, 0) if side else (3, 4)
    inside = lane >= ZLANE[3] if side == 0 else lane < ZLANE[2]
    first = min(ZLANE[near], ZLANE[far])
    out = {r: force[r, 0:3, :] for r in range(ROWS)}
    xs = [5 * x + y for x in (near, far) for y in range(5)]
    ys = [5 * x + y for y in (near, far) for x in range(5)]
    corner = [5 * x + y for x in (near, far) for y in (near, far)]
    for d, rows in ((4, xs), (2, ys), (6, corner)):
        for m, r in enumerate(rows):
            out[r] = out[r] + got[me ^ d, 3 * m:3 * m + 3, :]
    for d, rows in ((1, list(range(ROWS))), (5, xs), (3, ys), (7, corner)):
        for n, r in enumerate(rows):
            v = got[me ^ d, 3 * (n // 2):3 * (n // 2) + 3, :]
            out[r] = out[r] + jnp.where(inside, roll_lanes(v, first - 64 * (n % 2)), 0.0)
    return out


def far_messages(force, chunks, side):
    me = place_in(side)
    at = ZLANE[0 if side else 4]
    xs, ys, whole, corner = ([force[r] for r in rows] for rows in far_rows(side))
    for d, tiles in ((4, xs), (2, ys), (6, corner), (1, strips4(whole, at)), (5, strips4(xs, at)), (3, strips4(ys, at)),
                     (7, strips4(corner, at))):
        put(chunks, me ^ d, tiles)


def add_far(force, got, side):
    lane = iota(1, (3, 128))
    me = place_in(side)
    near, far = (1, 0) if side else (3, 4)
    at = ZLANE[near]
    inside = (lane >= at) & (lane < at + 27)
    xs, ys, whole, corner = far_rows(side)
    out = {r: force[r, 0:3, :] for r in whole}
    xs = [r + 5 * (near - far) for r in xs]
    ys = [r + near - far for r in ys]
    corner = [5 * near + near]
    for d, rows in ((4, xs), (2, ys), (6, corner)):
        for m, r in enumerate(rows):
            out[r] = out[r] + got[me ^ d, 3 * m:3 * m + 3, :]
    for d, rows in ((1, whole), (5, xs), (3, ys), (7, corner)):
        for n, r in enumerate(rows):
            v = got[me ^ d, 3 * (n // 4):3 * (n // 4) + 3, :]
            out[r] = out[r] + jnp.where(inside, roll_lanes(v, at - 32 * (n % 4)), 0.0)
    return out


def weight_refs(refs):
    return dict(zip(WEIGHT_NAMES, refs))


def first_pairs(part, got, *refs):
    tab, force, base, chunks = refs[10:14]
    prepare(*refs[:10], *refs[14:32])
    nrow, nlane, live, crow, clane = refs[14:19]
    w = weight_refs(refs[21:32])
    s = dict(zip(ALL_SCRATCH, refs[32:]))
    have = {(x, y): part[4 * (x - 1) + y - 1] for x in range(1, 5) for y in range(1, 5)}
    for (x, y), v in widen(have, got, place_in(1), 0).items():
        tab[5 * x + y] = v
    pair_step(lambda x, y: tab[5 * x + y], nrow, nlane, live, crow, clane, w, s, force)
    sub, lane = iota(0), iota(1)
    mine = (sub < 3) & (lane >= ZLANE[1]) & (lane < ZLANE[4])
    for k, r in enumerate(MIDDLE):
        v = tab[r]
        rest = (v + STEP * roll_rows(v, -4)) * (1.0 / (STEP * STEP)) * masses(jnp.broadcast_to(tab[r, 3:4, :], TILE))
        base[k] = jnp.where(mine, rest, 0.0)
    sum_messages(force, base, chunks, 1)


def next_pairs(force, got, table, nrow, nlane, live, crow, clane, *refs):
    w = weight_refs(refs[:11])
    total, force2, chunks = refs[11:14]
    s = dict(zip(ALL_SCRATCH, refs[14:]))
    lane = iota(1, (3, 128))
    mine = (lane >= ZLANE[1]) & (lane < ZLANE[4])
    for r, f in add_messages(force, got, 0).items():
        mass = inverse_mass(jnp.broadcast_to(table[r, 3:4, :], (3, 128)))
        moved = (STEP * STEP) * f * mass
        if r in MIDDLE:
            total[MIDDLE.index(r), 0:3, :] = f
            half = (0.5 * STEP) * f * mass
            kick = table[r, 4:7, :] + half + half
            moved = jnp.where(mine, table[r, 0:3, :] + STEP * kick, moved)
        s["table"][r] = table[r]
        s["table"][r, 0:3, :] = moved
    pair_step(lambda x, y: s["table"][5 * x + y], nrow, nlane, live, crow, clane, w, s, force2)
    far_messages(force2, chunks, 0)


def sum_kernel(force, base, got, out, chunks):
    for r, v in add_messages(force, got, 1).items():
        out[r, 0:3, :] = v
    sum_messages(out, base, chunks, 0)


def far_kernel(force, got, out, chunks):
    for r, v in add_far(force, got, 0).items():
        out[r, 0:3, :] = v
    far_messages(out, chunks, 1)


def end_kernel(force, got, total, irow, ilane, own, new_pos, new_vel, new_frc, both):
    summed = add_far(force, got, 1)
    for k, r in enumerate(MIDDLE):
        both[k, 0:3, :] = summed[r]
        both[k, 3:6, :] = total[k, 0:3, :]
        both[k, 6:8, :] = jnp.zeros((2, 128), f32)
    mass = inverse_mass(own[3:4, :])
    for h in range(4):
        lanes = slice(128 * h, 128 * h + 128)
        ir = jnp.broadcast_to(irow[h:h + 1, :], TILE)
        il = jnp.broadcast_to(ilane[h:h + 1, :], TILE)
        acc = jnp.zeros(TILE, f32)
        for k, r in enumerate(MIDDLE):
            acc = jnp.where(ir == r, lane_take(both[k], il), acc)
        last, first = acc[0:3], acc[3:6]
        m = mass[:, lanes]
        half = (0.5 * STEP) * first * m
        kick = own[4:7, lanes] + half + half
        new_pos[:, lanes] = own[0:3, lanes] + STEP * kick
        new_vel[:, lanes] = kick + (0.5 * STEP) * last * m
        new_frc[:, lanes] = last


ALL_SCRATCH = dict(PAIR_SCRATCH, shifted=(ROWS, 8, 128), table=(ROWS, 8, 128), spread=(8, 8, 128))


def shape(*dims, kind=f32):
    return jax.ShapeDtypeStruct(dims, kind)


def call(kernel, outs, *args, scratch=(), limit=4 << 20, flops=1 << 20, space=pltpu.VMEM):
    vm = pl.BlockSpec(memory_space=pltpu.VMEM)
    return pl.pallas_call(
        kernel,
        out_shape=tuple(outs),
        in_specs=[pl.BlockSpec(memory_space=space)] * len(args),
        out_specs=tuple([vm] * len(outs)),
        scratch_shapes=list(scratch),
        compiler_params=pltpu.CompilerParams(vmem_limit_bytes=limit),
        cost_estimate=pl.CostEstimate(flops=flops, bytes_accessed=1 << 18, transcendentals=0),
    )(*args)


def groups(side):
    out = []
    for x in range(side, SIZES[0] + side, 2):
        for y in range(side, SIZES[1] + side, 2):
            for z in range(side, SIZES[2] + side, 2):
                out.append([(((x + a) % SIZES[0]) * SIZES[1] + (y + b) % SIZES[1]) * SIZES[2] + (z + c) % SIZES[2]
                            for a in range(2) for b in range(2) for c in range(2)])
    return out


def trade(chunks, side):
    return lax.all_to_all(chunks, AXES, 0, 0, axis_index_groups=groups(side), tiled=True)


def local(positions, velocities, forces, species, cell_ids, centers, neighbours,
          w_embed, w_mix, w_value, w_env, w_latent, w_head, w_energy):
    table_shape = shape(ROWS, 8, 128)
    sums, fars = shape(8, SUM_ROWS, 128), shape(8, FAR_ROWS, 128)
    int_tile, flat = shape(8, 128, kind=i32), shape(4, 128, kind=i32)
    scratch = [pltpu.VMEM(v, f32) for v in ALL_SCRATCH.values()]

    small = (neighbours, centers.reshape(1, NB), w_embed.T, w_energy.reshape(1, C))
    chunks, mid, cid, own = call(
        start_kernel, [shape(8, FIRST, 8, 128), shape(9, 8, 128), shape(16, 128, kind=i32), shape(8, ATOMS)],
        jnp.concatenate([positions, velocities, forces], 0), species.reshape(1, ATOMS), cell_ids, *small,
        scratch=[pltpu.VMEM((128, 128), i32)])
    got = trade(chunks, 0)
    weight_shapes = [shape(m, k, kind=bf16) for m, k in (
        (C, 48), (C, 192), (384, 192), (C, 768), (C, 192), (C, 192), (256, 192), (C, 1152), (C, 192), (16, 192))]
    part, chunks = call(second_kernel, [shape(16, 8, 128), shape(8, FIRST, 8, 128)], got, mid)
    got = trade(chunks, 1)
    indices = [int_tile, int_tile, shape(8, 128), int_tile, int_tile, flat, flat]
    table, force, base, chunks, *prepared = call(
        first_pairs, [table_shape, table_shape, shape(9, 8, 128), sums] + indices + weight_shapes + [shape(C, 128)],
        part, got, small[0], small[1], cid, small[2], w_mix, w_value[0].T, w_env[0].T, w_latent[0], w_head, small[3], scratch=scratch, limit=24 << 20, flops=1 << 30)
    idx, (irow, ilane), weights = prepared[:5], prepared[5:7], prepared[7:]
    force, chunks = call(sum_kernel, [table_shape, sums], force, base, trade(chunks, 1))
    total, force, chunks = call(
        next_pairs, [shape(9, 8, 128), table_shape, fars], force, trade(chunks, 0), table, *idx, *weights, scratch=scratch,
        limit=24 << 20, flops=1 << 30)
    force, chunks = call(far_kernel, [table_shape, fars], force, trade(chunks, 0))
    return call(end_kernel, [shape(3, ATOMS)] * 3, force, trade(chunks, 1), total, irow, ilane, own,
                scratch=[pltpu.VMEM((9, 8, 128), f32)])


def solution(mesh):
    from jax.sharding import PartitionSpec as P

    rows = P(None, AXES)
    in_specs = (rows, rows, rows, P(AXES), P(*AXES, None), P(AXES), P(AXES, None)) + (P(),) * 7
    return jax.shard_map(local, mesh=mesh, in_specs=in_specs, out_specs=(rows, rows, rows), check_vma=False)
```
